32 devices in a mesh: wa: 8 (over z, x), col: 4 (over y, core).
Axes of the slice: x: 2, y: 2, z: 4, core: 2. Of those that a mesh axis runs over, the one named last changes fastest.
Arguments:
- tokens: bfloat16 [4, 8, 512, 768], P('col', None, 'wa'), may hold values from -6 to 6
- tap: bfloat16 [4, 8, 512, 768], P('col', None, 'wa'), may hold values from -6 to 6
- ln1_gain: bfloat16 [768], P(('wa', 'col')), may hold values from 0.5 to 1.5
- ln1_bias: bfloat16 [768], P(('wa', 'col')), may hold values from -3 to 3
- qkv_weight: bfloat16 [768, 2304], P(('wa', 'col')), may hold values from -0.21875 to 0.21875
- query_bias: bfloat16 [768], P(('wa', 'col')), may hold values from -3 to 3
- value_bias: bfloat16 [768], P(('wa', 'col')), may hold values from -3 to 3
- out_weight: bfloat16 [768, 768], P(('wa', 'col')), may hold values from -0.875 to 0.875
- out_bias: bfloat16 [768], P(('wa', 'col')), may hold values from -3 to 3
- ln2_gain: bfloat16 [768], P(('wa', 'col')), may hold values from 0.5 to 1.5
- ln2_bias: bfloat16 [768], P(('wa', 'col')), may hold values from -3 to 3
- fc1_weight: bfloat16 [768, 3072], P(('wa', 'col')), may hold values from -0.21875 to 0.21875
- fc1_bias: bfloat16 [3072], P(('wa', 'col')), may hold values from -3 to 3
- fc2_weight: bfloat16 [3072, 768], P(('wa', 'col')), may hold values from -0.109375 to 0.109375
- fc2_bias: bfloat16 [768], P(('wa', 'col')), may hold values from -3 to 3
- block_up: bfloat16 [768, 1024], P(('wa', 'col')), may hold values from -0.21875 to 0.21875
- tap_up: bfloat16 [768, 1024], P(('wa', 'col')), may hold values from -0.21875 to 0.21875
- conv1_weight: bfloat16 [27, 128, 256], P(None, 'col'), may hold values from -0.078125 to 0.078125
- conv2_weight: bfloat16 [27, 128, 128], P(None, 'col'), may hold values from -0.109375 to 0.109375
- skip_weight: bfloat16 [128, 256], P('col'), may hold values from -0.375 to 0.375
- cotangent: bfloat16 [4, 8, 128, 4096], P(None, 'wa', 'col'), may hold values from -6 to 6
Outputs:
- section_out: bfloat16 [4, 8, 128, 4096], P(None, 'wa', 'col')
- input_grad: float32 [4, 8, 512, 768], P('col', None, 'wa')
- tap_grad: float32 [4, 8, 512, 768], P('col', None, 'wa')
- grad_ln1_gain: float32 [768], P(('wa', 'col'))
- grad_ln1_bias: float32 [768], P(('wa', 'col'))
- grad_qkv_weight: float32 [768, 2304], P(('wa', 'col'))
- grad_query_bias: float32 [768], P(('wa', 'col'))
- grad_value_bias: float32 [768], P(('wa', 'col'))
- grad_out_weight: float32 [768, 768], P(('wa', 'col'))
- grad_out_bias: float32 [768], P(('wa', 'col'))
- grad_ln2_gain: float32 [768], P(('wa', 'col'))
- grad_ln2_bias: float32 [768], P(('wa', 'col'))
- grad_fc1_weight: float32 [768, 3072], P(('wa', 'col'))
- grad_fc1_bias: float32 [3072], P(('wa', 'col'))
- grad_fc2_weight: float32 [3072, 768], P(('wa', 'col'))
- grad_fc2_bias: float32 [768], P(('wa', 'col'))
- grad_block_up: float32 [768, 1024], P(('wa', 'col'))
- grad_tap_up: float32 [768, 1024], P(('wa', 'col'))
- grad_conv1_weight: float32 [27, 128, 256], P(None, 'col')
- grad_conv2_weight: float32 [27, 128, 128], P(None, 'col')
- grad_skip_weight: float32 [128, 256], P('col')
The draws below stay inside these ranges and needn't reach their ends.
All inputs are finite; a program needn't handle non-finite values.
Results may differ from the reference program's by a relative error of at most 0.028.
Values may be sent and summed in bfloat16 or wider, within the bound.
No kernel may reach another device: no remote copies, remote signals or barrier semaphores. Data moves between devices by JAX's collectives and lax.ppermute only.
A program may use at most 320 MiB of HBM per device.

```python
import jax
import jax.numpy as jnp
from jax import lax

D = 768
HEADS = 12
HEAD_DIM = 64
MLP = 3072
DEC = 128
GRID = 8
PATCHES = 512
SIDE = 16
VOX = 4096
CAT = 256
UPW = 1024
CROP_GROUPS = 4
CROP_SPAN = 8
CROPS = 32


def block_levels(rng, extent, cuts, smallest, top_value):
    loudness, own = 1.0, jax.random.fold_in(rng, 6)
    for dim, shards_of in cuts:
        steps = jnp.exp(jax.random.uniform(jax.random.fold_in(own, dim), (shards_of,), jnp.float32, smallest / len(cuts), top_value / len(cuts)))
        loudness = loudness * jnp.repeat(steps, extent[dim] // shards_of).reshape([-1 if axis == dim else 1 for axis in range(len(extent))])
    return loudness


def normal_values(rng, shape, scale, bound, pieces=(), held_as=jnp.bfloat16):
    entries = scale * jax.random.normal(rng, shape, jnp.float32)
    if pieces:
        entries = entries * block_levels(rng, shape, pieces, -0.22, 0.18)
    return jnp.clip(entries, -bound, bound).astype(held_as)


def setup_inputs(seed: int = 0) -> dict:
    key_of = jax.random.split(jax.random.key(seed), 22)
    return {
        "tokens": normal_values(key_of[0], (CROP_GROUPS, CROP_SPAN, PATCHES, D), 1.0, 6.0, ((0, 4), (2, 8))),
        "tap": normal_values(key_of[1], (CROP_GROUPS, CROP_SPAN, PATCHES, D), 1.0, 6.0, ((0, 4), (2, 8))),
        "ln1_gain": jnp.clip(1.0 + 0.1 * jax.random.normal(key_of[2], (D,), jnp.float32), 0.5, 1.5).astype(jnp.bfloat16),
        "ln1_bias": normal_values(key_of[3], (D,), 0.5, 3.0, ((0, 32),)),
        "qkv_weight": normal_values(key_of[4], (D, 3 * D), D ** -0.5, 0.21875, ((0, 32),)),
        "query_bias": normal_values(key_of[5], (D,), 0.5, 3.0, ((0, 32),)),
        "value_bias": normal_values(key_of[6], (D,), 0.5, 3.0, ((0, 32),)),
        "out_weight": normal_values(key_of[7], (D, D), (D // 16) ** -0.5, 0.875, ((0, 32),)),
        "out_bias": normal_values(key_of[8], (D,), 0.5, 3.0, ((0, 32),)),
        "ln2_gain": jnp.clip(1.0 + 0.1 * jax.random.normal(key_of[9], (D,), jnp.float32), 0.5, 1.5).astype(jnp.bfloat16),
        "ln2_bias": normal_values(key_of[10], (D,), 0.5, 3.0, ((0, 32),)),
        "fc1_weight": normal_values(key_of[11], (D, MLP), D ** -0.5, 0.21875, ((0, 32),)),
        "fc1_bias": normal_values(key_of[12], (MLP,), 0.5, 3.0, ((0, 32),)),
        "fc2_weight": normal_values(key_of[13], (MLP, D), MLP ** -0.5, 0.109375, ((0, 32),)),
        "fc2_bias": normal_values(key_of[14], (D,), 0.5, 3.0, ((0, 32),)),
        "block_up": normal_values(key_of[15], (D, UPW), D ** -0.5, 0.21875, ((0, 32),)),
        "tap_up": normal_values(key_of[16], (D, UPW), D ** -0.5, 0.21875, ((0, 32),)),
        "conv1_weight": normal_values(key_of[17], (27, DEC, CAT), (27 * CAT) ** -0.5, 0.078125, ((1, 4),)),
        "conv2_weight": normal_values(key_of[18], (27, DEC, DEC), (27 * DEC) ** -0.5, 0.109375, ((1, 4),)),
        "skip_weight": normal_values(key_of[19], (DEC, CAT), CAT ** -0.5, 0.375, ((0, 4),)),
        "cotangent": normal_values(key_of[20], (CROP_GROUPS, CROP_SPAN, DEC, VOX), 1.0, 6.0, ((1, 8), (2, 4))),
    }


@jax.custom_vjp
def low(v):
    return lax.optimization_barrier(v.astype(jnp.bfloat16)).astype(jnp.float32)

@jax.custom_vjp
def low_back(v):
    return v

def low_keep(v):
    return (low(v), None)

def low_pass(kept, grad):
    return (grad,)

def back_keep(v):
    return (v, None)

def back_low(kept, grad):
    return (low(grad),)
low.defvjp(low_keep, low_pass)
low_back.defvjp(back_keep, back_low)

def matmul(left, right):
    return jnp.dot(left, right, precision=lax.Precision.HIGHEST, preferred_element_type=jnp.float32)

def standardize(values, epsilon):
    center = values - lax.optimization_barrier(jnp.mean(values, axis=-1, keepdims=True))
    return center * lax.rsqrt(lax.optimization_barrier(jnp.mean(center * center, axis=-1, keepdims=True)) + epsilon)

def to_volume(columns):
    blocks = columns.reshape(GRID, GRID, GRID, 2, 2, 2, DEC)
    return blocks.transpose(6, 0, 3, 1, 4, 2, 5).reshape(DEC, VOX)

def conv_three(maps, weight):
    kernel = weight.reshape(3, 3, 3, weight.shape[1], weight.shape[2]).transpose(3, 4, 0, 1, 2)
    image = maps.reshape(1, maps.shape[0], SIDE, SIDE, SIDE)
    result = lax.conv_general_dilated(image, kernel, (1, 1, 1), 'SAME', dimension_numbers=('NCDHW', 'OIDHW', 'NCDHW'), precision=lax.Precision.HIGHEST)
    return result.reshape(weight.shape[1], VOX)

def crop_forward(token_crop, tap_crop, params):
    gain_one, bias_one, qkv_full, query_bias, value_bias, out_full, out_shift, gain_two, bias_two, fc1_full, fc1_shift, fc2_full, fc2_shift, block_full, tap_full, conv_one, conv_two, skip_full = params
    normed_one = low(standardize(token_crop, 1e-06) * gain_one + bias_one)
    bias_all = jnp.concatenate([query_bias, jnp.zeros_like(query_bias), value_bias])
    qkv = low(low_back(matmul(normed_one, qkv_full) + bias_all))
    heads = qkv.reshape(PATCHES, 3, HEADS, HEAD_DIM).transpose(1, 2, 0, 3)
    scores = low_back(jnp.einsum('hqd,hkd->hqk', heads[0], heads[1], precision=lax.Precision.HIGHEST) * 0.125)
    attention = low(jax.nn.softmax(scores, axis=-1))
    mixed = jnp.einsum('hqk,hkd->hqd', attention, heads[2], precision=lax.Precision.HIGHEST)
    mixed = low(low_back(mixed.transpose(1, 0, 2).reshape(PATCHES, D)))
    first = token_crop + low_back(matmul(mixed, out_full) + out_shift)
    normed_two = low(standardize(first, 1e-06) * gain_two + bias_two)
    hidden = low_back(matmul(normed_two, fc1_full) + fc1_shift)
    active = low(jax.nn.gelu(hidden, approximate=False))
    second = first + low_back(matmul(active, fc2_full) + fc2_shift)
    up_block = low(low_back(matmul(low(second), block_full)))
    up_tap = low(low_back(matmul(tap_crop, tap_full)))
    joined = jnp.concatenate([to_volume(up_block), to_volume(up_tap)], axis=0)
    conv_first = low_back(conv_three(joined, conv_one))
    hidden_maps = low(jax.nn.silu(standardize(conv_first, 1e-05)))
    conv_second = low_back(conv_three(hidden_maps, conv_two))
    skip_maps = low_back(matmul(skip_full, joined))
    return jax.nn.silu(standardize(conv_second, 1e-05) + standardize(skip_maps, 1e-05))

def reference(tokens, tap, ln1_gain, ln1_bias, qkv_weight, query_bias, value_bias, out_weight, out_bias, ln2_gain, ln2_bias, fc1_weight, fc1_bias, fc2_weight, fc2_bias, block_up, tap_up, conv1_weight, conv2_weight, skip_weight, cotangent):
    params = (ln1_gain, ln1_bias, qkv_weight, query_bias, value_bias, out_weight, out_bias, ln2_gain, ln2_bias, fc1_weight, fc1_bias, fc2_weight, fc2_bias, block_up, tap_up, conv1_weight, conv2_weight, skip_weight)
    params = tuple((item.astype(jnp.float32) for item in params))

    def whole(token_values, tap_values, weights):
        token_crops = token_values.reshape(CROPS, PATCHES, D)
        tap_crops = tap_values.reshape(CROPS, PATCHES, D)

        def one_crop(pair):
            return crop_forward(pair[0], pair[1], weights)
        maps = lax.map(jax.checkpoint(one_crop), (token_crops, tap_crops))
        return maps.reshape(CROP_GROUPS, CROP_SPAN, DEC, VOX)
    section, pullback = jax.vjp(whole, tokens.astype(jnp.float32), tap.astype(jnp.float32), params)
    grad_tokens, grad_tap, grad_params = pullback(cotangent.astype(jnp.float32))
    return (section.astype(jnp.bfloat16), grad_tokens, grad_tap, grad_params[0], grad_params[1], grad_params[2], grad_params[3], grad_params[4], grad_params[5], grad_params[6], grad_params[7], grad_params[8], grad_params[9], grad_params[10], grad_params[11], grad_params[12], grad_params[13], grad_params[14], grad_params[15], grad_params[16], grad_params[17])
```

```python
import jax
import jax.numpy as jnp
from jax import lax
from jax.sharding import Mesh, PartitionSpec as P

D = 768
HEADS = 12
HEAD_DIM = 64
MLP = 3072
DEC = 128
GRID = 8
PATCHES = 512
SIDE = 16
VOX = 4096
PLANE = SIDE * SIDE
BF = jnp.bfloat16
F32 = jnp.float32


def cut_axis(devices, label):
    places = [getattr(item, "coords", None) for item in devices]
    if len(devices) == 1 or any(place is None for place in places):
        return [(label, len(devices), False)]
    full = [tuple(item.coords) + (item.core_on_chip,) for item in devices]
    found = []
    for axis in range(4):
        values = [place[axis] for place in full]
        if len(set(values)) > 1:
            stride = next(k for k in range(len(values)) if values[k] != values[0])
            found.append((stride, len(set(values)), axis))
    found.sort(reverse=True)
    step = 1
    for stride, size, _ in reversed(found):
        if stride != step:
            return [(label, len(devices), False)]
        step *= size
    if step != len(devices):
        return [(label, len(devices), False)]
    return [(label + "xyzc"[axis], size, axis == 3) for _, size, axis in found]


class Axes:
    def __init__(self, mesh):
        grid = mesh.devices
        wa = cut_axis(list(grid[:, 0]), "wa")
        col = cut_axis(list(grid[0, :]), "col")
        parts = wa + col
        self.sizes = {name: size for name, size, _ in parts}
        self.names = tuple(self.sizes)
        self.wa = tuple(name for name, _, _ in wa)
        self.col = tuple(name for name, _, _ in col)
        self.wa_count, self.col_count = grid.shape
        self.mesh = Mesh(grid.reshape(tuple(self.sizes.values())), self.names)
        core = [name for name, _, is_core in parts if is_core]
        links = [name for name, _, is_core in parts if not is_core]
        links.sort(key=lambda name: -self.sizes[name])
        self.order_a = tuple(links + core)
        if len(links) > 2:
            links = links[:-2] + [links[-1], links[-2]]
        self.order_b = tuple(links + core)


def swap(value, axis):
    return lax.ppermute(value, axis, [(0, 1), (1, 0)])


def turn(value, axis, size, step):
    return lax.ppermute(value, axis, [(k, (k + step) % size) for k in range(size)])


def gather_axis(value, axis, size):
    place = lax.axis_index(axis)
    if size == 2:
        mine, other = value[None], swap(value, axis)[None]
        return jnp.where(
            place == 0,
            jnp.concatenate([mine, other]),
            jnp.concatenate([other, mine]),
        )
    got = [turn(value, axis, size, step) for step in range(1, size)]
    out = jnp.zeros((size,) + value.shape, value.dtype)
    out = lax.dynamic_update_index_in_dim(out, value, place, 0)
    for step in range(1, size):
        out = lax.dynamic_update_index_in_dim(out, got[step - 1], (place - step) % size, 0)
    return out


def gather_rows(value, order, names):
    rows, columns = value.shape
    dims = []
    sizes = {name: lax.axis_size(name) for name in order}
    for name in order:
        value = gather_axis(value, name, sizes[name])
        dims.insert(0, name)
    kept = [name for name in names if name in dims]
    value = value.transpose([dims.index(name) for name in kept] + [len(dims), len(dims) + 1])
    return value.reshape(-1, columns)


def scatter_axis(value, axis, size, dim):
    place = lax.axis_index(axis)
    mine = lax.dynamic_index_in_dim(value, place, dim, False).astype(F32)
    got = [
        turn(
            lax.dynamic_index_in_dim(value, (place + step) % size, dim, False), axis, size, step
        )
        for step in range(1, size)
    ]
    for item in got:
        mine = mine + item.astype(F32)
    return mine


def scatter_rows(value, order, names):
    columns = value.shape[1]
    dims = [name for name in names if name in order]
    value = value.reshape([lax.axis_size(name) for name in dims] + [-1, columns])
    for name in reversed(order):
        dim = dims.index(name)
        dims.pop(dim)
        value = scatter_axis(value.astype(BF), name, lax.axis_size(name), dim)
    return value


def product(left, right):
    return jnp.dot(left, right, preferred_element_type=F32)


def product_rows(left, right):
    return lax.dot_general(left, right, (((0,), (0,)), ((), ())), preferred_element_type=F32)


def product_back(left, right):
    return lax.dot_general(left, right, (((1,), (1,)), ((), ())), preferred_element_type=F32)


def standardize(values, epsilon, axis):
    center = values - jnp.mean(values, axis=axis, keepdims=True)
    factor = lax.rsqrt(jnp.mean(center * center, axis=axis, keepdims=True) + epsilon)
    return (center * factor, factor)


def norm_back(upstream, normed, factor, axis):
    middle = upstream - jnp.mean(upstream, axis=axis, keepdims=True)
    return factor * (middle - normed * jnp.mean(upstream * normed, axis=axis, keepdims=True))


def gelu_exact(values):
    return jax.nn.gelu(values, approximate=False)


def local_back(function, inputs, upstream):
    return jax.vjp(function, inputs)[1](upstream)[0]


def silu_back(values):
    gate = jax.nn.sigmoid(values)
    return gate * (1.0 + values * (1.0 - gate))


def to_volume(columns):
    blocks = columns.reshape(GRID, GRID, GRID, 2, 2, 2, DEC)
    return blocks.transpose(0, 3, 1, 4, 2, 5, 6).reshape(VOX, DEC)


def from_volume(maps):
    blocks = maps.reshape(GRID, 2, GRID, 2, GRID, 2, DEC)
    return blocks.transpose(0, 2, 4, 1, 3, 5, 6).reshape(PATCHES, 8 * DEC)


def cross_stack(maps):
    cube = maps.reshape(PLANE, SIDE, maps.shape[1])
    before = jnp.pad(cube[:, :-1], ((0, 0), (1, 0), (0, 0)))
    after = jnp.pad(cube[:, 1:], ((0, 0), (0, 1), (0, 0)))
    return jnp.concatenate([before, cube, after], axis=2).reshape(VOX, -1)


def plane_shift(values, along_d, along_h):
    cube = values.reshape(SIDE, SIDE, SIDE, -1)
    for axis, step in ((0, along_d), (1, along_h)):
        if step:
            pads = [(0, 0)] * 4
            pads[axis] = (max(-step, 0), max(step, 0))
            cube = lax.slice_in_dim(
                jnp.pad(cube, pads), max(step, 0), max(step, 0) + SIDE, axis=axis
            )
    return cube.reshape(VOX, -1)


def shift_pairs():
    return [(along_d, along_h) for along_d in (-1, 0, 1) for along_h in (-1, 0, 1)]


def conv_sum(wide, columns):
    total = 0.0
    for slot, (along_d, along_h) in enumerate(shift_pairs()):
        total = total + plane_shift(
            wide[:, slot * columns : (slot + 1) * columns], along_d, along_h
        )
    return total


def conv_forward(stacked, weight):
    outs, ins = weight.shape[1:]
    table = weight.reshape(9, 3, outs, ins).transpose(1, 3, 0, 2).reshape(3 * ins, 9 * outs)
    return conv_sum(product(stacked, table), outs)


def conv_input_grad(stacked, weight):
    outs, ins = weight.shape[1:]
    table = weight[::-1].reshape(9, 3, outs, ins).transpose(1, 2, 0, 3).reshape(3 * outs, 9 * ins)
    return conv_sum(product(stacked, table), ins)


def conv_weight_grad(stacked, maps):
    outs, ins = stacked.shape[1] // 3, maps.shape[1]
    shifted = jnp.concatenate([plane_shift(maps, *pair) for pair in shift_pairs()], axis=1)
    table = product_rows(stacked, shifted).reshape(3, outs, 9, ins)
    return table[::-1].transpose(2, 0, 1, 3).reshape(27, outs, ins)


def split_heads(block):
    parts = block.reshape(PATCHES, 3, HEADS, HEAD_DIM).transpose(1, 2, 0, 3)
    return (parts[0], parts[1], parts[2])


def attention_weights(queries, keys):
    scores = jnp.einsum("hqd,hkd->hqk", queries, keys, preferred_element_type=F32) * 0.125
    expo = jnp.exp(scores - jnp.max(scores, axis=-1, keepdims=True))
    return expo / jnp.sum(expo, axis=-1, keepdims=True)


def attend(block):
    queries, keys, values = split_heads(block)
    weights = attention_weights(queries, keys)
    mixed = jnp.einsum("hqk,hkd->hqd", weights.astype(BF), values, preferred_element_type=F32)
    return mixed.transpose(1, 0, 2).reshape(PATCHES, D).astype(BF)


def attend_back(block, grad_block):
    queries, keys, values = split_heads(block)
    weights = attention_weights(queries, keys)
    grad_heads = grad_block.reshape(PATCHES, HEADS, HEAD_DIM).transpose(1, 0, 2)
    grad_weights = jnp.einsum("hqd,hkd->hqk", grad_heads, values, preferred_element_type=F32)
    grad_values = jnp.einsum(
        "hqk,hqd->hkd", weights.astype(BF), grad_heads, preferred_element_type=F32
    )
    grad_scores = weights * (grad_weights - jnp.sum(grad_weights * weights, axis=-1, keepdims=True))
    grad_scores = grad_scores.astype(BF)
    grad_queries = jnp.einsum("hqk,hkd->hqd", grad_scores, keys, preferred_element_type=F32) * 0.125
    grad_keys = jnp.einsum("hqk,hqd->hkd", grad_scores, queries, preferred_element_type=F32) * 0.125
    stacked = jnp.stack([grad_queries, grad_keys, grad_values])
    return stacked.transpose(2, 0, 1, 3).reshape(PATCHES, 3 * D).astype(BF)


def make_body(axes):
    names, wa, col = axes.names, axes.wa, axes.col
    col_count = axes.col_count

    def body(
        tokens,
        tap,
        ln1_gain,
        ln1_bias,
        qkv_weight,
        query_bias,
        value_bias,
        out_weight,
        out_bias,
        ln2_gain,
        ln2_bias,
        fc1_weight,
        fc1_bias,
        fc2_weight,
        fc2_bias,
        block_up,
        tap_up,
        conv1_weight,
        conv2_weight,
        skip_weight,
        cotangent,
    ):
        rows_here = ln1_gain.shape[0]
        vectors = [
            item.reshape(rows_here, -1)
            for item in (
                ln1_gain, ln1_bias, query_bias, value_bias, out_bias, ln2_gain, ln2_bias,
                fc2_bias, fc1_bias,
            )
        ]
        vectors = jnp.concatenate(vectors, axis=1)
        extra = vectors.shape[1]
        vectors = jnp.pad(vectors, ((0, 0), (0, 128 - extra)))
        first_group = gather_rows(
            jnp.concatenate([qkv_weight, out_weight, vectors], axis=1), axes.order_a, names
        )
        fc1_full = gather_rows(fc1_weight, axes.order_b, names)
        fc2_full = gather_rows(fc2_weight, axes.order_a, names)
        up_full = gather_rows(jnp.concatenate([block_up, tap_up], axis=1), axes.order_b, names)
        qkv_full, out_full = first_group[:, : 3 * D], first_group[:, 3 * D : 4 * D]
        small = first_group[:, 4 * D : 4 * D + extra].astype(F32)
        gain_one, bias_one, query_bias_full, value_bias_full, out_shift, gain_two, bias_two, fc2_shift = (
            small[:, k] for k in range(8)
        )
        fc1_shift = small[:, 8:].reshape(-1)
        block_full, tap_full = up_full[:, : 8 * DEC], up_full[:, 8 * DEC :]

        conv_shard = jnp.concatenate([conv1_weight, conv2_weight], axis=2)
        skip_shard = jnp.pad(skip_weight, ((0, 0), (0, DEC)))
        conv_shard = jnp.concatenate([conv_shard, skip_shard[None]], axis=0)
        conv_all = lax.all_gather(conv_shard, col, axis=1, tiled=True)
        conv1_full, conv2_full = conv_all[:27, :, : 2 * DEC], conv_all[:27, :, 2 * DEC :]
        skip_full = conv_all[27, :, : 2 * DEC]

        rows_bf = lax.all_to_all(tokens, wa, split_axis=1, concat_axis=2, tiled=True).reshape(-1, D)
        tap_rows = lax.all_to_all(tap, wa, split_axis=1, concat_axis=2, tiled=True).reshape(-1, D)
        rows = rows_bf.astype(F32)
        normed_one, factor_one = standardize(rows, 1e-06, -1)
        input_one = (normed_one * gain_one + bias_one).astype(BF)
        bias_all = jnp.concatenate([query_bias_full, jnp.zeros_like(query_bias_full), value_bias_full])
        qkv_rows = (product(input_one, qkv_full) + bias_all).astype(BF)
        attn_rows = attend(qkv_rows)
        first = rows + product(attn_rows, out_full) + out_shift
        normed_two, factor_two = standardize(first, 1e-06, -1)
        input_two = (normed_two * gain_two + bias_two).astype(BF)
        hidden = product(input_two, fc1_full) + fc1_shift
        active = gelu_exact(hidden).astype(BF)
        second = first + product(active, fc2_full) + fc2_shift
        block_out = second.astype(BF)

        maps_block = to_volume(product(block_out, block_full).astype(BF))
        maps_tap = to_volume(product(tap_rows, tap_full).astype(BF))
        joined = jnp.concatenate([maps_block, maps_tap], axis=1)
        conv_one = conv_forward(cross_stack(joined), conv1_full)
        normed_c1, factor_c1 = standardize(conv_one, 1e-05, 0)
        hidden_maps = jax.nn.silu(normed_c1).astype(BF)
        conv_two = conv_forward(cross_stack(hidden_maps), conv2_full)
        normed_c2, factor_c2 = standardize(conv_two, 1e-05, 0)
        normed_skip, factor_skip = standardize(product_back(joined, skip_full), 1e-05, 0)
        summed = normed_c2 + normed_skip
        section = jax.nn.silu(summed).astype(BF)
        section_out = lax.all_to_all(
            section.T.reshape(1, 1, DEC, VOX), col, split_axis=2, concat_axis=0, tiled=True
        )

        upstream = lax.all_to_all(cotangent, col, split_axis=0, concat_axis=2, tiled=True)
        upstream = upstream.reshape(DEC, VOX).T.astype(F32)
        grad_summed = upstream * silu_back(summed)
        grad_c2 = norm_back(grad_summed, normed_c2, factor_c2, 0).astype(BF)
        grad_skip = norm_back(grad_summed, normed_skip, factor_skip, 0).astype(BF)
        stack_c2 = cross_stack(grad_c2)
        grad_hidden = conv_input_grad(stack_c2, conv2_full)
        grad_c1 = norm_back(grad_hidden * silu_back(normed_c1), normed_c1, factor_c1, 0).astype(BF)
        stack_c1 = cross_stack(grad_c1)
        grad_joined = conv_input_grad(stack_c1, conv1_full) + product(grad_skip, skip_full)
        grad_joined = grad_joined.astype(BF)
        weight_c2 = conv_weight_grad(stack_c2, hidden_maps)
        weight_c1 = conv_weight_grad(stack_c1, joined)
        weight_skip = product_rows(grad_skip, joined)

        conv_grads = jnp.concatenate([weight_c1, weight_c2], axis=2)
        skip_grads = jnp.pad(weight_skip, ((0, 0), (0, DEC)))[None]
        conv_grads = jnp.concatenate([conv_grads, skip_grads], axis=0).astype(BF)
        columns = conv_grads.shape[2]
        conv_grads = conv_grads.reshape(28, col_count, -1, columns).transpose(1, 0, 2, 3)
        conv_grads = scatter_rows(
            conv_grads.reshape(-1, columns), [n for n in axes.order_a if n in col], names
        )
        row_count = conv_grads.shape[0]
        wa_order = [n for n in axes.order_a if n in wa]
        conv_grads = scatter_rows(conv_grads, wa_order, names).astype(BF)
        conv_grads = gather_rows(conv_grads, wa_order, names).reshape(28, -1, columns)
        conv_grads = conv_grads.astype(F32)

        grad_up_block = from_volume(grad_joined[:, :DEC])
        grad_up_tap = from_volume(grad_joined[:, DEC:])
        grad_ups = jnp.concatenate(
            [product_rows(block_out, grad_up_block), product_rows(tap_rows, grad_up_tap)], axis=1
        )
        grad_ups = scatter_rows(grad_ups, axes.order_b, names)
        grad_tap_rows = product_back(grad_up_tap, tap_full).astype(BF)
        grad_second = product_back(grad_up_block, block_full)
        grad_mlp = grad_second.astype(BF)
        grad_fc2 = scatter_rows(product_rows(active, grad_mlp), axes.order_a, names)
        grad_fc2_shift = jnp.sum(grad_mlp.astype(F32), axis=0)
        grad_active = product_back(grad_mlp, fc2_full)
        grad_hidden_rows = local_back(gelu_exact, hidden, grad_active).astype(BF)
        grad_fc1 = scatter_rows(product_rows(input_two, grad_hidden_rows), axes.order_b, names)
        grad_fc1_shift = jnp.sum(grad_hidden_rows.astype(F32), axis=0)
        grad_input_two = product_back(grad_hidden_rows, fc1_full)
        grad_gain_two = jnp.sum(grad_input_two * normed_two, axis=0)
        grad_bias_two = jnp.sum(grad_input_two, axis=0)
        grad_first = grad_second + norm_back(grad_input_two * gain_two, normed_two, factor_two, -1)
        grad_attn = grad_first.astype(BF)
        grad_out = product_rows(attn_rows, grad_attn)
        grad_out_shift = jnp.sum(grad_attn.astype(F32), axis=0)
        grad_mixed = product_back(grad_attn, out_full).astype(BF)
        grad_qkv = attend_back(qkv_rows, grad_mixed)
        grad_qkv_full = product_rows(input_one, grad_qkv)
        column_sums = jnp.sum(grad_qkv.astype(F32), axis=0)
        grad_input_one = product_back(grad_qkv, qkv_full)
        grad_gain_one = jnp.sum(grad_input_one * normed_one, axis=0)
        grad_bias_one = jnp.sum(grad_input_one, axis=0)
        grad_rows = grad_first + norm_back(grad_input_one * gain_one, normed_one, factor_one, -1)
        small_grads = jnp.stack(
            [
                grad_gain_one, grad_bias_one, column_sums[:D], column_sums[2 * D :], grad_out_shift,
                grad_gain_two, grad_bias_two, grad_fc2_shift,
            ],
            axis=1,
        )
        small_grads = jnp.concatenate([small_grads, grad_fc1_shift.reshape(D, -1)], axis=1)
        small_grads = jnp.pad(small_grads, ((0, 0), (0, 128 - extra)))
        first_grads = scatter_rows(
            jnp.concatenate([grad_qkv_full, grad_out, small_grads], axis=1), axes.order_a, names
        )
        small_sums = first_grads[:, 4 * D : 4 * D + extra]
        home_rows = lax.all_to_all(
            grad_rows.astype(BF).reshape(1, 1, PATCHES, D), wa, split_axis=2, concat_axis=1, tiled=True
        ).astype(F32)
        home_tap = lax.all_to_all(
            grad_tap_rows.reshape(1, 1, PATCHES, D), wa, split_axis=2, concat_axis=1, tiled=True
        ).astype(F32)
        return (
            section_out,
            home_rows,
            home_tap,
            small_sums[:, 0],
            small_sums[:, 1],
            first_grads[:, : 3 * D],
            small_sums[:, 2],
            small_sums[:, 3],
            first_grads[:, 3 * D : 4 * D],
            small_sums[:, 4],
            small_sums[:, 5],
            small_sums[:, 6],
            grad_fc1,
            small_sums[:, 8:].reshape(-1),
            grad_fc2,
            small_sums[:, 7],
            grad_ups[:, : 8 * DEC],
            grad_ups[:, 8 * DEC :],
            conv_grads[:27, :, : 2 * DEC],
            conv_grads[:27, :, 2 * DEC :],
            conv_grads[27, :, : 2 * DEC],
        )

    return body


def solution(mesh):
    axes = Axes(mesh)
    wa, col = axes.wa, axes.col
    both = wa + col
    tall, flat = P(both, None), P(both)
    rows = P(col, None, wa, None)
    maps = P(None, wa, col, None)
    kernel, wide = P(None, col, None), P(col, None)
    in_specs = (
        rows, rows, flat, flat, tall, flat, flat, tall, flat, flat, flat, tall, flat, tall, flat,
        tall, tall, kernel, kernel, wide, maps,
    )
    out_specs = (
        maps, rows, rows, flat, flat, tall, flat, flat, tall, flat, flat, flat, tall, flat, tall,
        flat, tall, tall, kernel, kernel, wide,
    )
    return jax.shard_map(
        make_body(axes), mesh=axes.mesh, in_specs=in_specs, out_specs=out_specs, check_vma=False
    )
```

```python
import jax
import jax.numpy as jnp
from jax import lax
from jax.experimental import pallas as pl
from jax.experimental.pallas import tpu as pltpu
from jax.sharding import Mesh, PartitionSpec as P

D = 768
HEADS = 12
HEAD_DIM = 64
MLP = 3072
DEC = 128
GRID = 8
PATCHES = 512
SIDE = 16
VOX = 4096
PLANE = SIDE * SIDE
BF = jnp.bfloat16
F32 = jnp.float32
VMEM_BYTES = 56 * 2**20


def cut_axis(devices, label):
    places = [getattr(item, "coords", None) for item in devices]
    if len(devices) == 1 or any(place is None for place in places):
        return [(label, len(devices), False)]
    full = [tuple(item.coords) + (item.core_on_chip,) for item in devices]
    found = []
    for axis in range(4):
        values = [place[axis] for place in full]
        if len(set(values)) > 1:
            stride = next(k for k in range(len(values)) if values[k] != values[0])
            found.append((stride, len(set(values)), axis))
    found.sort(reverse=True)
    step = 1
    for stride, size, _ in reversed(found):
        if stride != step:
            return [(label, len(devices), False)]
        step *= size
    if step != len(devices):
        return [(label, len(devices), False)]
    return [(label + "xyzc"[axis], size, axis == 3) for _, size, axis in found]


class Axes:
    def __init__(self, mesh):
        grid = mesh.devices
        wa = cut_axis(list(grid[:, 0]), "wa")
        col = cut_axis(list(grid[0, :]), "col")
        parts = wa + col
        self.sizes = {name: size for name, size, _ in parts}
        self.names = tuple(self.sizes)
        self.wa = tuple(name for name, _, _ in wa)
        self.col = tuple(name for name, _, _ in col)
        self.wa_count, self.col_count = grid.shape
        self.mesh = Mesh(grid.reshape(tuple(self.sizes.values())), self.names)
        core = [name for name, _, is_core in parts if is_core]
        links = [name for name, _, is_core in parts if not is_core]
        links.sort(key=lambda name: -self.sizes[name])
        self.order_a = tuple(links + core)
        if len(links) > 2:
            links = links[:-2] + [links[-1], links[-2]]
        self.order_b = tuple(links + core)


def swap(value, axis):
    return lax.ppermute(value, axis, [(0, 1), (1, 0)])


def turn(value, axis, size, step):
    return lax.ppermute(value, axis, [(k, (k + step) % size) for k in range(size)])


def gather_axis(value, axis, size):
    place = lax.axis_index(axis)
    if size == 2:
        mine, other = value[None], swap(value, axis)[None]
        return jnp.where(
            place == 0,
            jnp.concatenate([mine, other]),
            jnp.concatenate([other, mine]),
        )
    got = [turn(value, axis, size, step) for step in range(1, size)]
    out = jnp.zeros((size,) + value.shape, value.dtype)
    out = lax.dynamic_update_index_in_dim(out, value, place, 0)
    for step in range(1, size):
        out = lax.dynamic_update_index_in_dim(out, got[step - 1], (place - step) % size, 0)
    return out


def gather_rows(value, order, names):
    rows, columns = value.shape
    dims = []
    sizes = {name: lax.axis_size(name) for name in order}
    for name in order:
        value = gather_axis(value, name, sizes[name])
        dims.insert(0, name)
    kept = [name for name in names if name in dims]
    value = value.transpose([dims.index(name) for name in kept] + [len(dims), len(dims) + 1])
    return value.reshape(-1, columns)


def scatter_axis(value, axis, size, dim):
    place = lax.axis_index(axis)
    mine = lax.dynamic_index_in_dim(value, place, dim, False).astype(F32)
    got = [
        turn(
            lax.dynamic_index_in_dim(value, (place + step) % size, dim, False), axis, size, step
        )
        for step in range(1, size)
    ]
    for item in got:
        mine = mine + item.astype(F32)
    return mine


def scatter_rows(value, order, names):
    columns = value.shape[1]
    dims = [name for name in names if name in order]
    value = value.reshape([lax.axis_size(name) for name in dims] + [-1, columns])
    for name in reversed(order):
        dim = dims.index(name)
        dims.pop(dim)
        value = scatter_axis(value.astype(BF), name, lax.axis_size(name), dim)
    return value


def product(left, right):
    return jnp.dot(left, right, preferred_element_type=F32)


def product_rows(left, right):
    return lax.dot_general(left, right, (((0,), (0,)), ((), ())), preferred_element_type=F32)


def product_back(left, right):
    return lax.dot_general(left, right, (((1,), (1,)), ((), ())), preferred_element_type=F32)


def standardize(values, epsilon, axis):
    center = values - jnp.mean(values, axis=axis, keepdims=True)
    factor = lax.rsqrt(jnp.mean(center * center, axis=axis, keepdims=True) + epsilon)
    return (center * factor, factor)


def norm_back(upstream, normed, factor, axis):
    middle = upstream - jnp.mean(upstream, axis=axis, keepdims=True)
    return factor * (middle - normed * jnp.mean(upstream * normed, axis=axis, keepdims=True))


def gelu_exact(values):
    return jax.nn.gelu(values, approximate=False)


def local_back(function, inputs, upstream):
    return jax.vjp(function, inputs)[1](upstream)[0]


def halves(value):
    rows, columns = value.shape
    cut = value.reshape(rows // 16, 2, 8, columns)
    return (cut[:, 0], cut[:, 1])


def join_halves(low, high):
    count, _, columns = low.shape
    return jnp.concatenate(
        [low.reshape(count, 1, 8, columns), high.reshape(count, 1, 8, columns)], axis=1
    ).reshape(count * 16, columns)


def side_steps(low, high):
    place = lax.broadcasted_iota(jnp.int32, low.shape, 1)
    back = jnp.where(place == 0, 0.0, pltpu.roll(high, 1, 1))
    ahead = jnp.where(place == 7, 0.0, pltpu.roll(low, 7, 1))
    return (join_halves(back, low), join_halves(high, ahead))


def put_stack(ref, z, value):
    columns = value.shape[1]
    before, after = side_steps(*halves(value))
    ref[z, :, :columns] = before.astype(BF)
    ref[z, :, columns : 2 * columns] = value.astype(BF)
    ref[z, :, 2 * columns :] = after.astype(BF)


def silu_gate(values):
    return 1.0 / (1.0 + jnp.exp(-values))


def planes(step, carry=None):
    return lax.fori_loop(0, SIDE, step, carry)


def forward_table(raw_ref, table_ref, first, ins):
    parts, _, rows, _ = raw_ref.shape
    for k in range(9):
        for along in range(3):
            for part in range(parts):
                table_ref[
                    k * DEC + part * rows : k * DEC + (part + 1) * rows,
                    along * ins : (along + 1) * ins,
                ] = raw_ref[part, 3 * k + along, :, first : first + ins]


def backward_table(raw_ref, table_ref, first, ins):
    parts, _, rows, _ = raw_ref.shape
    for k in range(9):
        for along in range(3):
            for part in range(parts):
                table_ref[
                    along * DEC + part * rows : along * DEC + (part + 1) * rows,
                    k * ins : (k + 1) * ins,
                ] = raw_ref[part, 3 * k + 2 - along, :, first : first + ins]


def skip_table(raw_ref):
    return jnp.concatenate([raw_ref[part, 27, :, : 2 * DEC] for part in range(raw_ref.shape[0])])


def conv_planes(source, table_ref, total_ref, columns, forward):
    for z in range(SIDE + 2):
        total_ref[z] = jnp.zeros((PLANE, columns), F32)

    def step(z, _):
        if forward:
            wide = product_back(source(z), table_ref[...])
        else:
            wide = product(source(z), table_ref[...])
        none = jnp.zeros((SIDE, columns), F32)
        for along_d in (-1, 0, 1):
            parts = [
                wide[:, k * columns : (k + 1) * columns]
                for k in range(3 * along_d + 3, 3 * along_d + 6)
            ]
            to = along_d if not forward else -along_d
            early, late = (parts[0], parts[2]) if not forward else (parts[2], parts[0])
            moved = (
                parts[1]
                + jnp.concatenate([early[SIDE:], none])
                + jnp.concatenate([none, late[:-SIDE]])
            )
            total_ref[z + 1 + to] = total_ref[z + 1 + to] + moved

    planes(step)


def column_sum(value):
    return jnp.sum(value, axis=0, keepdims=True)


def map_stats(total_ref, first):
    zero = jnp.zeros((1, total_ref.shape[2]), F32)
    mean = planes(lambda z, run: run + column_sum(total_ref[z + first]), zero) / VOX

    def spread(z, run):
        center = total_ref[z + first] - mean
        return run + column_sum(center * center)

    return (mean, lax.rsqrt(planes(spread, zero) / VOX + 1e-05))


def sort_matrix():
    here = lax.broadcasted_iota(jnp.int32, (PLANE, PLANE), 0)
    there = lax.broadcasted_iota(jnp.int32, (PLANE, PLANE), 1)
    own = (here & -16) + 2 * (here & 7) + ((here >> 3) & 1)
    return (own == there).astype(F32).astype(BF)


def unit_matrix():
    here = lax.broadcasted_iota(jnp.int32, (DEC, DEC), 0)
    there = lax.broadcasted_iota(jnp.int32, (DEC, DEC), 1)
    return (here == there).astype(F32).astype(BF)


def plane_of(ref, z):
    return ref[lax.shift_right_logical(z, 1), z & 1].reshape(PLANE, ref.shape[-1])


def decoder_forward_kernel(
    block_ref, tap_ref, up_ref, raw_ref, cot_ref,
    joined_ref, hidden_ref, normed_ref, factor_ref, grad_two_ref, grad_skip_ref, section_ref,
    wide_ref, stack_ref, table_one, table_two, total_ref, skip_ref, grad_ref,
):
    forward_table(raw_ref, table_one, 0, 2 * DEC)
    forward_table(raw_ref, table_two, 2 * DEC, DEC)
    for source, rows_ref in enumerate((block_ref, tap_ref)):
        for i in range(2):
            for j in range(2):
                start = source * 8 * DEC + (i * 2 + j) * 2 * DEC
                part = product(rows_ref[...], up_ref[:, start : start + 2 * DEC])
                part = part.astype(BF).astype(F32)
                low = part[:, :DEC].reshape(GRID * GRID, 8, DEC)
                high = part[:, DEC:].reshape(GRID * GRID, 8, DEC)
                before, after = side_steps(low, high)
                for block, value in enumerate((before, join_halves(low, high), after)):
                    at = block * 2 * DEC + source * DEC
                    value = value.astype(BF).reshape(GRID, GRID, SIDE, DEC)
                    wide_ref[:, i, :, j, :, at : at + DEC] = value
                    if block == 1:
                        joined_ref[:, i, :, j, :, source * DEC : (source + 1) * DEC] = value

    conv_planes(lambda z: plane_of(wide_ref, z), table_one, total_ref, DEC, True)
    mean, factor = map_stats(total_ref, 1)
    factor_ref[...] = factor

    def act(z, _):
        normed = (total_ref[z + 1] - mean) * factor
        normed_ref[z] = normed
        value = (normed * silu_gate(normed)).astype(BF)
        hidden_ref[z] = value
        put_stack(stack_ref, z, value.astype(F32))

    planes(act)
    conv_planes(lambda z: stack_ref[z], table_two, total_ref, DEC, True)
    skip = skip_table(raw_ref)

    def skip_step(z, _):
        skip_ref[z] = product_back(plane_of(joined_ref, z), skip)

    planes(skip_step)
    mean_two, factor_two = map_stats(total_ref, 1)
    mean_skip, factor_skip = map_stats(skip_ref, 0)
    sort, unit = sort_matrix(), unit_matrix()
    zero = jnp.zeros((1, DEC), F32)

    def out_step(z, sums):
        two = (total_ref[z + 1] - mean_two) * factor_two
        side = (skip_ref[z] - mean_skip) * factor_skip
        both = two + side
        gate = silu_gate(both)
        columns = pl.ds(pl.multiple_of(z * PLANE, PLANE), PLANE)
        turned = product_back(unit, (both * gate).astype(BF)).astype(BF)
        section_ref[:, columns] = product(turned, sort).astype(BF)
        grad = product_back(sort, cot_ref[:, columns]) * (gate * (1.0 + both * (1.0 - gate)))
        total_ref[z + 1] = two
        skip_ref[z] = side
        grad_ref[z] = grad
        return (
            sums[0] + column_sum(grad),
            sums[1] + column_sum(grad * two),
            sums[2] + column_sum(grad * side),
        )

    plain, by_two, by_skip = planes(out_step, (zero, zero, zero))

    def back_step(z, _):
        middle = grad_ref[z] - plain / VOX
        grad_two_ref[z] = (factor_two * (middle - total_ref[z + 1] * (by_two / VOX))).astype(BF)
        grad_skip_ref[z] = (factor_skip * (middle - skip_ref[z] * (by_skip / VOX))).astype(BF)

    planes(back_step)


def decoder_backward_kernel(
    grad_two_ref, grad_skip_ref, normed_ref, factor_ref, raw_ref,
    grad_one_ref, rows_block_ref, rows_tap_ref,
    stack_ref, table_one, table_two, total_ref, wide_ref,
):
    backward_table(raw_ref, table_one, 0, 2 * DEC)
    backward_table(raw_ref, table_two, 2 * DEC, DEC)

    def stack_step(z, _):
        put_stack(stack_ref, z, grad_two_ref[z].astype(F32))

    planes(stack_step)
    conv_planes(lambda z: stack_ref[z], table_two, total_ref, DEC, False)
    zero = jnp.zeros((1, DEC), F32)

    def act(z, sums):
        normed = normed_ref[z]
        gate = silu_gate(normed)
        grad = total_ref[z + 1] * (gate * (1.0 + normed * (1.0 - gate)))
        total_ref[z + 1] = grad
        return (sums[0] + column_sum(grad), sums[1] + column_sum(grad * normed))

    plain, by_normed = planes(act, (zero, zero))

    def back_step(z, _):
        middle = total_ref[z + 1] - plain / VOX
        value = (factor_ref[...] * (middle - normed_ref[z] * (by_normed / VOX))).astype(BF)
        grad_one_ref[z] = value
        put_stack(stack_ref, z, value.astype(F32))

    planes(back_step)
    conv_planes(lambda z: stack_ref[z], table_one, wide_ref, 2 * DEC, False)
    skip = skip_table(raw_ref)

    def row_step(a, _):
        rows = pl.ds(pl.multiple_of(a * GRID * GRID, GRID * GRID), GRID * GRID)
        for i in range(2):
            z = 2 * a + i
            value = wide_ref[z + 1] + product(grad_skip_ref[z], skip)
            value = value.reshape(GRID, 2, 2, 8, 2 * DEC)
            for j in range(2):
                for l in range(2):
                    at = ((i * 2 + j) * 2 + l) * DEC
                    part = value[:, j, l].reshape(GRID * GRID, 2 * DEC).astype(BF)
                    rows_block_ref[rows, at : at + DEC] = part[:, :DEC]
                    rows_tap_ref[rows, at : at + DEC] = part[:, DEC:]

    lax.fori_loop(0, GRID, row_step, None)


def turn_stack(source_ref, turned_ref, unit):
    def step(z, _):
        value = source_ref[z].astype(F32)
        before, after = side_steps(*halves(value))
        columns = pl.ds(pl.multiple_of(z * PLANE, PLANE), PLANE)
        for block, item in enumerate((before, value, after)):
            turned_ref[block * DEC : (block + 1) * DEC, columns] = product_back(
                unit, item.astype(BF)
            ).astype(BF)

    planes(step)


def put_shifted(source, shifted_ref):
    columns = shifted_ref.shape[2] // 3
    for z in (0, SIDE + 1):
        shifted_ref[z] = jnp.zeros(shifted_ref.shape[1:], BF)

    def step(z, _):
        value = source(z)
        none = jnp.zeros((SIDE, columns), BF)
        shifted_ref[z + 1, :, :columns] = jnp.concatenate([none, value[:-SIDE]])
        shifted_ref[z + 1, :, columns : 2 * columns] = value
        shifted_ref[z + 1, :, 2 * columns :] = jnp.concatenate([value[SIDE:], none])

    planes(step)


def weight_grad(turned_ref, shifted_ref, out_ref, first, ins):
    parts, _, rows, _ = out_ref.shape
    for along_d in range(3):
        shifted = shifted_ref[along_d : along_d + SIDE].reshape(VOX, 3 * ins)
        table = product(turned_ref[...], shifted).astype(BF)
        for along_h in range(3):
            for block in range(3):
                slot = (along_d * 3 + along_h) * 3 + 2 - block
                for part in range(parts):
                    out_ref[part, slot, :, first : first + ins] = table[
                        block * DEC + part * rows : block * DEC + (part + 1) * rows,
                        along_h * ins : (along_h + 1) * ins,
                    ]


def decoder_weights_kernel(
    grad_two_ref, hidden_ref, grad_one_ref, joined_ref, grad_skip_ref,
    out_ref,
    turned_ref, shifted_ref, narrow_ref,
):
    unit = unit_matrix()
    turn_stack(grad_two_ref, turned_ref, unit)
    put_shifted(lambda z: hidden_ref[z], narrow_ref)
    weight_grad(turned_ref, narrow_ref, out_ref, 2 * DEC, DEC)
    turn_stack(grad_one_ref, turned_ref, unit)
    put_shifted(lambda z: joined_ref[z], shifted_ref)
    weight_grad(turned_ref, shifted_ref, out_ref, 0, 2 * DEC)

    def step(z, _):
        columns = pl.ds(pl.multiple_of(z * PLANE, PLANE), PLANE)
        turned_ref[:DEC, columns] = product_back(unit, grad_skip_ref[z]).astype(BF)

    planes(step)
    table = product(turned_ref[:DEC], joined_ref[...].reshape(VOX, 2 * DEC)).astype(BF)
    parts, _, rows, columns = out_ref.shape
    for part in range(parts):
        out_ref[part, 27, :, : 2 * DEC] = table[part * rows : (part + 1) * rows]
        out_ref[part, 27, :, 2 * DEC :] = jnp.zeros((rows, columns - 2 * DEC), BF)


def local_call(kernel, outs, scratch, work, *operands):
    vmem = pl.BlockSpec(memory_space=pltpu.VMEM)
    moved = sum(item.size * item.dtype.itemsize for item in operands)
    return pl.pallas_call(
        kernel,
        out_shape=[jax.ShapeDtypeStruct(shape, dtype) for shape, dtype in outs],
        in_specs=[vmem] * len(operands),
        out_specs=[vmem] * len(outs),
        scratch_shapes=[pltpu.VMEM(shape, dtype) for shape, dtype in scratch],
        compiler_params=pltpu.CompilerParams(vmem_limit_bytes=VMEM_BYTES),
        cost_estimate=pl.CostEstimate(flops=work, bytes_accessed=2 * moved, transcendentals=0),
    )(*operands)


MAP = (SIDE, PLANE, DEC)


def decoder_forward(block_out, tap_rows, up_full, raw, upstream):
    cube = (GRID, 2, GRID, 2, SIDE)
    return local_call(
        decoder_forward_kernel,
        [
            (cube + (2 * DEC,), BF), (MAP, BF), (MAP, F32), ((1, DEC), F32), (MAP, BF), (MAP, BF),
            ((DEC, VOX), BF),
        ],
        [
            (cube + (6 * DEC,), BF), ((SIDE, PLANE, 3 * DEC), BF), ((9 * DEC, 6 * DEC), BF),
            ((9 * DEC, 3 * DEC), BF), ((SIDE + 2, PLANE, DEC), F32), (MAP, F32), (MAP, F32),
        ],
        15 * 10**9,
        block_out, tap_rows, up_full, raw, upstream,
    )


def decoder_backward(grad_two, grad_skip, normed, factor, raw):
    return local_call(
        decoder_backward_kernel,
        [(MAP, BF), ((PATCHES, 8 * DEC), BF), ((PATCHES, 8 * DEC), BF)],
        [
            ((SIDE, PLANE, 3 * DEC), BF), ((3 * DEC, 18 * DEC), BF), ((3 * DEC, 9 * DEC), BF),
            ((SIDE + 2, PLANE, DEC), F32), ((SIDE + 2, PLANE, 2 * DEC), F32),
        ],
        12 * 10**9,
        grad_two, grad_skip, normed, factor, raw,
    )


def decoder_weights(grad_two, hidden, grad_one, joined, grad_skip, shape):
    return local_call(
        decoder_weights_kernel,
        [(shape, BF)],
        [
            ((3 * DEC, VOX), BF), ((SIDE + 2, PLANE, 6 * DEC), BF),
            ((SIDE + 2, PLANE, 3 * DEC), BF),
        ],
        12 * 10**9,
        grad_two, hidden, grad_one, joined, grad_skip,
    )[0]


def split_heads(block):
    parts = block.reshape(PATCHES, 3, HEADS, HEAD_DIM).transpose(1, 2, 0, 3)
    return (parts[0], parts[1], parts[2])


def attention_weights(queries, keys):
    scores = jnp.einsum("hqd,hkd->hqk", queries, keys, preferred_element_type=F32) * 0.125
    expo = jnp.exp(scores - jnp.max(scores, axis=-1, keepdims=True))
    return expo / jnp.sum(expo, axis=-1, keepdims=True)


def attend(block):
    queries, keys, values = split_heads(block)
    weights = attention_weights(queries, keys)
    mixed = jnp.einsum("hqk,hkd->hqd", weights.astype(BF), values, preferred_element_type=F32)
    return mixed.transpose(1, 0, 2).reshape(PATCHES, D).astype(BF)


def attend_back(block, grad_block):
    queries, keys, values = split_heads(block)
    weights = attention_weights(queries, keys)
    grad_heads = grad_block.reshape(PATCHES, HEADS, HEAD_DIM).transpose(1, 0, 2)
    grad_weights = jnp.einsum("hqd,hkd->hqk", grad_heads, values, preferred_element_type=F32)
    grad_values = jnp.einsum(
        "hqk,hqd->hkd", weights.astype(BF), grad_heads, preferred_element_type=F32
    )
    grad_scores = weights * (grad_weights - jnp.sum(grad_weights * weights, axis=-1, keepdims=True))
    grad_scores = grad_scores.astype(BF)
    grad_queries = jnp.einsum("hqk,hkd->hqd", grad_scores, keys, preferred_element_type=F32) * 0.125
    grad_keys = jnp.einsum("hqk,hqd->hkd", grad_scores, queries, preferred_element_type=F32) * 0.125
    stacked = jnp.stack([grad_queries, grad_keys, grad_values])
    return stacked.transpose(2, 0, 1, 3).reshape(PATCHES, 3 * D).astype(BF)


def make_body(axes):
    names, wa, col = axes.names, axes.wa, axes.col

    def body(
        tokens,
        tap,
        ln1_gain,
        ln1_bias,
        qkv_weight,
        query_bias,
        value_bias,
        out_weight,
        out_bias,
        ln2_gain,
        ln2_bias,
        fc1_weight,
        fc1_bias,
        fc2_weight,
        fc2_bias,
        block_up,
        tap_up,
        conv1_weight,
        conv2_weight,
        skip_weight,
        cotangent,
    ):
        rows_here = ln1_gain.shape[0]
        vectors = [
            item.reshape(rows_here, -1)
            for item in (
                ln1_gain, ln1_bias, query_bias, value_bias, out_bias, ln2_gain, ln2_bias,
                fc2_bias, fc1_bias,
            )
        ]
        vectors = jnp.concatenate(vectors, axis=1)
        extra = vectors.shape[1]
        vectors = jnp.pad(vectors, ((0, 0), (0, 128 - extra)))
        first_group = gather_rows(
            jnp.concatenate([qkv_weight, out_weight, vectors], axis=1), axes.order_a, names
        )
        fc1_full = gather_rows(fc1_weight, axes.order_b, names)
        fc2_full = gather_rows(fc2_weight, axes.order_a, names)
        up_full = gather_rows(jnp.concatenate([block_up, tap_up], axis=1), axes.order_b, names)
        qkv_full, out_full = first_group[:, : 3 * D], first_group[:, 3 * D : 4 * D]
        small = first_group[:, 4 * D : 4 * D + extra].astype(F32)
        gain_one, bias_one, query_bias_full, value_bias_full, out_shift, gain_two, bias_two, fc2_shift = (
            small[:, k] for k in range(8)
        )
        fc1_shift = small[:, 8:].reshape(-1)
        block_full, tap_full = up_full[:, : 8 * DEC], up_full[:, 8 * DEC :]

        conv_shard = jnp.concatenate([conv1_weight, conv2_weight], axis=2)
        skip_shard = jnp.pad(skip_weight, ((0, 0), (0, DEC)))
        conv_shard = jnp.concatenate([conv_shard, skip_shard[None]], axis=0)
        raw = lax.all_gather(conv_shard, col, axis=0, tiled=False)

        rows_bf = lax.all_to_all(tokens, wa, split_axis=1, concat_axis=2, tiled=True).reshape(-1, D)
        tap_rows = lax.all_to_all(tap, wa, split_axis=1, concat_axis=2, tiled=True).reshape(-1, D)
        rows = rows_bf.astype(F32)
        normed_one, factor_one = standardize(rows, 1e-06, -1)
        input_one = (normed_one * gain_one + bias_one).astype(BF)
        bias_all = jnp.concatenate([query_bias_full, jnp.zeros_like(query_bias_full), value_bias_full])
        qkv_rows = (product(input_one, qkv_full) + bias_all).astype(BF)
        attn_rows = attend(qkv_rows)
        first = rows + product(attn_rows, out_full) + out_shift
        normed_two, factor_two = standardize(first, 1e-06, -1)
        input_two = (normed_two * gain_two + bias_two).astype(BF)
        hidden = product(input_two, fc1_full) + fc1_shift
        active = gelu_exact(hidden).astype(BF)
        second = first + product(active, fc2_full) + fc2_shift
        block_out = second.astype(BF)

        upstream = lax.all_to_all(cotangent, col, split_axis=0, concat_axis=2, tiled=True)
        joined, hidden_maps, normed_c1, factor_c1, grad_c2, grad_skip, section = decoder_forward(
            block_out, tap_rows, up_full, raw, upstream.reshape(DEC, VOX)
        )
        section_out = lax.all_to_all(
            section.reshape(1, 1, DEC, VOX), col, split_axis=2, concat_axis=0, tiled=True
        )
        grad_c1, grad_up_block, grad_up_tap = decoder_backward(
            grad_c2, grad_skip, normed_c1, factor_c1, raw
        )
        conv_grads = decoder_weights(
            grad_c2, hidden_maps, grad_c1, joined.reshape(SIDE, PLANE, 2 * DEC), grad_skip, raw.shape
        )

        columns = conv_grads.shape[3]
        conv_grads = scatter_rows(
            conv_grads.reshape(-1, columns), [n for n in axes.order_a if n in col], names
        )
        wa_order = [n for n in axes.order_a if n in wa]
        conv_grads = scatter_rows(conv_grads, wa_order, names).astype(BF)
        conv_grads = gather_rows(conv_grads, wa_order, names).reshape(28, -1, columns)
        conv_grads = conv_grads.astype(F32)

        grad_ups = jnp.concatenate(
            [product_rows(block_out, grad_up_block), product_rows(tap_rows, grad_up_tap)], axis=1
        )
        grad_ups = scatter_rows(grad_ups, axes.order_b, names)
        grad_tap_rows = product_back(grad_up_tap, tap_full).astype(BF)
        grad_second = product_back(grad_up_block, block_full)
        grad_mlp = grad_second.astype(BF)
        grad_fc2 = scatter_rows(product_rows(active, grad_mlp), axes.order_a, names)
        grad_fc2_shift = jnp.sum(grad_mlp.astype(F32), axis=0)
        grad_active = product_back(grad_mlp, fc2_full)
        grad_hidden_rows = local_back(gelu_exact, hidden, grad_active).astype(BF)
        grad_fc1 = scatter_rows(product_rows(input_two, grad_hidden_rows), axes.order_b, names)
        grad_fc1_shift = jnp.sum(grad_hidden_rows.astype(F32), axis=0)
        grad_input_two = product_back(grad_hidden_rows, fc1_full)
        grad_gain_two = jnp.sum(grad_input_two * normed_two, axis=0)
        grad_bias_two = jnp.sum(grad_input_two, axis=0)
        grad_first = grad_second + norm_back(grad_input_two * gain_two, normed_two, factor_two, -1)
        grad_attn = grad_first.astype(BF)
        grad_out = product_rows(attn_rows, grad_attn)
        grad_out_shift = jnp.sum(grad_attn.astype(F32), axis=0)
        grad_mixed = product_back(grad_attn, out_full).astype(BF)
        grad_qkv = attend_back(qkv_rows, grad_mixed)
        grad_qkv_full = product_rows(input_one, grad_qkv)
        column_sums = jnp.sum(grad_qkv.astype(F32), axis=0)
        grad_input_one = product_back(grad_qkv, qkv_full)
        grad_gain_one = jnp.sum(grad_input_one * normed_one, axis=0)
        grad_bias_one = jnp.sum(grad_input_one, axis=0)
        grad_rows = grad_first + norm_back(grad_input_one * gain_one, normed_one, factor_one, -1)
        small_grads = jnp.stack(
            [
                grad_gain_one, grad_bias_one, column_sums[:D], column_sums[2 * D :], grad_out_shift,
                grad_gain_two, grad_bias_two, grad_fc2_shift,
            ],
            axis=1,
        )
        small_grads = jnp.concatenate([small_grads, grad_fc1_shift.reshape(D, -1)], axis=1)
        small_grads = jnp.pad(small_grads, ((0, 0), (0, 128 - extra)))
        first_grads = scatter_rows(
            jnp.concatenate([grad_qkv_full, grad_out, small_grads], axis=1), axes.order_a, names
        )
        small_sums = first_grads[:, 4 * D : 4 * D + extra]
        home_rows = lax.all_to_all(
            grad_rows.astype(BF).reshape(1, 1, PATCHES, D), wa, split_axis=2, concat_axis=1, tiled=True
        ).astype(F32)
        home_tap = lax.all_to_all(
            grad_tap_rows.reshape(1, 1, PATCHES, D), wa, split_axis=2, concat_axis=1, tiled=True
        ).astype(F32)
        return (
            section_out,
            home_rows,
            home_tap,
            small_sums[:, 0],
            small_sums[:, 1],
            first_grads[:, : 3 * D],
            small_sums[:, 2],
            small_sums[:, 3],
            first_grads[:, 3 * D : 4 * D],
            small_sums[:, 4],
            small_sums[:, 5],
            small_sums[:, 6],
            grad_fc1,
            small_sums[:, 8:].reshape(-1),
            grad_fc2,
            small_sums[:, 7],
            grad_ups[:, : 8 * DEC],
            grad_ups[:, 8 * DEC :],
            conv_grads[:27, :, : 2 * DEC],
            conv_grads[:27, :, 2 * DEC :],
            conv_grads[27, :, : 2 * DEC],
        )

    return body


def solution(mesh):
    axes = Axes(mesh)
    wa, col = axes.wa, axes.col
    both = wa + col
    tall, flat = P(both, None), P(both)
    rows = P(col, None, wa, None)
    maps = P(None, wa, col, None)
    kernel, wide = P(None, col, None), P(col, None)
    in_specs = (
        rows, rows, flat, flat, tall, flat, flat, tall, flat, flat, flat, tall, flat, tall, flat,
        tall, tall, kernel, kernel, wide, maps,
    )
    out_specs = (
        maps, rows, rows, flat, flat, tall, flat, flat, tall, flat, flat, flat, tall, flat, tall,
        flat, tall, tall, kernel, kernel, wide,
    )
    return jax.shard_map(
        make_body(axes), mesh=axes.mesh, in_specs=in_specs, out_specs=out_specs, check_vma=False
    )
```

```python
import jax
import jax.numpy as jnp
from jax import lax
from jax.experimental import pallas as pl
from jax.experimental.pallas import tpu as pltpu
from jax.sharding import Mesh, PartitionSpec as P

D = 768
HEADS = 12
HEAD_DIM = 64
MLP = 3072
DEC = 128
GRID = 8
PATCHES = 512
SIDE = 16
VOX = 4096
PLANE = SIDE * SIDE
BF = jnp.bfloat16
F32 = jnp.float32
VMEM_BYTES = 56 * 2**20
COST = 10**6


def cut_axis(devices, label):
    places = [getattr(item, "coords", None) for item in devices]
    if len(devices) == 1 or any(place is None for place in places):
        return [(label, len(devices), False)]
    full = [tuple(item.coords) + (item.core_on_chip,) for item in devices]
    found = []
    for axis in range(4):
        values = [place[axis] for place in full]
        if len(set(values)) > 1:
            stride = next(k for k in range(len(values)) if values[k] != values[0])
            found.append((stride, len(set(values)), axis))
    found.sort(reverse=True)
    step = 1
    for stride, size, _ in reversed(found):
        if stride != step:
            return [(label, len(devices), False)]
        step *= size
    if step != len(devices):
        return [(label, len(devices), False)]
    return [(label + "xyzc"[axis], size, axis == 3) for _, size, axis in found]


class Axes:
    def __init__(self, mesh):
        grid = mesh.devices
        wa = cut_axis(list(grid[:, 0]), "wa")
        col = cut_axis(list(grid[0, :]), "col")
        parts = wa + col
        self.sizes = {name: size for name, size, _ in parts}
        self.names = tuple(self.sizes)
        self.wa = tuple(name for name, _, _ in wa)
        self.col = tuple(name for name, _, _ in col)
        self.wa_count, self.col_count = grid.shape
        self.mesh = Mesh(grid.reshape(tuple(self.sizes.values())), self.names)
        core = [name for name, _, is_core in parts if is_core]
        links = [name for name, _, is_core in parts if not is_core]
        links.sort(key=lambda name: -self.sizes[name])
        self.core = core[0] if core else None
        self.links_a = tuple(links)
        if len(links) > 2:
            links = links[:-2] + [links[-1], links[-2]]
        self.links_b = tuple(links)

    def inside(self, names):
        return [n for n in self.links_a if n in names] + [n for n in (self.core,) if n in names]


def swap(value, axis):
    return lax.ppermute(value, axis, [(0, 1), (1, 0)])


def turn(value, axis, size, step):
    return lax.ppermute(value, axis, [(k, (k + step) % size) for k in range(size)])


def gather_axis(value, axis, size):
    place = lax.axis_index(axis)
    if size == 2:
        mine, other = value[None], swap(value, axis)[None]
        return jnp.where(
            place == 0,
            jnp.concatenate([mine, other]),
            jnp.concatenate([other, mine]),
        )
    got = [turn(value, axis, size, step) for step in range(1, size)]
    out = jnp.zeros((size,) + value.shape, value.dtype)
    out = lax.dynamic_update_index_in_dim(out, value, place, 0)
    for step in range(1, size):
        out = lax.dynamic_update_index_in_dim(out, got[step - 1], (place - step) % size, 0)
    return out


def keep_order(first, second, place, axis):
    return jnp.where(
        place == 0,
        jnp.concatenate([first, second], axis),
        jnp.concatenate([second, first], axis),
    )


def column_half(value, place):
    half = value.shape[-1] // 2
    return lax.dynamic_slice_in_dim(value, place * half, half, value.ndim - 1)


def gather_dims(value, order, names):
    dims, inner = [], value.ndim
    for name in order:
        value = gather_axis(value, name, lax.axis_size(name))
        dims.insert(0, name)
    kept = [name for name in names if name in dims]
    return value.transpose([dims.index(n) for n in kept] + [len(dims) + k for k in range(inner)])


class RowGather:
    def __init__(self, value, links, axes):
        self.axes, self.left, self.dims = axes, list(links), []
        place = lax.axis_index(axes.core)
        mine, other = column_half(value, place), column_half(value, 1 - place)
        self.value = keep_order(mine[None], swap(other, axes.core)[None], place, 0)

    def link(self):
        name = self.left.pop(0)
        self.value = gather_axis(self.value, name, lax.axis_size(name))
        self.dims.insert(0, name)

    def rows(self):
        axes, value = self.axes, self.value
        kept = [name for name in axes.names if name in self.dims]
        count = len(kept)
        value = value.transpose([self.dims.index(n) for n in kept] + [count, count + 1, count + 2])
        value = jnp.moveaxis(value, count, axes.names.index(axes.core))
        return value.reshape(-1, value.shape[-1])

    def finish(self, half):
        place = lax.axis_index(self.axes.core)
        return keep_order(half, swap(half, self.axes.core), place, 1)


def wait_for(value, *others):
    return lax.optimization_barrier((value, *others))[0]


def corner(value):
    return value.reshape(-1, value.shape[-1])[:16, :128]


def scatter_axis(value, axis, dim):
    size, place = lax.axis_size(axis), lax.axis_index(axis)
    got = [
        turn(lax.dynamic_index_in_dim(value, (place + step) % size, dim, False), axis, size, step)
        for step in range(1, size)
    ]
    total = lax.dynamic_index_in_dim(value, place, dim, False).astype(F32)
    for item in got:
        total = total + item.astype(F32)
    return total


def scatter_dims(value, order, names):
    dims = [name for name in names if name in order]
    for name in order:
        dim = dims.index(name)
        dims.pop(dim)
        value = scatter_axis(value.astype(BF), name, dim)
    return value


class RowSum:
    def __init__(self, keep, send, links, axes):
        self.axes, self.left = axes, list(reversed(links))
        self.dims = list(axes.names)
        got = swap(send, axes.core)
        self.value = (keep.astype(F32) + got.astype(F32)).astype(BF)
        columns = keep.shape[1]
        self.value = self.value.reshape([lax.axis_size(n) for n in self.dims] + [-1, columns])

    def link(self):
        name = self.left.pop(0)
        dim = self.dims.index(name)
        self.dims.pop(dim)
        self.value = scatter_axis(self.value, name, dim)
        if self.left:
            self.value = self.value.astype(BF)

    def finish(self):
        axes = self.axes
        place = lax.axis_index(axes.core)
        mine = lax.dynamic_index_in_dim(self.value, place, 0, False)
        other = lax.dynamic_index_in_dim(self.value, 1 - place, 0, False).astype(BF)
        return keep_order(mine, swap(other, axes.core).astype(F32), place, 1)


def swap_blocks(value, axes):
    return lax.all_to_all(value, axes, 0, 0, tiled=True)


def product(left, right):
    return jnp.dot(left, right, preferred_element_type=F32)


def product_rows(left, right):
    return lax.dot_general(left, right, (((0,), (0,)), ((), ())), preferred_element_type=F32)


def product_back(left, right):
    return lax.dot_general(left, right, (((1,), (1,)), ((), ())), preferred_element_type=F32)


def row_norm(values, epsilon):
    center = values - jnp.mean(values, axis=-1, keepdims=True)
    factor = lax.rsqrt(jnp.mean(center * center, axis=-1, keepdims=True) + epsilon)
    return (center * factor, factor)


def row_norm_back(upstream, normed, factor):
    middle = upstream - jnp.mean(upstream, axis=-1, keepdims=True)
    return factor * (middle - normed * jnp.mean(upstream * normed, axis=-1, keepdims=True))


def unit_matrix(size):
    here = lax.broadcasted_iota(jnp.int32, (size, size), 0)
    there = lax.broadcasted_iota(jnp.int32, (size, size), 1)
    return (here == there).astype(F32).astype(BF)


def turned(value, unit):
    return product_back(unit, value).astype(BF)


def head_masks():
    lane = lax.broadcasted_iota(jnp.int32, (PATCHES, 2 * HEAD_DIM), 1)
    return [(lane < HEAD_DIM).astype(F32).astype(BF), (lane >= HEAD_DIM).astype(F32).astype(BF)]


def low_lanes(shape):
    return lax.broadcasted_iota(jnp.int32, shape, 1) < HEAD_DIM


def attention_kernel(
    rows_ref, weight_ref,
    input_one_ref, qkv_ref, probs_ref, attn_ref, first_ref, input_two_ref, vectors_ref,
):
    rows = rows_ref[...].astype(F32)
    unit = unit_matrix(2 * HEAD_DIM)
    vectors_ref[...] = product_back(unit, weight_ref[:, 4 * D : 4 * D + DEC])[:16]
    gain_one, bias_one, query_bias, value_bias, out_shift, gain_two, bias_two = (
        vectors_ref[k : k + 1] for k in range(7)
    )
    normed, _ = row_norm(rows, 1e-06)
    input_one_ref[...] = (normed * gain_one + bias_one).astype(BF)
    for block, bias in enumerate((query_bias, None, value_bias)):
        columns = slice(block * D, (block + 1) * D)
        value = product(input_one_ref[...], weight_ref[:, columns])
        qkv_ref[:, columns] = (value if bias is None else value + bias).astype(BF)
    masks, wide_unit = head_masks(), unit_matrix(PATCHES)

    def pair_step(pair, _):
        at = pl.multiple_of(pair * 2 * HEAD_DIM, 2 * HEAD_DIM)
        columns = pl.ds(at, 2 * HEAD_DIM)
        queries = qkv_ref[:, columns]
        keys = qkv_ref[:, pl.ds(at + D, 2 * HEAD_DIM)]
        values = turned(qkv_ref[:, pl.ds(at + 2 * D, 2 * HEAD_DIM)], unit)
        mixed = []
        for head in range(2):
            scores = product_back(keys * masks[head], queries) * 0.125
            expo = jnp.exp(scores - jnp.max(scores, axis=0, keepdims=True))
            probs = (expo * (1.0 / jnp.sum(expo, axis=0, keepdims=True))).astype(BF)
            probs_ref[2 * pair + head] = probs
            part = product(values[head * HEAD_DIM : (head + 1) * HEAD_DIM], probs)
            mixed.append(part.astype(BF))
        attn_ref[:, columns] = product_back(wide_unit, jnp.concatenate(mixed)).astype(BF)

    lax.fori_loop(0, HEADS // 2, pair_step, None)
    first = rows + product(attn_ref[...], weight_ref[:, 3 * D : 4 * D]) + out_shift
    first_ref[...] = first
    normed, _ = row_norm(first, 1e-06)
    input_two_ref[...] = (normed * gain_two + bias_two).astype(BF)


CHUNK = 512


def mlp_kernel(
    input_ref, first_ref, fc1_ref, fc2_ref, fc1_shift_ref, fc2_shift_ref,
    active_ref, slope_ref, out_ref,
):
    total = first_ref[...] + fc2_shift_ref[...]
    for at in range(0, MLP, CHUNK):
        columns = slice(at, at + CHUNK)
        hidden = product(input_ref[...], fc1_ref[:, columns]) + fc1_shift_ref[:, columns]
        below = 0.5 * (1.0 + lax.erf(hidden * 0.7071067811865476))
        slope = below + hidden * (0.3989422804014327 * jnp.exp(-0.5 * hidden * hidden))
        slope_ref[:, columns] = slope.astype(BF)
        active_ref[:, columns] = (hidden * below).astype(BF)
        total = total + product(active_ref[:, columns], fc2_ref[columns])
    out_ref[...] = total.astype(BF)


def cut_columns(ref, place):
    half = ref.shape[1] // 2
    keep = pl.ds(pl.multiple_of(place * half, DEC), half)
    send = pl.ds(pl.multiple_of((1 - place) * half, DEC), half)
    return (keep, send)


def up_back_kernel(
    grad_block_ref, grad_tap_ref, block_ref, tap_ref, up_ref,
    grad_up_ref, grad_rows_ref, grad_second_ref, grad_mlp_ref, sums_ref,
):
    unit = unit_matrix(PLANE)
    for source, (grad_ref, rows_ref) in enumerate(
        ((grad_block_ref, block_ref), (grad_tap_ref, tap_ref))
    ):
        columns = slice(source * 8 * DEC, (source + 1) * 8 * DEC)
        for at in range(0, D, PLANE):
            rows = slice(at, at + PLANE)
            left = turned(rows_ref[:, rows], unit)
            grad_up_ref[rows, columns] = product(left, grad_ref[...]).astype(BF)
        back = product_back(grad_ref[...], up_ref[:, columns])
        if source == 0:
            grad_second_ref[...] = back
            grad_mlp_ref[...] = back.astype(BF)
            sums_ref[...] = column_sum(back.astype(BF).astype(F32))
        else:
            grad_rows_ref[...] = back.astype(BF)


def fc2_back_kernel(
    place_ref, grad_mlp_ref, active_ref, slope_ref, fc2_ref,
    keep_ref, send_ref, grad_hidden_ref, sums_ref,
):
    unit = unit_matrix(PLANE)
    keep, send = cut_columns(grad_mlp_ref, place_ref[0])
    for at in range(0, MLP, PLANE):
        rows = slice(at, at + PLANE)
        left = turned(active_ref[:, rows], unit)
        send_ref[rows] = product(left, grad_mlp_ref[:, send]).astype(BF)
        keep_ref[rows] = product(left, grad_mlp_ref[:, keep]).astype(BF)
    for at in range(0, MLP, CHUNK):
        rows = slice(at, at + CHUNK)
        grad = product_back(grad_mlp_ref[...], fc2_ref[rows]) * slope_ref[:, rows].astype(F32)
        grad = grad.astype(BF)
        grad_hidden_ref[:, rows] = grad
        sums_ref[:, rows] = column_sum(grad.astype(F32))


def fc1_back_kernel(
    place_ref, grad_hidden_ref, input_ref, first_ref, grad_second_ref, fc1_ref, weight_ref,
    vectors_ref,
    keep_ref, send_ref, grad_first_ref, grad_attn_ref, grad_mixed_ref, sums_ref,
):
    unit = unit_matrix(PLANE)
    keep, send = cut_columns(grad_hidden_ref, place_ref[0])
    for at in range(0, D, PLANE):
        rows = slice(at, at + PLANE)
        left = turned(input_ref[:, rows], unit)
        send_ref[rows] = product(left, grad_hidden_ref[:, send]).astype(BF)
        keep_ref[rows] = product(left, grad_hidden_ref[:, keep]).astype(BF)
    grad = product_back(grad_hidden_ref[...], fc1_ref[...])
    normed, factor = row_norm(first_ref[...], 1e-06)
    sums_ref[0:1] = column_sum(grad * normed)
    sums_ref[1:2] = column_sum(grad)
    grad = grad_second_ref[...] + row_norm_back(grad * vectors_ref[5:6], normed, factor)
    grad_first_ref[...] = grad
    grad = grad.astype(BF)
    grad_attn_ref[...] = grad
    sums_ref[2:3] = column_sum(grad.astype(F32))
    grad_mixed_ref[...] = product_back(grad, weight_ref[:, 3 * D : 4 * D]).astype(BF)


def attention_back_kernel(
    place_ref, grad_mixed_ref, grad_attn_ref, grad_first_ref, qkv_ref, probs_ref, attn_ref,
    input_ref, rows_ref, weight_ref, vectors_ref, small_ref,
    keep_ref, send_ref, grad_rows_ref,
    grad_qkv_ref, grad_ref, sums_ref,
):
    masks, unit, wide_unit = head_masks(), unit_matrix(2 * HEAD_DIM), unit_matrix(PATCHES)

    def pair_step(pair, _):
        at = pl.multiple_of(pair * 2 * HEAD_DIM, 2 * HEAD_DIM)
        columns = pl.ds(at, 2 * HEAD_DIM)
        queries = qkv_ref[:, columns]
        keys_turned = turned(qkv_ref[:, pl.ds(at + D, 2 * HEAD_DIM)], unit)
        values = qkv_ref[:, pl.ds(at + 2 * D, 2 * HEAD_DIM)]
        grads = grad_mixed_ref[:, columns]
        grad_q, grad_k, grad_v = [], [], []
        for head in range(2):
            probs = probs_ref[2 * pair + head]
            grad_probs = product_back(values * masks[head], grads)
            wide = probs.astype(F32)
            inner = jnp.sum(grad_probs * wide, axis=0, keepdims=True)
            grad_scores = (wide * (grad_probs - inner)).astype(BF)
            grad_v.append(product(probs, grads))
            grad_k.append(product(grad_scores, queries) * 0.125)
            part = product(keys_turned[head * HEAD_DIM : (head + 1) * HEAD_DIM], grad_scores)
            grad_q.append((part * 0.125).astype(BF))
        first = low_lanes((PATCHES, 2 * HEAD_DIM))
        grad_qkv_ref[:, columns] = product_back(wide_unit, jnp.concatenate(grad_q)).astype(BF)
        grad_qkv_ref[:, pl.ds(at + D, 2 * HEAD_DIM)] = jnp.where(first, *grad_k).astype(BF)
        grad_qkv_ref[:, pl.ds(at + 2 * D, 2 * HEAD_DIM)] = jnp.where(first, *grad_v).astype(BF)

    lax.fori_loop(0, HEADS // 2, pair_step, None)
    square = unit_matrix(PLANE)
    for at in range(0, D, PLANE):
        rows = slice(at, at + PLANE)
        left = turned(input_ref[:, rows], square)
        grad_ref[rows, : 3 * D] = product(left, grad_qkv_ref[...]).astype(BF)
        left = turned(attn_ref[:, rows], square)
        grad_ref[rows, 3 * D : 4 * D] = product(left, grad_attn_ref[...]).astype(BF)
    grad = product_back(grad_qkv_ref[...], weight_ref[:, : 3 * D])
    normed, factor = row_norm(rows_ref[...].astype(F32), 1e-06)
    sums_ref[...] = jnp.zeros(sums_ref.shape, F32)
    sums_ref[:16] = small_ref[...]
    sums_ref[0:1] = column_sum(grad * normed)
    sums_ref[1:2] = column_sum(grad)
    sums_ref[2:3] = column_sum(grad_qkv_ref[:, :D].astype(F32))
    sums_ref[3:4] = column_sum(grad_qkv_ref[:, 2 * D :].astype(F32))
    for at in range(0, D, DEC):
        rows = slice(at, at + DEC)
        grad_ref[rows, 4 * D : 4 * D + DEC] = turned(sums_ref[:, rows].astype(BF), unit)
        grad_ref[rows, 4 * D + DEC :] = jnp.zeros((DEC, DEC), BF)
    keep, send = cut_columns(grad_ref, place_ref[0])
    send_ref[...] = grad_ref[:, send]
    keep_ref[...] = grad_ref[:, keep]
    grad = grad_first_ref[...] + row_norm_back(grad * vectors_ref[0:1], normed, factor)
    grad_rows_ref[...] = grad.astype(BF)


def halves(value):
    rows, columns = value.shape
    cut = value.reshape(rows // 16, 2, 8, columns)
    return (cut[:, 0], cut[:, 1])


def join_halves(low, high):
    count, _, columns = low.shape
    return jnp.concatenate(
        [low.reshape(count, 1, 8, columns), high.reshape(count, 1, 8, columns)], axis=1
    ).reshape(count * 16, columns)


def side_steps(low, high):
    place = lax.broadcasted_iota(jnp.int32, low.shape, 1)
    back = jnp.where(place == 0, 0.0, pltpu.roll(high, 1, 1))
    ahead = jnp.where(place == 7, 0.0, pltpu.roll(low, 7, 1))
    return (join_halves(back, low), join_halves(high, ahead))


def put_stack(ref, z, value):
    columns = value.shape[1]
    before, after = side_steps(*halves(value))
    ref[z, :, :columns] = before.astype(BF)
    ref[z, :, columns : 2 * columns] = value.astype(BF)
    ref[z, :, 2 * columns :] = after.astype(BF)


def silu_gate(values):
    return 1.0 / (1.0 + jnp.exp(-values))


def planes(step, carry=None):
    return lax.fori_loop(0, SIDE, step, carry)


def forward_table(raw_ref, table_ref, first, ins):
    parts, _, rows, _ = raw_ref.shape
    for k in range(9):
        for along in range(3):
            for part in range(parts):
                table_ref[
                    k * DEC + part * rows : k * DEC + (part + 1) * rows,
                    along * ins : (along + 1) * ins,
                ] = raw_ref[part, 3 * k + along, :, first : first + ins]


def backward_table(raw_ref, table_ref, first, ins):
    parts, _, rows, _ = raw_ref.shape
    for k in range(9):
        for along in range(3):
            for part in range(parts):
                table_ref[
                    along * DEC + part * rows : along * DEC + (part + 1) * rows,
                    k * ins : (k + 1) * ins,
                ] = raw_ref[part, 3 * k + 2 - along, :, first : first + ins]


def skip_table(raw_ref):
    return jnp.concatenate([raw_ref[part, 27, :, : 2 * DEC] for part in range(raw_ref.shape[0])])


def conv_planes(source, table_ref, total_ref, columns, forward):
    for z in range(SIDE + 2):
        total_ref[z] = jnp.zeros((PLANE, columns), F32)

    def step(z, _):
        if forward:
            wide = product_back(source(z), table_ref[...])
        else:
            wide = product(source(z), table_ref[...])
        none = jnp.zeros((SIDE, columns), F32)
        for along_d in (-1, 0, 1):
            parts = [
                wide[:, k * columns : (k + 1) * columns]
                for k in range(3 * along_d + 3, 3 * along_d + 6)
            ]
            to = along_d if not forward else -along_d
            early, late = (parts[0], parts[2]) if not forward else (parts[2], parts[0])
            moved = (
                parts[1]
                + jnp.concatenate([early[SIDE:], none])
                + jnp.concatenate([none, late[:-SIDE]])
            )
            total_ref[z + 1 + to] = total_ref[z + 1 + to] + moved

    planes(step)


def column_sum(value):
    return jnp.sum(value, axis=0, keepdims=True)


def map_stats(total_ref, first):
    zero = jnp.zeros((1, total_ref.shape[2]), F32)
    mean = planes(lambda z, run: run + column_sum(total_ref[z + first]), zero) / VOX

    def spread(z, run):
        center = total_ref[z + first] - mean
        return run + column_sum(center * center)

    return (mean, lax.rsqrt(planes(spread, zero) / VOX + 1e-05))


def sort_matrix():
    here = lax.broadcasted_iota(jnp.int32, (PLANE, PLANE), 0)
    there = lax.broadcasted_iota(jnp.int32, (PLANE, PLANE), 1)
    own = (here & -16) + 2 * (here & 7) + ((here >> 3) & 1)
    return (own == there).astype(F32).astype(BF)


def plane_of(ref, z):
    return ref[lax.shift_right_logical(z, 1), z & 1].reshape(PLANE, ref.shape[-1])


def decoder_forward_kernel(
    block_ref, tap_ref, up_ref, raw_ref, cot_ref,
    joined_ref, hidden_ref, normed_ref, factor_ref, grad_two_ref, grad_skip_ref, section_ref,
    wide_ref, stack_ref, table_one, table_two, total_ref, skip_ref, grad_ref,
):
    forward_table(raw_ref, table_one, 0, 2 * DEC)
    forward_table(raw_ref, table_two, 2 * DEC, DEC)
    for source, rows_ref in enumerate((block_ref, tap_ref)):
        for i in range(2):
            for j in range(2):
                start = source * 8 * DEC + (i * 2 + j) * 2 * DEC
                part = product(rows_ref[...], up_ref[:, start : start + 2 * DEC])
                part = part.astype(BF).astype(F32)
                low = part[:, :DEC].reshape(GRID * GRID, 8, DEC)
                high = part[:, DEC:].reshape(GRID * GRID, 8, DEC)
                before, after = side_steps(low, high)
                for block, value in enumerate((before, join_halves(low, high), after)):
                    at = block * 2 * DEC + source * DEC
                    value = value.astype(BF).reshape(GRID, GRID, SIDE, DEC)
                    wide_ref[:, i, :, j, :, at : at + DEC] = value
                    if block == 1:
                        joined_ref[:, i, :, j, :, source * DEC : (source + 1) * DEC] = value

    conv_planes(lambda z: plane_of(wide_ref, z), table_one, total_ref, DEC, True)
    mean, factor = map_stats(total_ref, 1)
    factor_ref[...] = factor

    def act(z, _):
        normed = (total_ref[z + 1] - mean) * factor
        normed_ref[z] = normed
        value = (normed * silu_gate(normed)).astype(BF)
        hidden_ref[z] = value
        put_stack(stack_ref, z, value.astype(F32))

    planes(act)
    conv_planes(lambda z: stack_ref[z], table_two, total_ref, DEC, True)
    skip = skip_table(raw_ref)

    def skip_step(z, _):
        skip_ref[z] = product_back(plane_of(joined_ref, z), skip)

    planes(skip_step)
    mean_two, factor_two = map_stats(total_ref, 1)
    mean_skip, factor_skip = map_stats(skip_ref, 0)
    sort, unit = sort_matrix(), unit_matrix(DEC)
    zero = jnp.zeros((1, DEC), F32)

    def out_step(z, sums):
        two = (total_ref[z + 1] - mean_two) * factor_two
        side = (skip_ref[z] - mean_skip) * factor_skip
        both = two + side
        gate = silu_gate(both)
        columns = pl.ds(pl.multiple_of(z * PLANE, PLANE), PLANE)
        turned = product_back(unit, (both * gate).astype(BF)).astype(BF)
        section_ref[:, columns] = product(turned, sort).astype(BF)
        grad = product_back(sort, cot_ref[:, columns]) * (gate * (1.0 + both * (1.0 - gate)))
        total_ref[z + 1] = two
        skip_ref[z] = side
        grad_ref[z] = grad
        return (
            sums[0] + column_sum(grad),
            sums[1] + column_sum(grad * two),
            sums[2] + column_sum(grad * side),
        )

    plain, by_two, by_skip = planes(out_step, (zero, zero, zero))

    def back_step(z, _):
        middle = grad_ref[z] - plain / VOX
        grad_two_ref[z] = (factor_two * (middle - total_ref[z + 1] * (by_two / VOX))).astype(BF)
        grad_skip_ref[z] = (factor_skip * (middle - skip_ref[z] * (by_skip / VOX))).astype(BF)

    planes(back_step)


def decoder_backward_kernel(
    grad_two_ref, grad_skip_ref, normed_ref, factor_ref, raw_ref,
    grad_one_ref, rows_block_ref, rows_tap_ref,
    stack_ref, table_one, table_two, total_ref, wide_ref,
):
    backward_table(raw_ref, table_one, 0, 2 * DEC)
    backward_table(raw_ref, table_two, 2 * DEC, DEC)

    def stack_step(z, _):
        put_stack(stack_ref, z, grad_two_ref[z].astype(F32))

    planes(stack_step)
    conv_planes(lambda z: stack_ref[z], table_two, total_ref, DEC, False)
    zero = jnp.zeros((1, DEC), F32)

    def act(z, sums):
        normed = normed_ref[z]
        gate = silu_gate(normed)
        grad = total_ref[z + 1] * (gate * (1.0 + normed * (1.0 - gate)))
        total_ref[z + 1] = grad
        return (sums[0] + column_sum(grad), sums[1] + column_sum(grad * normed))

    plain, by_normed = planes(act, (zero, zero))

    def back_step(z, _):
        middle = total_ref[z + 1] - plain / VOX
        value = (factor_ref[...] * (middle - normed_ref[z] * (by_normed / VOX))).astype(BF)
        grad_one_ref[z] = value
        put_stack(stack_ref, z, value.astype(F32))

    planes(back_step)
    conv_planes(lambda z: stack_ref[z], table_one, wide_ref, 2 * DEC, False)
    skip = skip_table(raw_ref)

    def row_step(a, _):
        rows = pl.ds(pl.multiple_of(a * GRID * GRID, GRID * GRID), GRID * GRID)
        for i in range(2):
            z = 2 * a + i
            value = wide_ref[z + 1] + product(grad_skip_ref[z], skip)
            value = value.reshape(GRID, 2, 2, 8, 2 * DEC)
            for j in range(2):
                for l in range(2):
                    at = ((i * 2 + j) * 2 + l) * DEC
                    part = value[:, j, l].reshape(GRID * GRID, 2 * DEC).astype(BF)
                    rows_block_ref[rows, at : at + DEC] = part[:, :DEC]
                    rows_tap_ref[rows, at : at + DEC] = part[:, DEC:]

    lax.fori_loop(0, GRID, row_step, None)


def turn_stack(source_ref, turned_ref, unit):
    def step(z, _):
        value = source_ref[z].astype(F32)
        before, after = side_steps(*halves(value))
        columns = pl.ds(pl.multiple_of(z * PLANE, PLANE), PLANE)
        for block, item in enumerate((before, value, after)):
            turned_ref[block * DEC : (block + 1) * DEC, columns] = product_back(
                unit, item.astype(BF)
            ).astype(BF)

    planes(step)


def put_shifted(source, shifted_ref):
    columns = shifted_ref.shape[2] // 3
    for z in (0, SIDE + 1):
        shifted_ref[z] = jnp.zeros(shifted_ref.shape[1:], BF)

    def step(z, _):
        value = source(z)
        none = jnp.zeros((SIDE, columns), BF)
        shifted_ref[z + 1, :, :columns] = jnp.concatenate([none, value[:-SIDE]])
        shifted_ref[z + 1, :, columns : 2 * columns] = value
        shifted_ref[z + 1, :, 2 * columns :] = jnp.concatenate([value[SIDE:], none])

    planes(step)


def weight_grad(turned_ref, shifted_ref, out_ref, first, ins):
    parts, _, rows, _ = out_ref.shape
    for along_d in range(3):
        shifted = shifted_ref[along_d : along_d + SIDE].reshape(VOX, 3 * ins)
        table = product(turned_ref[...], shifted).astype(BF)
        for along_h in range(3):
            for block in range(3):
                slot = (along_d * 3 + along_h) * 3 + 2 - block
                for part in range(parts):
                    out_ref[part, slot, :, first : first + ins] = table[
                        block * DEC + part * rows : block * DEC + (part + 1) * rows,
                        along_h * ins : (along_h + 1) * ins,
                    ]


def decoder_weights_kernel(
    grad_two_ref, hidden_ref, grad_one_ref, joined_ref, grad_skip_ref,
    out_ref,
    turned_ref, shifted_ref, narrow_ref,
):
    unit = unit_matrix(DEC)
    turn_stack(grad_two_ref, turned_ref, unit)
    put_shifted(lambda z: hidden_ref[z], narrow_ref)
    weight_grad(turned_ref, narrow_ref, out_ref, 2 * DEC, DEC)
    turn_stack(grad_one_ref, turned_ref, unit)
    put_shifted(lambda z: joined_ref[z], shifted_ref)
    weight_grad(turned_ref, shifted_ref, out_ref, 0, 2 * DEC)

    def step(z, _):
        columns = pl.ds(pl.multiple_of(z * PLANE, PLANE), PLANE)
        turned_ref[:DEC, columns] = product_back(unit, grad_skip_ref[z]).astype(BF)

    planes(step)
    table = product(turned_ref[:DEC], joined_ref[...].reshape(VOX, 2 * DEC)).astype(BF)
    parts, _, rows, columns = out_ref.shape
    for part in range(parts):
        out_ref[part, 27, :, : 2 * DEC] = table[part * rows : (part + 1) * rows]
        out_ref[part, 27, :, 2 * DEC :] = jnp.zeros((rows, columns - 2 * DEC), BF)


def skip_operands(kernel, count, left):
    def run(*refs):
        kernel(*refs[:count], *refs[count + left :])

    return run


def local_call(kernel, outs, scratch, *operands, after=()):
    specs = [
        pl.BlockSpec(memory_space=pltpu.SMEM if item.ndim == 1 else pltpu.VMEM)
        for item in operands
    ]
    specs += [pl.BlockSpec(memory_space=pl.ANY)] * len(after)
    vmem = pl.BlockSpec(memory_space=pltpu.VMEM)
    return pl.pallas_call(
        skip_operands(kernel, len(operands), len(after)),
        out_shape=[jax.ShapeDtypeStruct(shape, dtype) for shape, dtype in outs],
        in_specs=specs,
        out_specs=[vmem] * len(outs),
        scratch_shapes=[pltpu.VMEM(shape, dtype) for shape, dtype in scratch],
        compiler_params=pltpu.CompilerParams(vmem_limit_bytes=VMEM_BYTES),
        cost_estimate=pl.CostEstimate(flops=COST, bytes_accessed=COST, transcendentals=0),
    )(*operands, *after)


MAP = (SIDE, PLANE, DEC)


def decoder_forward(*operands, after=()):
    cube = (GRID, 2, GRID, 2, SIDE)
    return local_call(
        decoder_forward_kernel,
        [
            (cube + (2 * DEC,), BF), (MAP, BF), (MAP, F32), ((1, DEC), F32), (MAP, BF), (MAP, BF),
            ((DEC, VOX), BF),
        ],
        [
            (cube + (6 * DEC,), BF), ((SIDE, PLANE, 3 * DEC), BF), ((9 * DEC, 6 * DEC), BF),
            ((9 * DEC, 3 * DEC), BF), ((SIDE + 2, PLANE, DEC), F32), (MAP, F32), (MAP, F32),
        ],
        *operands, after=after,
    )


def decoder_backward(*operands, after=()):
    return local_call(
        decoder_backward_kernel,
        [(MAP, BF), ((PATCHES, 8 * DEC), BF), ((PATCHES, 8 * DEC), BF)],
        [
            ((SIDE, PLANE, 3 * DEC), BF), ((3 * DEC, 18 * DEC), BF), ((3 * DEC, 9 * DEC), BF),
            ((SIDE + 2, PLANE, DEC), F32), ((SIDE + 2, PLANE, 2 * DEC), F32),
        ],
        *operands, after=after,
    )


def decoder_weights(*operands, shape, after=()):
    return local_call(
        decoder_weights_kernel,
        [(shape, BF)],
        [
            ((3 * DEC, VOX), BF), ((SIDE + 2, PLANE, 6 * DEC), BF),
            ((SIDE + 2, PLANE, 3 * DEC), BF),
        ],
        *operands, after=after,
    )[0]


def attention(rows, weight, after=()):
    flat = (PATCHES, D)
    return local_call(
        attention_kernel,
        [
            (flat, BF), ((PATCHES, 3 * D), BF), ((HEADS, PATCHES, PATCHES), BF), (flat, BF),
            (flat, F32), (flat, BF), ((16, D), F32),
        ],
        [], rows, weight, after=after,
    )


def mlp(rows, first, fc1, fc2, fc1_shift, fc2_shift, after=()):
    return local_call(
        mlp_kernel,
        [((PATCHES, MLP), BF), ((PATCHES, MLP), BF), ((PATCHES, D), BF)],
        [], rows, first, fc1, fc2, fc1_shift, fc2_shift, after=after,
    )


def up_back(grad_block, grad_tap, block_out, tap_rows, up_full, after=()):
    flat = (PATCHES, D)
    return local_call(
        up_back_kernel,
        [((D, 16 * DEC), BF), (flat, BF), (flat, F32), (flat, BF), ((1, D), F32)],
        [], grad_block, grad_tap, block_out, tap_rows, up_full, after=after,
    )


def fc2_back(place, grad_mlp, active, slope, fc2, after=()):
    half = ((MLP, D // 2), BF)
    return local_call(
        fc2_back_kernel,
        [half, half, ((PATCHES, MLP), BF), ((1, MLP), F32)],
        [], place, grad_mlp, active, slope, fc2, after=after,
    )


def fc1_back(place, grad_hidden, input_two, first, grad_second, fc1, weight, vectors, after=()):
    half, flat = ((D, MLP // 2), BF), (PATCHES, D)
    return local_call(
        fc1_back_kernel,
        [half, half, (flat, F32), (flat, BF), (flat, BF), ((8, D), F32)],
        [],
        place, grad_hidden, input_two, first, grad_second, fc1, weight, vectors, after=after,
    )


def attention_back(place, *operands, after=()):
    wide = 4 * D + 2 * DEC
    half = ((D, wide // 2), BF)
    return local_call(
        attention_back_kernel,
        [half, half, ((PATCHES, D), BF)],
        [((PATCHES, 3 * D), BF), ((D, wide), BF), ((DEC, D), F32)],
        place, *operands, after=after,
    )


def make_body(axes):
    names, wa, col = axes.names, axes.wa, axes.col
    both = wa + col

    def body(
        tokens,
        tap,
        ln1_gain,
        ln1_bias,
        qkv_weight,
        query_bias,
        value_bias,
        out_weight,
        out_bias,
        ln2_gain,
        ln2_bias,
        fc1_weight,
        fc1_bias,
        fc2_weight,
        fc2_bias,
        block_up,
        tap_up,
        conv1_weight,
        conv2_weight,
        skip_weight,
        cotangent,
    ):
        rows_here = ln1_gain.shape[0]
        place = lax.axis_index(axes.core).astype(jnp.int32).reshape(1)

        vectors = [
            item.reshape(rows_here, -1)
            for item in (
                ln1_gain, ln1_bias, query_bias, value_bias, out_bias, ln2_gain, ln2_bias,
                fc2_bias, fc1_bias,
            )
        ]
        vectors = jnp.concatenate(vectors, axis=1)
        extra = vectors.shape[1]
        vectors = jnp.pad(vectors, ((0, 0), (0, 2 * DEC - extra)))
        get_first = RowGather(
            jnp.concatenate([qkv_weight, out_weight, vectors], axis=1), axes.links_a, axes
        )
        get_fc1 = RowGather(fc1_weight, axes.links_b, axes)
        get_fc2 = RowGather(fc2_weight, axes.links_a, axes)
        up_full = lax.all_gather(
            jnp.concatenate([block_up, tap_up], axis=1), both, axis=0, tiled=True
        )
        conv_shard = jnp.concatenate([conv1_weight, conv2_weight], axis=2)
        skip_shard = jnp.pad(skip_weight, ((0, 0), (0, DEC)))
        conv_shard = jnp.concatenate([conv_shard, skip_shard[None]], axis=0)
        raw = lax.all_gather(conv_shard, col, axis=0, tiled=False)
        rows_bf = swap_blocks(tokens.reshape(axes.wa_count, -1, D), wa).reshape(PATCHES, D)
        get_first.link()
        get_fc1.value = wait_for(get_fc1.value, corner(get_first.value))
        get_fc1.link()
        get_first.link()
        get_fc2.value = wait_for(get_fc2.value, corner(get_fc1.value))
        get_fc2.link()
        for item in (get_first, get_fc1, get_fc2):
            while item.left:
                item.link()
        first_weight = get_first.finish(get_first.rows())
        tap = wait_for(tap, corner(get_fc2.value))
        tap_rows = swap_blocks(tap.reshape(axes.wa_count, -1, D), wa).reshape(PATCHES, D)
        cotangent = wait_for(cotangent, corner(get_fc2.value))
        upstream = swap_blocks(cotangent.reshape(axes.col_count, -1, VOX), col).reshape(DEC, VOX)

        input_one, qkv_rows, probs, attn_rows, first, input_two, vectors = attention(
            rows_bf, first_weight
        )
        fc1_full = get_fc1.finish(get_fc1.rows())
        fc2_full = get_fc2.finish(wait_for(get_fc2.rows(), corner(input_two)))
        fc1_shift = vectors[8:extra].T.reshape(1, MLP)
        active, slope, block_out = mlp(
            input_two, first, fc1_full, fc2_full, fc1_shift, vectors[7:8]
        )
        joined, hidden_maps, normed_c1, factor_c1, grad_c2, grad_skip, section = decoder_forward(
            block_out, tap_rows, up_full, raw, upstream
        )
        section_out = swap_blocks(section.reshape(axes.col_count, -1, VOX), col)

        grad_c1, grad_up_block, grad_up_tap = decoder_backward(
            grad_c2, grad_skip, normed_c1, factor_c1, raw
        )
        grad_up, grad_tap_rows, grad_second, grad_mlp, fc2_shift_sums = up_back(
            grad_up_block, grad_up_tap, block_out, tap_rows, up_full
        )
        grad_ups = lax.psum_scatter(grad_up, both, scatter_dimension=0, tiled=True).astype(F32)
        keep, send, grad_hidden, fc1_shift_sums = fc2_back(
            place, grad_mlp, active, slope, fc2_full
        )
        sum_fc2 = RowSum(keep, send, axes.links_a, axes)
        keep, send, grad_first, grad_attn, grad_mixed, sums_two = fc1_back(
            place, grad_hidden, input_two, first, grad_second, fc1_full, first_weight, vectors
        )
        sum_fc1 = RowSum(keep, send, axes.links_b, axes)
        small = jnp.concatenate(
            [
                jnp.zeros((4, D), F32), sums_two[2:3], sums_two[:2], fc2_shift_sums,
                fc1_shift_sums.reshape(D, -1).T, jnp.zeros((16 - extra, D), F32),
            ]
        )
        keep, send, grad_rows = attention_back(
            place, grad_mixed, grad_attn, grad_first, qkv_rows, probs, attn_rows, input_one,
            rows_bf, first_weight, vectors, small, after=(sum_fc2.value,),
        )
        sum_fc2.link()
        sum_first = RowSum(keep, send, axes.links_a, axes)
        conv_grads = decoder_weights(
            grad_c2, hidden_maps, grad_c1, joined.reshape(SIDE, PLANE, 2 * DEC), grad_skip,
            shape=raw.shape, after=(sum_fc1.value, sum_fc2.value),
        )
        sum_fc1.link()
        sum_fc2.link()

        columns = conv_grads.shape[3]
        conv_grads = conv_grads.reshape([lax.axis_size(n) for n in col] + [-1, columns])
        conv_grads = scatter_dims(conv_grads, axes.inside(col)[::-1], names)
        conv_grads = conv_grads.reshape([lax.axis_size(n) for n in wa] + [-1, columns])
        wa_order = axes.inside(wa)
        conv_grads = scatter_dims(conv_grads, wa_order[::-1], names).astype(BF)
        conv_grads = gather_dims(conv_grads, wa_order, names).reshape(28, -1, columns)
        conv_grads = conv_grads.astype(F32)

        home_rows = swap_blocks(grad_rows.reshape(axes.wa_count, -1, D), wa).astype(F32)[None]
        home_tap = swap_blocks(grad_tap_rows.reshape(axes.wa_count, -1, D), wa).astype(F32)[None]
        sums = (sum_fc2, sum_fc1, sum_first)
        for item in sums:
            while item.left:
                item.link()
        grad_fc2, grad_fc1, first_grads = (item.finish() for item in sums)
        small_sums = first_grads[:, 4 * D : 4 * D + extra]
        return (
            section_out[:, None],
            home_rows,
            home_tap,
            small_sums[:, 0],
            small_sums[:, 1],
            first_grads[:, : 3 * D],
            small_sums[:, 2],
            small_sums[:, 3],
            first_grads[:, 3 * D : 4 * D],
            small_sums[:, 4],
            small_sums[:, 5],
            small_sums[:, 6],
            grad_fc1,
            small_sums[:, 8:extra].reshape(-1),
            grad_fc2,
            small_sums[:, 7],
            grad_ups[:, : 8 * DEC],
            grad_ups[:, 8 * DEC :],
            conv_grads[:27, :, : 2 * DEC],
            conv_grads[:27, :, 2 * DEC :],
            conv_grads[27, :, : 2 * DEC],
        )

    return body


def solution(mesh):
    axes = Axes(mesh)
    wa, col = axes.wa, axes.col
    both = wa + col
    tall, flat = P(both, None), P(both)
    rows = P(col, None, wa, None)
    maps = P(None, wa, col, None)
    kernel, wide = P(None, col, None), P(col, None)
    in_specs = (
        rows, rows, flat, flat, tall, flat, flat, tall, flat, flat, flat, tall, flat, tall, flat,
        tall, tall, kernel, kernel, wide, maps,
    )
    out_specs = (
        maps, rows, rows, flat, flat, tall, flat, flat, tall, flat, flat, flat, tall, flat, tall,
        flat, tall, tall, kernel, kernel, wide,
    )
    return jax.shard_map(
        make_body(axes), mesh=axes.mesh, in_specs=in_specs, out_specs=out_specs, check_vma=False
    )
```

```python
import jax
import jax.numpy as jnp
from jax import lax
from jax.experimental import pallas as pl
from jax.experimental.pallas import tpu as pltpu
from jax.sharding import Mesh, PartitionSpec as P

D = 768
HEADS = 12
HEAD_DIM = 64
MLP = 3072
DEC = 128
GRID = 8
PATCHES = 512
SIDE = 16
VOX = 4096
PLANE = SIDE * SIDE
BF = jnp.bfloat16
F32 = jnp.float32
VMEM_BYTES = 56 * 2**20
COST = 3 * 10**10


def cut_axis(devices, label):
    places = [getattr(item, "coords", None) for item in devices]
    if len(devices) == 1 or any(place is None for place in places):
        return [(label, len(devices), False)]
    full = [tuple(item.coords) + (item.core_on_chip,) for item in devices]
    found = []
    for axis in range(4):
        values = [place[axis] for place in full]
        if len(set(values)) > 1:
            stride = next(k for k in range(len(values)) if values[k] != values[0])
            found.append((stride, len(set(values)), axis))
    found.sort(reverse=True)
    step = 1
    for stride, size, _ in reversed(found):
        if stride != step:
            return [(label, len(devices), False)]
        step *= size
    if step != len(devices):
        return [(label, len(devices), False)]
    return [(label + "xyzc"[axis], size, axis == 3) for _, size, axis in found]


class Axes:
    def __init__(self, mesh):
        grid = mesh.devices
        wa = cut_axis(list(grid[:, 0]), "wa")
        col = cut_axis(list(grid[0, :]), "col")
        parts = wa + col
        self.sizes = {name: size for name, size, _ in parts}
        self.names = tuple(self.sizes)
        self.wa = tuple(name for name, _, _ in wa)
        self.col = tuple(name for name, _, _ in col)
        self.wa_count, self.col_count = grid.shape
        self.mesh = Mesh(grid.reshape(tuple(self.sizes.values())), self.names)
        core = [name for name, _, is_core in parts if is_core]
        links = [name for name, _, is_core in parts if not is_core]
        links.sort(key=lambda name: -self.sizes[name])
        self.core = core[0] if core else None
        self.links_a = tuple(links)
        if len(links) > 2:
            links = links[:-2] + [links[-1], links[-2]]
        self.links_b = tuple(links)

    def inside(self, names):
        return [n for n in self.links_a if n in names] + [n for n in (self.core,) if n in names]


def swap(value, axis):
    return lax.ppermute(value, axis, [(0, 1), (1, 0)])


def turn(value, axis, size, step):
    return lax.ppermute(value, axis, [(k, (k + step) % size) for k in range(size)])


def gather_axis(value, axis, size):
    place = lax.axis_index(axis)
    if size == 2:
        mine, other = value[None], swap(value, axis)[None]
        return jnp.where(
            place == 0,
            jnp.concatenate([mine, other]),
            jnp.concatenate([other, mine]),
        )
    got = [turn(value, axis, size, step) for step in range(1, size)]
    out = jnp.zeros((size,) + value.shape, value.dtype)
    out = lax.dynamic_update_index_in_dim(out, value, place, 0)
    for step in range(1, size):
        out = lax.dynamic_update_index_in_dim(out, got[step - 1], (place - step) % size, 0)
    return out


def keep_order(first, second, place, axis):
    return jnp.where(
        place == 0,
        jnp.concatenate([first, second], axis),
        jnp.concatenate([second, first], axis),
    )


def column_half(value, place):
    half = value.shape[-1] // 2
    return lax.dynamic_slice_in_dim(value, place * half, half, value.ndim - 1)


def gather_dims(value, order, names):
    dims, inner = [], value.ndim
    for name in order:
        value = gather_axis(value, name, lax.axis_size(name))
        dims.insert(0, name)
    kept = [name for name in names if name in dims]
    return value.transpose([dims.index(n) for n in kept] + [len(dims) + k for k in range(inner)])


class RowGather:
    def __init__(self, value, links, axes):
        self.axes, self.left, self.dims = axes, list(links), []
        place = lax.axis_index(axes.core)
        mine, other = column_half(value, place), column_half(value, 1 - place)
        self.value = keep_order(mine[None], swap(other, axes.core)[None], place, 0)

    def link(self):
        name = self.left.pop(0)
        self.value = gather_axis(self.value, name, lax.axis_size(name))
        self.dims.insert(0, name)

    def rows(self):
        axes, value = self.axes, self.value
        kept = [name for name in axes.names if name in self.dims]
        count = len(kept)
        value = value.transpose([self.dims.index(n) for n in kept] + [count, count + 1, count + 2])
        value = jnp.moveaxis(value, count, axes.names.index(axes.core))
        return value.reshape(-1, value.shape[-1])

    def finish(self, half):
        place = lax.axis_index(self.axes.core)
        return keep_order(half, swap(half, self.axes.core), place, 1)


def wait_for(value, *others):
    return lax.optimization_barrier((value, *others))[0]


def corner(value):
    return value.reshape(-1, value.shape[-1])[:16, :128]


def scatter_axis(value, axis, dim):
    size, place = lax.axis_size(axis), lax.axis_index(axis)
    got = [
        turn(lax.dynamic_index_in_dim(value, (place + step) % size, dim, False), axis, size, step)
        for step in range(1, size)
    ]
    total = lax.dynamic_index_in_dim(value, place, dim, False).astype(F32)
    for item in got:
        total = total + item.astype(F32)
    return total


def scatter_dims(value, order, names):
    dims = [name for name in names if name in order]
    for name in order:
        dim = dims.index(name)
        dims.pop(dim)
        value = scatter_axis(value.astype(BF), name, dim)
    return value


class RowSum:
    def __init__(self, keep, send, links, axes):
        self.axes, self.left = axes, list(reversed(links))
        self.dims = list(axes.names)
        got = swap(send, axes.core)
        self.value = (keep.astype(F32) + got.astype(F32)).astype(BF)
        columns = keep.shape[1]
        self.value = self.value.reshape([lax.axis_size(n) for n in self.dims] + [-1, columns])

    def link(self):
        name = self.left.pop(0)
        dim = self.dims.index(name)
        self.dims.pop(dim)
        self.value = scatter_axis(self.value, name, dim)
        if self.left:
            self.value = self.value.astype(BF)

    def finish(self):
        axes = self.axes
        place = lax.axis_index(axes.core)
        mine = lax.dynamic_index_in_dim(self.value, place, 0, False)
        other = lax.dynamic_index_in_dim(self.value, 1 - place, 0, False).astype(BF)
        return keep_order(mine, swap(other, axes.core).astype(F32), place, 1)


def swap_blocks(value, axes):
    return lax.all_to_all(value, axes, 0, 0, tiled=True)


def product(left, right):
    return jnp.dot(left, right, preferred_element_type=F32)


def product_rows(left, right):
    return lax.dot_general(left, right, (((0,), (0,)), ((), ())), preferred_element_type=F32)


def product_back(left, right):
    return lax.dot_general(left, right, (((1,), (1,)), ((), ())), preferred_element_type=F32)


def row_norm(values, epsilon):
    center = values - jnp.mean(values, axis=-1, keepdims=True)
    factor = lax.rsqrt(jnp.mean(center * center, axis=-1, keepdims=True) + epsilon)
    return (center * factor, factor)


def row_norm_back(upstream, normed, factor):
    middle = upstream - jnp.mean(upstream, axis=-1, keepdims=True)
    return factor * (middle - normed * jnp.mean(upstream * normed, axis=-1, keepdims=True))


def unit_matrix(size):
    here = lax.broadcasted_iota(jnp.int32, (size, size), 0)
    there = lax.broadcasted_iota(jnp.int32, (size, size), 1)
    return (here == there).astype(F32).astype(BF)


def turned(value, unit):
    return product_back(unit, value).astype(BF)


def head_masks():
    lane = lax.broadcasted_iota(jnp.int32, (PATCHES, 2 * HEAD_DIM), 1)
    return [(lane < HEAD_DIM).astype(F32).astype(BF), (lane >= HEAD_DIM).astype(F32).astype(BF)]


def low_lanes(shape):
    return lax.broadcasted_iota(jnp.int32, shape, 1) < HEAD_DIM


def attention_kernel(
    rows_ref, weight_ref,
    input_one_ref, qkv_ref, probs_ref, attn_ref, first_ref, input_two_ref, vectors_ref,
):
    rows = rows_ref[...].astype(F32)
    unit = unit_matrix(2 * HEAD_DIM)
    vectors_ref[...] = product_back(unit, weight_ref[:, 4 * D : 4 * D + DEC])[:16]
    gain_one, bias_one, query_bias, value_bias, out_shift, gain_two, bias_two = (
        vectors_ref[k : k + 1] for k in range(7)
    )
    normed, _ = row_norm(rows, 1e-06)
    input_one_ref[...] = (normed * gain_one + bias_one).astype(BF)
    for block, bias in enumerate((query_bias, None, value_bias)):
        columns = slice(block * D, (block + 1) * D)
        value = product(input_one_ref[...], weight_ref[:, columns])
        qkv_ref[:, columns] = (value if bias is None else value + bias).astype(BF)
    masks, wide_unit = head_masks(), unit_matrix(PATCHES)

    def pair_step(pair, _):
        at = pl.multiple_of(pair * 2 * HEAD_DIM, 2 * HEAD_DIM)
        columns = pl.ds(at, 2 * HEAD_DIM)
        queries = qkv_ref[:, columns]
        keys = qkv_ref[:, pl.ds(at + D, 2 * HEAD_DIM)]
        values = turned(qkv_ref[:, pl.ds(at + 2 * D, 2 * HEAD_DIM)], unit)
        mixed = []
        for head in range(2):
            scores = product_back(keys * masks[head], queries) * 0.125
            expo = jnp.exp(scores - jnp.max(scores, axis=0, keepdims=True))
            probs = (expo * (1.0 / jnp.sum(expo, axis=0, keepdims=True))).astype(BF)
            probs_ref[2 * pair + head] = probs
            part = product(values[head * HEAD_DIM : (head + 1) * HEAD_DIM], probs)
            mixed.append(part.astype(BF))
        attn_ref[:, columns] = product_back(wide_unit, jnp.concatenate(mixed)).astype(BF)

    lax.fori_loop(0, HEADS // 2, pair_step, None, unroll=PAIRS)
    first = rows + product(attn_ref[...], weight_ref[:, 3 * D : 4 * D]) + out_shift
    first_ref[...] = first
    normed, _ = row_norm(first, 1e-06)
    input_two_ref[...] = (normed * gain_two + bias_two).astype(BF)


CHUNK = 512


def mlp_kernel(
    input_ref, first_ref, fc1_ref, fc2_ref, fc1_shift_ref, fc2_shift_ref,
    active_ref, slope_ref, out_ref,
):
    total = first_ref[...] + fc2_shift_ref[...]
    for at in range(0, MLP, CHUNK):
        columns = slice(at, at + CHUNK)
        hidden = product(input_ref[...], fc1_ref[:, columns]) + fc1_shift_ref[:, columns]
        below = 0.5 * (1.0 + lax.erf(hidden * 0.7071067811865476))
        slope = below + hidden * (0.3989422804014327 * jnp.exp(-0.5 * hidden * hidden))
        slope_ref[:, columns] = slope.astype(BF)
        active_ref[:, columns] = (hidden * below).astype(BF)
        total = total + product(active_ref[:, columns], fc2_ref[columns])
    out_ref[...] = total.astype(BF)


def cut_columns(ref, place):
    half = ref.shape[1] // 2
    keep = pl.ds(pl.multiple_of(place * half, DEC), half)
    send = pl.ds(pl.multiple_of((1 - place) * half, DEC), half)
    return (keep, send)


def up_back_kernel(
    grad_block_ref, grad_tap_ref, block_ref, tap_ref, up_ref,
    grad_up_ref, grad_rows_ref, grad_second_ref, grad_mlp_ref, sums_ref,
):
    unit = unit_matrix(PLANE)
    for source, (grad_ref, rows_ref) in enumerate(
        ((grad_block_ref, block_ref), (grad_tap_ref, tap_ref))
    ):
        columns = slice(source * 8 * DEC, (source + 1) * 8 * DEC)
        for at in range(0, D, PLANE):
            rows = slice(at, at + PLANE)
            left = turned(rows_ref[:, rows], unit)
            grad_up_ref[rows, columns] = product(left, grad_ref[...]).astype(BF)
        back = product_back(grad_ref[...], up_ref[:, columns])
        if source == 0:
            grad_second_ref[...] = back
            grad_mlp_ref[...] = back.astype(BF)
            sums_ref[...] = column_sum(back.astype(BF).astype(F32))
        else:
            grad_rows_ref[...] = back.astype(BF)


def fc2_back_kernel(
    place_ref, grad_mlp_ref, active_ref, slope_ref, fc2_ref,
    keep_ref, send_ref, grad_hidden_ref, sums_ref,
):
    unit = unit_matrix(PLANE)
    keep, send = cut_columns(grad_mlp_ref, place_ref[0])
    for at in range(0, MLP, PLANE):
        rows = slice(at, at + PLANE)
        left = turned(active_ref[:, rows], unit)
        send_ref[rows] = product(left, grad_mlp_ref[:, send]).astype(BF)
        keep_ref[rows] = product(left, grad_mlp_ref[:, keep]).astype(BF)
    for at in range(0, MLP, CHUNK):
        rows = slice(at, at + CHUNK)
        grad = product_back(grad_mlp_ref[...], fc2_ref[rows]) * slope_ref[:, rows].astype(F32)
        grad = grad.astype(BF)
        grad_hidden_ref[:, rows] = grad
        sums_ref[:, rows] = column_sum(grad.astype(F32))


def fc1_back_kernel(
    place_ref, grad_hidden_ref, input_ref, first_ref, grad_second_ref, fc1_ref, weight_ref,
    vectors_ref,
    keep_ref, send_ref, grad_first_ref, grad_attn_ref, grad_mixed_ref, sums_ref,
):
    unit = unit_matrix(PLANE)
    keep, send = cut_columns(grad_hidden_ref, place_ref[0])
    for at in range(0, D, PLANE):
        rows = slice(at, at + PLANE)
        left = turned(input_ref[:, rows], unit)
        send_ref[rows] = product(left, grad_hidden_ref[:, send]).astype(BF)
        keep_ref[rows] = product(left, grad_hidden_ref[:, keep]).astype(BF)
    grad = product_back(grad_hidden_ref[...], fc1_ref[...])
    normed, factor = row_norm(first_ref[...], 1e-06)
    sums_ref[0:1] = column_sum(grad * normed)
    sums_ref[1:2] = column_sum(grad)
    grad = grad_second_ref[...] + row_norm_back(grad * vectors_ref[5:6], normed, factor)
    grad_first_ref[...] = grad
    grad = grad.astype(BF)
    grad_attn_ref[...] = grad
    sums_ref[2:3] = column_sum(grad.astype(F32))
    grad_mixed_ref[...] = product_back(grad, weight_ref[:, 3 * D : 4 * D]).astype(BF)


def attention_back_kernel(
    place_ref, grad_mixed_ref, grad_attn_ref, grad_first_ref, qkv_ref, probs_ref, attn_ref,
    input_ref, rows_ref, weight_ref, vectors_ref, small_ref,
    keep_ref, send_ref, grad_rows_ref,
    grad_qkv_ref, grad_ref, sums_ref,
):
    masks, unit, wide_unit = head_masks(), unit_matrix(2 * HEAD_DIM), unit_matrix(PATCHES)

    def pair_step(pair, _):
        at = pl.multiple_of(pair * 2 * HEAD_DIM, 2 * HEAD_DIM)
        columns = pl.ds(at, 2 * HEAD_DIM)
        queries = qkv_ref[:, columns]
        keys_turned = turned(qkv_ref[:, pl.ds(at + D, 2 * HEAD_DIM)], unit)
        values = qkv_ref[:, pl.ds(at + 2 * D, 2 * HEAD_DIM)]
        grads = grad_mixed_ref[:, columns]
        grad_q, grad_k, grad_v = [], [], []
        for head in range(2):
            probs = probs_ref[2 * pair + head]
            grad_probs = product_back(values * masks[head], grads)
            wide = probs.astype(F32)
            inner = jnp.sum(grad_probs * wide, axis=0, keepdims=True)
            grad_scores = (wide * (grad_probs - inner)).astype(BF)
            grad_v.append(product(probs, grads))
            grad_k.append(product(grad_scores, queries) * 0.125)
            part = product(keys_turned[head * HEAD_DIM : (head + 1) * HEAD_DIM], grad_scores)
            grad_q.append((part * 0.125).astype(BF))
        first = low_lanes((PATCHES, 2 * HEAD_DIM))
        grad_qkv_ref[:, columns] = product_back(wide_unit, jnp.concatenate(grad_q)).astype(BF)
        grad_qkv_ref[:, pl.ds(at + D, 2 * HEAD_DIM)] = jnp.where(first, *grad_k).astype(BF)
        grad_qkv_ref[:, pl.ds(at + 2 * D, 2 * HEAD_DIM)] = jnp.where(first, *grad_v).astype(BF)

    lax.fori_loop(0, HEADS // 2, pair_step, None, unroll=PAIRS)
    square = unit_matrix(PLANE)
    for at in range(0, D, PLANE):
        rows = slice(at, at + PLANE)
        left = turned(input_ref[:, rows], square)
        grad_ref[rows, : 3 * D] = product(left, grad_qkv_ref[...]).astype(BF)
        left = turned(attn_ref[:, rows], square)
        grad_ref[rows, 3 * D : 4 * D] = product(left, grad_attn_ref[...]).astype(BF)
    grad = product_back(grad_qkv_ref[...], weight_ref[:, : 3 * D])
    normed, factor = row_norm(rows_ref[...].astype(F32), 1e-06)
    sums_ref[...] = jnp.zeros(sums_ref.shape, F32)
    sums_ref[:16] = small_ref[...]
    sums_ref[0:1] = column_sum(grad * normed)
    sums_ref[1:2] = column_sum(grad)
    sums_ref[2:3] = column_sum(grad_qkv_ref[:, :D].astype(F32))
    sums_ref[3:4] = column_sum(grad_qkv_ref[:, 2 * D :].astype(F32))
    for at in range(0, D, DEC):
        rows = slice(at, at + DEC)
        grad_ref[rows, 4 * D : 4 * D + DEC] = turned(sums_ref[:, rows].astype(BF), unit)
        grad_ref[rows, 4 * D + DEC :] = jnp.zeros((DEC, DEC), BF)
    keep, send = cut_columns(grad_ref, place_ref[0])
    send_ref[...] = grad_ref[:, send]
    keep_ref[...] = grad_ref[:, keep]
    grad = grad_first_ref[...] + row_norm_back(grad * vectors_ref[0:1], normed, factor)
    grad_rows_ref[...] = grad.astype(BF)


def halves(value):
    rows, columns = value.shape
    cut = value.reshape(rows // 16, 2, 8, columns)
    return (cut[:, 0], cut[:, 1])


def join_halves(low, high):
    count, _, columns = low.shape
    return jnp.concatenate(
        [low.reshape(count, 1, 8, columns), high.reshape(count, 1, 8, columns)], axis=1
    ).reshape(count * 16, columns)


def side_steps(low, high):
    place = lax.broadcasted_iota(jnp.int32, low.shape, 1)
    back = jnp.where(place == 0, 0.0, pltpu.roll(high, 1, 1))
    ahead = jnp.where(place == 7, 0.0, pltpu.roll(low, 7, 1))
    return (join_halves(back, low), join_halves(high, ahead))


def put_stack(ref, z, value):
    columns = value.shape[1]
    before, after = side_steps(*halves(value))
    ref[z, :, :columns] = before.astype(BF)
    ref[z, :, columns : 2 * columns] = value.astype(BF)
    ref[z, :, 2 * columns :] = after.astype(BF)


def silu_gate(values):
    return 1.0 / (1.0 + jnp.exp(-values))


UNROLL = 4
PAIRS = 3


def planes(step, carry=None):
    return lax.fori_loop(0, SIDE, step, carry, unroll=UNROLL)


def forward_table(raw_ref, table_ref, first, ins):
    parts, _, rows, _ = raw_ref.shape
    for k in range(9):
        for along in range(3):
            for part in range(parts):
                table_ref[
                    k * DEC + part * rows : k * DEC + (part + 1) * rows,
                    along * ins : (along + 1) * ins,
                ] = raw_ref[part, 3 * k + along, :, first : first + ins]


def backward_table(raw_ref, table_ref, first, ins):
    parts, _, rows, _ = raw_ref.shape
    for k in range(9):
        for along in range(3):
            for part in range(parts):
                table_ref[
                    along * DEC + part * rows : along * DEC + (part + 1) * rows,
                    k * ins : (k + 1) * ins,
                ] = raw_ref[part, 3 * k + 2 - along, :, first : first + ins]


def skip_table(raw_ref):
    return jnp.concatenate([raw_ref[part, 27, :, : 2 * DEC] for part in range(raw_ref.shape[0])])


GROUP = 4


def conv_planes(source, table_ref, total_ref, columns, forward):
    for z in range(SIDE + 2):
        total_ref[z] = jnp.zeros((PLANE, columns), F32)

    def step(group, _):
        start = group * GROUP
        value = jnp.concatenate([source(start + k) for k in range(GROUP)])
        if forward:
            wide = product_back(value, table_ref[...])
        else:
            wide = product(value, table_ref[...])
        none = jnp.zeros((SIDE, columns), F32)
        for plane in range(GROUP):
            for along_d in (-1, 0, 1):
                parts = [
                    wide[plane * PLANE : (plane + 1) * PLANE, k * columns : (k + 1) * columns]
                    for k in range(3 * along_d + 3, 3 * along_d + 6)
                ]
                to = along_d if not forward else -along_d
                early, late = (parts[0], parts[2]) if not forward else (parts[2], parts[0])
                moved = (
                    parts[1]
                    + jnp.concatenate([early[SIDE:], none])
                    + jnp.concatenate([none, late[:-SIDE]])
                )
                at = start + plane + 1 + to
                total_ref[at] = total_ref[at] + moved

    lax.fori_loop(0, SIDE // GROUP, step, None)


def column_sum(value):
    return jnp.sum(value, axis=0, keepdims=True)


def row_sums(value):
    return jnp.sum(value.reshape(-1, 8, value.shape[1]), axis=0)


def map_stats(total_ref, first):
    zero = jnp.zeros((8, total_ref.shape[2]), F32)
    mean = planes(lambda z, run: run + row_sums(total_ref[z + first]), zero)
    mean = column_sum(mean) / VOX

    def spread(z, run):
        center = total_ref[z + first] - mean
        return run + row_sums(center * center)

    return (mean, lax.rsqrt(column_sum(planes(spread, zero)) / VOX + 1e-05))


def sort_matrix():
    here = lax.broadcasted_iota(jnp.int32, (PLANE, PLANE), 0)
    there = lax.broadcasted_iota(jnp.int32, (PLANE, PLANE), 1)
    own = (here & -16) + 2 * (here & 7) + ((here >> 3) & 1)
    return (own == there).astype(F32).astype(BF)


def plane_of(ref, z):
    return ref[lax.shift_right_logical(z, 1), z & 1].reshape(PLANE, ref.shape[-1])


def decoder_forward_kernel(
    block_ref, tap_ref, up_ref, raw_ref, cot_ref,
    joined_ref, hidden_ref, normed_ref, factor_ref, grad_two_ref, grad_skip_ref, section_ref,
    wide_ref, stack_ref, table_one, table_two, total_ref, skip_ref, grad_ref,
):
    forward_table(raw_ref, table_one, 0, 2 * DEC)
    forward_table(raw_ref, table_two, 2 * DEC, DEC)
    for source, rows_ref in enumerate((block_ref, tap_ref)):
        for i in range(2):
            for j in range(2):
                start = source * 8 * DEC + (i * 2 + j) * 2 * DEC
                part = product(rows_ref[...], up_ref[:, start : start + 2 * DEC])
                part = part.astype(BF).astype(F32)
                low = part[:, :DEC].reshape(GRID * GRID, 8, DEC)
                high = part[:, DEC:].reshape(GRID * GRID, 8, DEC)
                before, after = side_steps(low, high)
                for block, value in enumerate((before, join_halves(low, high), after)):
                    at = block * 2 * DEC + source * DEC
                    value = value.astype(BF).reshape(GRID, GRID, SIDE, DEC)
                    wide_ref[:, i, :, j, :, at : at + DEC] = value
                    if block == 1:
                        joined_ref[:, i, :, j, :, source * DEC : (source + 1) * DEC] = value

    conv_planes(lambda z: plane_of(wide_ref, z), table_one, total_ref, DEC, True)
    mean, factor = map_stats(total_ref, 1)
    factor_ref[...] = factor

    def act(z, _):
        normed = (total_ref[z + 1] - mean) * factor
        normed_ref[z] = normed
        value = (normed * silu_gate(normed)).astype(BF)
        hidden_ref[z] = value
        put_stack(stack_ref, z, value.astype(F32))

    planes(act)
    conv_planes(lambda z: stack_ref[z], table_two, total_ref, DEC, True)
    skip = skip_table(raw_ref)

    def skip_step(z, _):
        skip_ref[z] = product_back(plane_of(joined_ref, z), skip)

    planes(skip_step)
    mean_two, factor_two = map_stats(total_ref, 1)
    mean_skip, factor_skip = map_stats(skip_ref, 0)
    sort, unit = sort_matrix(), unit_matrix(DEC)
    zero = jnp.zeros((8, DEC), F32)

    def out_step(z, sums):
        two = (total_ref[z + 1] - mean_two) * factor_two
        side = (skip_ref[z] - mean_skip) * factor_skip
        both = two + side
        gate = silu_gate(both)
        columns = pl.ds(pl.multiple_of(z * PLANE, PLANE), PLANE)
        turned = product_back(unit, (both * gate).astype(BF)).astype(BF)
        section_ref[:, columns] = product(turned, sort).astype(BF)
        grad = product_back(sort, cot_ref[:, columns]) * (gate * (1.0 + both * (1.0 - gate)))
        total_ref[z + 1] = two
        skip_ref[z] = side
        grad_ref[z] = grad
        return (
            sums[0] + row_sums(grad),
            sums[1] + row_sums(grad * two),
            sums[2] + row_sums(grad * side),
        )

    plain, by_two, by_skip = (column_sum(item) for item in planes(out_step, (zero, zero, zero)))

    def back_step(z, _):
        middle = grad_ref[z] - plain / VOX
        grad_two_ref[z] = (factor_two * (middle - total_ref[z + 1] * (by_two / VOX))).astype(BF)
        grad_skip_ref[z] = (factor_skip * (middle - skip_ref[z] * (by_skip / VOX))).astype(BF)

    planes(back_step)


def decoder_backward_kernel(
    grad_two_ref, grad_skip_ref, normed_ref, factor_ref, raw_ref,
    grad_one_ref, rows_block_ref, rows_tap_ref,
    stack_ref, table_one, table_two, total_ref, wide_ref,
):
    backward_table(raw_ref, table_one, 0, 2 * DEC)
    backward_table(raw_ref, table_two, 2 * DEC, DEC)

    def stack_step(z, _):
        put_stack(stack_ref, z, grad_two_ref[z].astype(F32))

    planes(stack_step)
    conv_planes(lambda z: stack_ref[z], table_two, total_ref, DEC, False)
    zero = jnp.zeros((8, DEC), F32)

    def act(z, sums):
        normed = normed_ref[z]
        gate = silu_gate(normed)
        grad = total_ref[z + 1] * (gate * (1.0 + normed * (1.0 - gate)))
        total_ref[z + 1] = grad
        return (sums[0] + row_sums(grad), sums[1] + row_sums(grad * normed))

    plain, by_normed = (column_sum(item) for item in planes(act, (zero, zero)))

    def back_step(z, _):
        middle = total_ref[z + 1] - plain / VOX
        value = (factor_ref[...] * (middle - normed_ref[z] * (by_normed / VOX))).astype(BF)
        grad_one_ref[z] = value
        put_stack(stack_ref, z, value.astype(F32))

    planes(back_step)
    conv_planes(lambda z: stack_ref[z], table_one, wide_ref, 2 * DEC, False)
    skip = skip_table(raw_ref)

    def row_step(a, _):
        rows = pl.ds(pl.multiple_of(a * GRID * GRID, GRID * GRID), GRID * GRID)
        for i in range(2):
            z = 2 * a + i
            value = wide_ref[z + 1] + product(grad_skip_ref[z], skip)
            value = value.reshape(GRID, 2, 2, 8, 2 * DEC)
            for j in range(2):
                for l in range(2):
                    at = ((i * 2 + j) * 2 + l) * DEC
                    part = value[:, j, l].reshape(GRID * GRID, 2 * DEC).astype(BF)
                    rows_block_ref[rows, at : at + DEC] = part[:, :DEC]
                    rows_tap_ref[rows, at : at + DEC] = part[:, DEC:]

    lax.fori_loop(0, GRID, row_step, None)


def turn_stack(source_ref, turned_ref, unit):
    def step(z, _):
        value = source_ref[z].astype(F32)
        before, after = side_steps(*halves(value))
        columns = pl.ds(pl.multiple_of(z * PLANE, PLANE), PLANE)
        for block, item in enumerate((before, value, after)):
            turned_ref[block * DEC : (block + 1) * DEC, columns] = product_back(
                unit, item.astype(BF)
            ).astype(BF)

    planes(step)


def put_shifted(source, shifted_ref):
    columns = shifted_ref.shape[2] // 3
    for z in (0, SIDE + 1):
        shifted_ref[z] = jnp.zeros(shifted_ref.shape[1:], BF)

    def step(z, _):
        value = source(z)
        none = jnp.zeros((SIDE, columns), BF)
        shifted_ref[z + 1, :, :columns] = jnp.concatenate([none, value[:-SIDE]])
        shifted_ref[z + 1, :, columns : 2 * columns] = value
        shifted_ref[z + 1, :, 2 * columns :] = jnp.concatenate([value[SIDE:], none])

    planes(step)


def weight_grad(turned_ref, shifted_ref, out_ref, first, ins):
    parts, _, rows, _ = out_ref.shape
    for along_d in range(3):
        shifted = shifted_ref[along_d : along_d + SIDE].reshape(VOX, 3 * ins)
        table = product(turned_ref[...], shifted).astype(BF)
        for along_h in range(3):
            for block in range(3):
                slot = (along_d * 3 + along_h) * 3 + 2 - block
                for part in range(parts):
                    out_ref[part, slot, :, first : first + ins] = table[
                        block * DEC + part * rows : block * DEC + (part + 1) * rows,
                        along_h * ins : (along_h + 1) * ins,
                    ]


def decoder_weights_kernel(
    grad_two_ref, hidden_ref, grad_one_ref, joined_ref, grad_skip_ref,
    out_ref,
    turned_ref, shifted_ref, narrow_ref,
):
    unit = unit_matrix(DEC)
    turn_stack(grad_two_ref, turned_ref, unit)
    put_shifted(lambda z: hidden_ref[z], narrow_ref)
    weight_grad(turned_ref, narrow_ref, out_ref, 2 * DEC, DEC)
    turn_stack(grad_one_ref, turned_ref, unit)
    put_shifted(lambda z: joined_ref[z], shifted_ref)
    weight_grad(turned_ref, shifted_ref, out_ref, 0, 2 * DEC)

    def step(z, _):
        columns = pl.ds(pl.multiple_of(z * PLANE, PLANE), PLANE)
        turned_ref[:DEC, columns] = product_back(unit, grad_skip_ref[z]).astype(BF)

    planes(step)
    table = product(turned_ref[:DEC], joined_ref[...].reshape(VOX, 2 * DEC)).astype(BF)
    parts, _, rows, columns = out_ref.shape
    for part in range(parts):
        out_ref[part, 27, :, : 2 * DEC] = table[part * rows : (part + 1) * rows]
        out_ref[part, 27, :, 2 * DEC :] = jnp.zeros((rows, columns - 2 * DEC), BF)


def skip_operands(kernel, count, left):
    def run(*refs):
        kernel(*refs[:count], *refs[count + left :])

    return run


def local_call(kernel, outs, scratch, *operands, after=()):
    specs = [
        pl.BlockSpec(memory_space=pltpu.SMEM if item.ndim == 1 else pltpu.VMEM)
        for item in operands
    ]
    specs += [pl.BlockSpec(memory_space=pl.ANY)] * len(after)
    vmem = pl.BlockSpec(memory_space=pltpu.VMEM)
    return pl.pallas_call(
        skip_operands(kernel, len(operands), len(after)),
        out_shape=[jax.ShapeDtypeStruct(shape, dtype) for shape, dtype in outs],
        in_specs=specs,
        out_specs=[vmem] * len(outs),
        scratch_shapes=[pltpu.VMEM(shape, dtype) for shape, dtype in scratch],
        compiler_params=pltpu.CompilerParams(vmem_limit_bytes=VMEM_BYTES),
        cost_estimate=pl.CostEstimate(flops=COST, bytes_accessed=COST, transcendentals=0),
    )(*operands, *after)


MAP = (SIDE, PLANE, DEC)


def decoder_forward(*operands, after=()):
    cube = (GRID, 2, GRID, 2, SIDE)
    return local_call(
        decoder_forward_kernel,
        [
            (cube + (2 * DEC,), BF), (MAP, BF), (MAP, F32), ((1, DEC), F32), (MAP, BF), (MAP, BF),
            ((DEC, VOX), BF),
        ],
        [
            (cube + (6 * DEC,), BF), ((SIDE, PLANE, 3 * DEC), BF), ((9 * DEC, 6 * DEC), BF),
            ((9 * DEC, 3 * DEC), BF), ((SIDE + 2, PLANE, DEC), F32), (MAP, F32), (MAP, F32),
        ],
        *operands, after=after,
    )


def decoder_backward(*operands, after=()):
    return local_call(
        decoder_backward_kernel,
        [(MAP, BF), ((PATCHES, 8 * DEC), BF), ((PATCHES, 8 * DEC), BF)],
        [
            ((SIDE, PLANE, 3 * DEC), BF), ((3 * DEC, 18 * DEC), BF), ((3 * DEC, 9 * DEC), BF),
            ((SIDE + 2, PLANE, DEC), F32), ((SIDE + 2, PLANE, 2 * DEC), F32),
        ],
        *operands, after=after,
    )


def decoder_weights(*operands, shape, after=()):
    return local_call(
        decoder_weights_kernel,
        [(shape, BF)],
        [
            ((3 * DEC, VOX), BF), ((SIDE + 2, PLANE, 6 * DEC), BF),
            ((SIDE + 2, PLANE, 3 * DEC), BF),
        ],
        *operands, after=after,
    )[0]


def attention(rows, weight, after=()):
    flat = (PATCHES, D)
    return local_call(
        attention_kernel,
        [
            (flat, BF), ((PATCHES, 3 * D), BF), ((HEADS, PATCHES, PATCHES), BF), (flat, BF),
            (flat, F32), (flat, BF), ((16, D), F32),
        ],
        [], rows, weight, after=after,
    )


def mlp(rows, first, fc1, fc2, fc1_shift, fc2_shift, after=()):
    return local_call(
        mlp_kernel,
        [((PATCHES, MLP), BF), ((PATCHES, MLP), BF), ((PATCHES, D), BF)],
        [], rows, first, fc1, fc2, fc1_shift, fc2_shift, after=after,
    )


def up_back(grad_block, grad_tap, block_out, tap_rows, up_full, after=()):
    flat = (PATCHES, D)
    return local_call(
        up_back_kernel,
        [((D, 16 * DEC), BF), (flat, BF), (flat, F32), (flat, BF), ((1, D), F32)],
        [], grad_block, grad_tap, block_out, tap_rows, up_full, after=after,
    )


def fc2_back(place, grad_mlp, active, slope, fc2, after=()):
    half = ((MLP, D // 2), BF)
    return local_call(
        fc2_back_kernel,
        [half, half, ((PATCHES, MLP), BF), ((1, MLP), F32)],
        [], place, grad_mlp, active, slope, fc2, after=after,
    )


def fc1_back(place, grad_hidden, input_two, first, grad_second, fc1, weight, vectors, after=()):
    half, flat = ((D, MLP // 2), BF), (PATCHES, D)
    return local_call(
        fc1_back_kernel,
        [half, half, (flat, F32), (flat, BF), (flat, BF), ((8, D), F32)],
        [],
        place, grad_hidden, input_two, first, grad_second, fc1, weight, vectors, after=after,
    )


def attention_back(place, *operands, after=()):
    wide = 4 * D + 2 * DEC
    half = ((D, wide // 2), BF)
    return local_call(
        attention_back_kernel,
        [half, half, ((PATCHES, D), BF)],
        [((PATCHES, 3 * D), BF), ((D, wide), BF), ((DEC, D), F32)],
        place, *operands, after=after,
    )


def make_body(axes):
    names, wa, col = axes.names, axes.wa, axes.col
    both = wa + col

    def body(
        tokens,
        tap,
        ln1_gain,
        ln1_bias,
        qkv_weight,
        query_bias,
        value_bias,
        out_weight,
        out_bias,
        ln2_gain,
        ln2_bias,
        fc1_weight,
        fc1_bias,
        fc2_weight,
        fc2_bias,
        block_up,
        tap_up,
        conv1_weight,
        conv2_weight,
        skip_weight,
        cotangent,
    ):
        rows_here = ln1_gain.shape[0]
        place = lax.axis_index(axes.core).astype(jnp.int32).reshape(1)

        vectors = [
            item.reshape(rows_here, -1)
            for item in (
                ln1_gain, ln1_bias, query_bias, value_bias, out_bias, ln2_gain, ln2_bias,
                fc2_bias, *jnp.split(fc1_bias, MLP // D),
            )
        ]
        vectors = jnp.concatenate(vectors, axis=1)
        extra = vectors.shape[1]
        vectors = jnp.pad(vectors, ((0, 0), (0, 2 * DEC - extra)))
        get_first = RowGather(
            jnp.concatenate([qkv_weight, out_weight, vectors], axis=1), axes.links_a, axes
        )
        get_fc1 = RowGather(fc1_weight, axes.links_b, axes)
        get_fc2 = RowGather(fc2_weight, axes.links_a, axes)
        up_full = lax.all_gather(
            jnp.concatenate([block_up, tap_up], axis=1), both, axis=0, tiled=True
        )
        conv_shard = jnp.concatenate([conv1_weight, conv2_weight], axis=2)
        skip_shard = jnp.pad(skip_weight, ((0, 0), (0, DEC)))
        conv_shard = jnp.concatenate([conv_shard, skip_shard[None]], axis=0)
        raw = lax.all_gather(conv_shard, col, axis=0, tiled=False)
        rows_bf = swap_blocks(tokens.reshape(axes.wa_count, -1, D), wa).reshape(PATCHES, D)
        get_first.link()
        get_fc1.value = wait_for(get_fc1.value, corner(get_first.value))
        get_fc1.link()
        get_first.link()
        get_fc2.value = wait_for(get_fc2.value, corner(get_fc1.value))
        get_fc2.link()
        for item in (get_first, get_fc1, get_fc2):
            while item.left:
                item.link()
        first_weight = get_first.finish(get_first.rows())
        tap = wait_for(tap, corner(get_fc2.value))
        tap_rows = swap_blocks(tap.reshape(axes.wa_count, -1, D), wa).reshape(PATCHES, D)
        cotangent = wait_for(cotangent, corner(get_fc2.value))
        upstream = swap_blocks(cotangent.reshape(axes.col_count, -1, VOX), col).reshape(DEC, VOX)

        input_one, qkv_rows, probs, attn_rows, first, input_two, vectors = attention(
            rows_bf, first_weight
        )
        fc1_full = get_fc1.finish(get_fc1.rows())
        fc2_full = get_fc2.finish(wait_for(get_fc2.rows(), corner(input_two)))
        fc1_shift = vectors[8:extra].reshape(extra - 8, -1, rows_here).transpose(1, 0, 2)
        fc1_shift = fc1_shift.reshape(1, MLP)
        active, slope, block_out = mlp(
            input_two, first, fc1_full, fc2_full, fc1_shift, vectors[7:8],
            after=(tap_rows,),
        )
        joined, hidden_maps, normed_c1, factor_c1, grad_c2, grad_skip, section = decoder_forward(
            block_out, tap_rows, up_full, raw, upstream
        )
        section_out = swap_blocks(section.reshape(axes.col_count, -1, VOX), col)

        grad_c1, grad_up_block, grad_up_tap = decoder_backward(
            grad_c2, grad_skip, normed_c1, factor_c1, raw
        )
        grad_up, grad_tap_rows, grad_second, grad_mlp, fc2_shift_sums = up_back(
            grad_up_block, grad_up_tap, block_out, tap_rows, up_full,
        )
        grad_ups = lax.psum_scatter(grad_up, both, scatter_dimension=0, tiled=True).astype(F32)
        keep, send, grad_hidden, fc1_shift_sums = fc2_back(
            place, grad_mlp, active, slope, fc2_full
        )
        sum_fc2 = RowSum(keep, send, axes.links_a, axes)
        keep, send, grad_first, grad_attn, grad_mixed, sums_two = fc1_back(
            place, grad_hidden, input_two, first, grad_second, fc1_full, first_weight, vectors
        )
        sum_fc1 = RowSum(keep, send, axes.links_b, axes)
        small = jnp.concatenate(
            [
                jnp.zeros((4, D), F32), sums_two[2:3], sums_two[:2], fc2_shift_sums,
                fc1_shift_sums.reshape(-1, extra - 8, rows_here).transpose(1, 0, 2).reshape(-1, D),
                jnp.zeros((16 - extra, D), F32),
            ]
        )
        keep, send, grad_rows = attention_back(
            place, grad_mixed, grad_attn, grad_first, qkv_rows, probs, attn_rows, input_one,
            rows_bf, first_weight, vectors, small, after=(sum_fc2.value,),
        )
        sum_fc2.link()
        sum_first = RowSum(keep, send, axes.links_a, axes)
        conv_grads = decoder_weights(
            grad_c2, hidden_maps, grad_c1, joined.reshape(SIDE, PLANE, 2 * DEC), grad_skip,
            shape=raw.shape, after=(sum_fc1.value, sum_fc2.value),
        )
        sum_fc1.link()
        sum_fc2.link()

        columns = conv_grads.shape[3]
        conv_grads = conv_grads.reshape([lax.axis_size(n) for n in col] + [-1, columns])
        conv_grads = scatter_dims(conv_grads, axes.inside(col)[::-1], names)
        conv_grads = conv_grads.reshape([lax.axis_size(n) for n in wa] + [-1, columns])
        wa_order = axes.inside(wa)
        conv_grads = scatter_dims(conv_grads, wa_order[::-1], names).astype(BF)
        conv_grads = gather_dims(conv_grads, wa_order, names).reshape(28, -1, columns)
        conv_grads = conv_grads.astype(F32)

        home_rows = swap_blocks(grad_rows.reshape(axes.wa_count, -1, D), wa).astype(F32)[None]
        home_tap = swap_blocks(grad_tap_rows.reshape(axes.wa_count, -1, D), wa).astype(F32)[None]
        sums = (sum_fc2, sum_fc1, sum_first)
        for item in sums:
            while item.left:
                item.link()
        grad_fc2, grad_fc1, first_grads = (item.finish() for item in sums)
        small_sums = first_grads[:, 4 * D : 4 * D + extra]
        return (
            section_out[:, None],
            home_rows,
            home_tap,
            small_sums[:, 0],
            small_sums[:, 1],
            first_grads[:, : 3 * D],
            small_sums[:, 2],
            small_sums[:, 3],
            first_grads[:, 3 * D : 4 * D],
            small_sums[:, 4],
            small_sums[:, 5],
            small_sums[:, 6],
            grad_fc1,
            small_sums[:, 8:extra].T.reshape(-1),
            grad_fc2,
            small_sums[:, 7],
            grad_ups[:, : 8 * DEC],
            grad_ups[:, 8 * DEC :],
            conv_grads[:27, :, : 2 * DEC],
            conv_grads[:27, :, 2 * DEC :],
            conv_grads[27, :, : 2 * DEC],
        )

    return body


def solution(mesh):
    axes = Axes(mesh)
    wa, col = axes.wa, axes.col
    both = wa + col
    tall, flat = P(both, None), P(both)
    rows = P(col, None, wa, None)
    maps = P(None, wa, col, None)
    kernel, wide = P(None, col, None), P(col, None)
    in_specs = (
        rows, rows, flat, flat, tall, flat, flat, tall, flat, flat, flat, tall, flat, tall, flat,
        tall, tall, kernel, kernel, wide, maps,
    )
    out_specs = (
        maps, rows, rows, flat, flat, tall, flat, flat, tall, flat, flat, flat, tall, flat, tall,
        flat, tall, tall, kernel, kernel, wide,
    )
    return jax.shard_map(
        make_body(axes), mesh=axes.mesh, in_specs=in_specs, out_specs=out_specs, check_vma=False
    )
```

```python
import jax
import jax.numpy as jnp
from jax import lax
from jax.experimental import pallas as pl
from jax.experimental.pallas import tpu as pltpu
from jax.sharding import Mesh, PartitionSpec as P

D = 768
HEADS = 12
HEAD_DIM = 64
MLP = 3072
DEC = 128
GRID = 8
PATCHES = 512
SIDE = 16
VOX = 4096
PLANE = SIDE * SIDE
BF = jnp.bfloat16
F32 = jnp.float32
VMEM_BYTES = 56 * 2**20
COST = 3 * 10**10


def cut_axis(devices, label):
    places = [getattr(item, "coords", None) for item in devices]
    if len(devices) == 1 or any(place is None for place in places):
        return [(label, len(devices), False)]
    full = [tuple(item.coords) + (item.core_on_chip,) for item in devices]
    found = []
    for axis in range(4):
        values = [place[axis] for place in full]
        if len(set(values)) > 1:
            stride = next(k for k in range(len(values)) if values[k] != values[0])
            found.append((stride, len(set(values)), axis))
    found.sort(reverse=True)
    step = 1
    for stride, size, _ in reversed(found):
        if stride != step:
            return [(label, len(devices), False)]
        step *= size
    if step != len(devices):
        return [(label, len(devices), False)]
    return [(label + "xyzc"[axis], size, axis == 3) for _, size, axis in found]


class Axes:
    def __init__(self, mesh):
        grid = mesh.devices
        wa = cut_axis(list(grid[:, 0]), "wa")
        col = cut_axis(list(grid[0, :]), "col")
        parts = wa + col
        self.sizes = {name: size for name, size, _ in parts}
        self.names = tuple(self.sizes)
        self.wa = tuple(name for name, _, _ in wa)
        self.col = tuple(name for name, _, _ in col)
        self.wa_count, self.col_count = grid.shape
        self.mesh = Mesh(grid.reshape(tuple(self.sizes.values())), self.names)
        core = [name for name, _, is_core in parts if is_core]
        links = [name for name, _, is_core in parts if not is_core]
        links.sort(key=lambda name: -self.sizes[name])
        self.core = core[0] if core else None
        self.links_a = tuple(links)
        if len(links) > 2:
            links = links[:-2] + [links[-1], links[-2]]
        self.links_b = tuple(links)

    def inside(self, names):
        return [n for n in self.links_a if n in names] + [n for n in (self.core,) if n in names]


def swap(value, axis):
    return lax.ppermute(value, axis, [(0, 1), (1, 0)])


def turn(value, axis, size, step):
    return lax.ppermute(value, axis, [(k, (k + step) % size) for k in range(size)])


def gather_axis(value, axis, size):
    place = lax.axis_index(axis)
    if size == 2:
        mine, other = value[None], swap(value, axis)[None]
        return jnp.where(
            place == 0,
            jnp.concatenate([mine, other]),
            jnp.concatenate([other, mine]),
        )
    got = [turn(value, axis, size, step) for step in range(1, size)]
    out = jnp.zeros((size,) + value.shape, value.dtype)
    out = lax.dynamic_update_index_in_dim(out, value, place, 0)
    for step in range(1, size):
        out = lax.dynamic_update_index_in_dim(out, got[step - 1], (place - step) % size, 0)
    return out


def keep_order(first, second, place, axis):
    return jnp.where(
        place == 0,
        jnp.concatenate([first, second], axis),
        jnp.concatenate([second, first], axis),
    )


def column_half(value, place):
    half = value.shape[-1] // 2
    return lax.dynamic_slice_in_dim(value, place * half, half, value.ndim - 1)


def gather_dims(value, order, names):
    dims, inner = [], value.ndim
    for name in order:
        value = gather_axis(value, name, lax.axis_size(name))
        dims.insert(0, name)
    kept = [name for name in names if name in dims]
    return value.transpose([dims.index(n) for n in kept] + [len(dims) + k for k in range(inner)])


class RowGather:
    def __init__(self, value, links, axes):
        self.axes, self.left, self.dims = axes, list(links), []
        place = lax.axis_index(axes.core)
        mine, other = column_half(value, place), column_half(value, 1 - place)
        self.value = keep_order(mine[None], swap(other, axes.core)[None], place, 0)

    def link(self):
        name = self.left.pop(0)
        self.value = gather_axis(self.value, name, lax.axis_size(name))
        self.dims.insert(0, name)

    def rows(self):
        axes, value = self.axes, self.value
        kept = [name for name in axes.names if name in self.dims]
        count = len(kept)
        value = value.transpose([self.dims.index(n) for n in kept] + [count, count + 1, count + 2])
        value = jnp.moveaxis(value, count, axes.names.index(axes.core))
        return value.reshape(-1, value.shape[-1])

    def finish(self, half):
        place = lax.axis_index(self.axes.core)
        return keep_order(half, swap(half, self.axes.core), place, 1)


def wait_for(value, *others):
    return lax.optimization_barrier((value, *others))[0]


def corner(value):
    return value.reshape(-1, value.shape[-1])[:16, :128]


def scatter_axis(value, axis, dim):
    size, place = lax.axis_size(axis), lax.axis_index(axis)
    got = [
        turn(lax.dynamic_index_in_dim(value, (place + step) % size, dim, False), axis, size, step)
        for step in range(1, size)
    ]
    total = lax.dynamic_index_in_dim(value, place, dim, False).astype(F32)
    for item in got:
        total = total + item.astype(F32)
    return total


def scatter_dims(value, order, names):
    dims = [name for name in names if name in order]
    for name in order:
        dim = dims.index(name)
        dims.pop(dim)
        value = scatter_axis(value.astype(BF), name, dim)
    return value


class RowSum:
    def __init__(self, keep, send, links, axes):
        self.axes, self.left = axes, list(reversed(links))
        self.dims = list(axes.names)
        got = swap(send, axes.core)
        self.value = (keep.astype(F32) + got.astype(F32)).astype(BF)
        columns = keep.shape[1]
        self.value = self.value.reshape([lax.axis_size(n) for n in self.dims] + [-1, columns])

    def link(self):
        name = self.left.pop(0)
        dim = self.dims.index(name)
        self.dims.pop(dim)
        self.value = scatter_axis(self.value, name, dim)
        if self.left:
            self.value = self.value.astype(BF)

    def finish(self):
        axes = self.axes
        place = lax.axis_index(axes.core)
        mine = lax.dynamic_index_in_dim(self.value, place, 0, False)
        other = lax.dynamic_index_in_dim(self.value, 1 - place, 0, False).astype(BF)
        return keep_order(mine, swap(other, axes.core).astype(F32), place, 1)


def swap_blocks(value, axes):
    return lax.all_to_all(value, axes, 0, 0, tiled=True)


def product(left, right):
    return jnp.dot(left, right, preferred_element_type=F32)


def product_rows(left, right):
    return lax.dot_general(left, right, (((0,), (0,)), ((), ())), preferred_element_type=F32)


def product_back(left, right):
    return lax.dot_general(left, right, (((1,), (1,)), ((), ())), preferred_element_type=F32)


def row_norm(values, epsilon):
    center = values - jnp.mean(values, axis=-1, keepdims=True)
    factor = lax.rsqrt(jnp.mean(center * center, axis=-1, keepdims=True) + epsilon)
    return (center * factor, factor)


def row_norm_back(upstream, normed, factor):
    middle = upstream - jnp.mean(upstream, axis=-1, keepdims=True)
    return factor * (middle - normed * jnp.mean(upstream * normed, axis=-1, keepdims=True))


def unit_matrix(size):
    here = lax.broadcasted_iota(jnp.int32, (size, size), 0)
    there = lax.broadcasted_iota(jnp.int32, (size, size), 1)
    return (here == there).astype(F32).astype(BF)


def turned(value, unit):
    return product_back(unit, value).astype(BF)


def head_masks():
    lane = lax.broadcasted_iota(jnp.int32, (PATCHES, 2 * HEAD_DIM), 1)
    return [(lane < HEAD_DIM).astype(F32).astype(BF), (lane >= HEAD_DIM).astype(F32).astype(BF)]


def low_lanes(shape):
    return lax.broadcasted_iota(jnp.int32, shape, 1) < HEAD_DIM


def attention_kernel(
    rows_ref, weight_ref,
    input_one_ref, qkv_ref, probs_ref, attn_ref, first_ref, input_two_ref, vectors_ref,
):
    rows = rows_ref[...].astype(F32)
    unit = unit_matrix(2 * HEAD_DIM)
    vectors_ref[...] = product_back(unit, weight_ref[:, 4 * D : 4 * D + DEC])[:16]
    gain_one, bias_one, query_bias, value_bias, out_shift, gain_two, bias_two = (
        vectors_ref[k : k + 1] for k in range(7)
    )
    normed, _ = row_norm(rows, 1e-06)
    input_one_ref[...] = (normed * gain_one + bias_one).astype(BF)
    for block, bias in enumerate((query_bias, None, value_bias)):
        columns = slice(block * D, (block + 1) * D)
        value = product(input_one_ref[...], weight_ref[:, columns])
        qkv_ref[:, columns] = (value if bias is None else value + bias).astype(BF)
    masks, wide_unit = head_masks(), unit_matrix(PATCHES)

    def pair_step(pair, _):
        at = pl.multiple_of(pair * 2 * HEAD_DIM, 2 * HEAD_DIM)
        columns = pl.ds(at, 2 * HEAD_DIM)
        queries = qkv_ref[:, columns]
        keys = qkv_ref[:, pl.ds(at + D, 2 * HEAD_DIM)]
        values = turned(qkv_ref[:, pl.ds(at + 2 * D, 2 * HEAD_DIM)], unit)
        mixed = []
        for head in range(2):
            scores = product_back(keys * masks[head], queries) * 0.125
            expo = jnp.exp(scores - jnp.max(scores, axis=0, keepdims=True))
            probs = (expo * (1.0 / jnp.sum(expo, axis=0, keepdims=True))).astype(BF)
            probs_ref[2 * pair + head] = probs
            part = product(values[head * HEAD_DIM : (head + 1) * HEAD_DIM], probs)
            mixed.append(part.astype(BF))
        attn_ref[:, columns] = product_back(wide_unit, jnp.concatenate(mixed)).astype(BF)

    lax.fori_loop(0, HEADS // 2, pair_step, None, unroll=PAIRS)
    first = rows + product(attn_ref[...], weight_ref[:, 3 * D : 4 * D]) + out_shift
    first_ref[...] = first
    normed, _ = row_norm(first, 1e-06)
    input_two_ref[...] = (normed * gain_two + bias_two).astype(BF)


CHUNK = 512


def mlp_kernel(
    input_ref, first_ref, fc1_ref, fc2_ref, fc1_shift_ref, fc2_shift_ref,
    active_ref, slope_ref, out_ref,
):
    total = first_ref[...] + fc2_shift_ref[...]
    for at in range(0, MLP, CHUNK):
        columns = slice(at, at + CHUNK)
        hidden = product(input_ref[...], fc1_ref[:, columns]) + fc1_shift_ref[:, columns]
        below = 0.5 * (1.0 + lax.erf(hidden * 0.7071067811865476))
        slope = below + hidden * (0.3989422804014327 * jnp.exp(-0.5 * hidden * hidden))
        slope_ref[:, columns] = slope.astype(BF)
        active_ref[:, columns] = (hidden * below).astype(BF)
        total = total + product(active_ref[:, columns], fc2_ref[columns])
    out_ref[...] = total.astype(BF)


def cut_columns(ref, place):
    half = ref.shape[1] // 2
    keep = pl.ds(pl.multiple_of(place * half, DEC), half)
    send = pl.ds(pl.multiple_of((1 - place) * half, DEC), half)
    return (keep, send)


def up_back_kernel(
    grad_block_ref, grad_tap_ref, block_ref, tap_ref, up_ref,
    grad_up_ref, grad_rows_ref, grad_second_ref, grad_mlp_ref, sums_ref,
):
    unit = unit_matrix(PLANE)
    for source, (grad_ref, rows_ref) in enumerate(
        ((grad_block_ref, block_ref), (grad_tap_ref, tap_ref))
    ):
        columns = slice(source * 8 * DEC, (source + 1) * 8 * DEC)
        for at in range(0, D, PLANE):
            rows = slice(at, at + PLANE)
            left = turned(rows_ref[:, rows], unit)
            grad_up_ref[rows, columns] = product(left, grad_ref[...]).astype(BF)
        back = product_back(grad_ref[...], up_ref[:, columns])
        if source == 0:
            grad_second_ref[...] = back
            grad_mlp_ref[...] = back.astype(BF)
            sums_ref[...] = column_sum(back.astype(BF).astype(F32))
        else:
            grad_rows_ref[...] = back.astype(BF)


def fc2_back_kernel(
    place_ref, grad_mlp_ref, active_ref, slope_ref, fc2_ref,
    keep_ref, send_ref, grad_hidden_ref, sums_ref,
):
    unit = unit_matrix(PLANE)
    keep, send = cut_columns(grad_mlp_ref, place_ref[0])
    for at in range(0, MLP, PLANE):
        rows = slice(at, at + PLANE)
        left = turned(active_ref[:, rows], unit)
        send_ref[rows] = product(left, grad_mlp_ref[:, send]).astype(BF)
        keep_ref[rows] = product(left, grad_mlp_ref[:, keep]).astype(BF)
    for at in range(0, MLP, CHUNK):
        rows = slice(at, at + CHUNK)
        grad = product_back(grad_mlp_ref[...], fc2_ref[rows]) * slope_ref[:, rows].astype(F32)
        grad = grad.astype(BF)
        grad_hidden_ref[:, rows] = grad
        sums_ref[:, rows] = column_sum(grad.astype(F32))


def fc1_back_kernel(
    place_ref, grad_hidden_ref, input_ref, first_ref, grad_second_ref, fc1_ref, weight_ref,
    vectors_ref,
    keep_ref, send_ref, grad_first_ref, grad_attn_ref, grad_mixed_ref, sums_ref,
):
    unit = unit_matrix(PLANE)
    keep, send = cut_columns(grad_hidden_ref, place_ref[0])
    for at in range(0, D, PLANE):
        rows = slice(at, at + PLANE)
        left = turned(input_ref[:, rows], unit)
        send_ref[rows] = product(left, grad_hidden_ref[:, send]).astype(BF)
        keep_ref[rows] = product(left, grad_hidden_ref[:, keep]).astype(BF)
    grad = product_back(grad_hidden_ref[...], fc1_ref[...])
    normed, factor = row_norm(first_ref[...], 1e-06)
    sums_ref[0:1] = column_sum(grad * normed)
    sums_ref[1:2] = column_sum(grad)
    grad = grad_second_ref[...] + row_norm_back(grad * vectors_ref[5:6], normed, factor)
    grad_first_ref[...] = grad
    grad = grad.astype(BF)
    grad_attn_ref[...] = grad
    sums_ref[2:3] = column_sum(grad.astype(F32))
    grad_mixed_ref[...] = product_back(grad, weight_ref[:, 3 * D : 4 * D]).astype(BF)


def attention_back_kernel(
    place_ref, grad_mixed_ref, grad_attn_ref, grad_first_ref, qkv_ref, probs_ref, attn_ref,
    input_ref, rows_ref, weight_ref, vectors_ref, small_ref,
    keep_ref, send_ref, grad_rows_ref,
    grad_qkv_ref, grad_ref, sums_ref,
):
    masks, unit, wide_unit = head_masks(), unit_matrix(2 * HEAD_DIM), unit_matrix(PATCHES)

    def pair_step(pair, _):
        at = pl.multiple_of(pair * 2 * HEAD_DIM, 2 * HEAD_DIM)
        columns = pl.ds(at, 2 * HEAD_DIM)
        queries = qkv_ref[:, columns]
        keys_turned = turned(qkv_ref[:, pl.ds(at + D, 2 * HEAD_DIM)], unit)
        values = qkv_ref[:, pl.ds(at + 2 * D, 2 * HEAD_DIM)]
        grads = grad_mixed_ref[:, columns]
        grad_q, grad_k, grad_v = [], [], []
        for head in range(2):
            probs = probs_ref[2 * pair + head]
            grad_probs = product_back(values * masks[head], grads)
            wide = probs.astype(F32)
            inner = jnp.sum(grad_probs * wide, axis=0, keepdims=True)
            grad_scores = (wide * (grad_probs - inner)).astype(BF)
            grad_v.append(product(probs, grads))
            grad_k.append(product(grad_scores, queries) * 0.125)
            part = product(keys_turned[head * HEAD_DIM : (head + 1) * HEAD_DIM], grad_scores)
            grad_q.append((part * 0.125).astype(BF))
        first = low_lanes((PATCHES, 2 * HEAD_DIM))
        grad_qkv_ref[:, columns] = product_back(wide_unit, jnp.concatenate(grad_q)).astype(BF)
        grad_qkv_ref[:, pl.ds(at + D, 2 * HEAD_DIM)] = jnp.where(first, *grad_k).astype(BF)
        grad_qkv_ref[:, pl.ds(at + 2 * D, 2 * HEAD_DIM)] = jnp.where(first, *grad_v).astype(BF)

    lax.fori_loop(0, HEADS // 2, pair_step, None, unroll=PAIRS)
    square = unit_matrix(PLANE)
    for at in range(0, D, PLANE):
        rows = slice(at, at + PLANE)
        left = turned(input_ref[:, rows], square)
        grad_ref[rows, : 3 * D] = product(left, grad_qkv_ref[...]).astype(BF)
        left = turned(attn_ref[:, rows], square)
        grad_ref[rows, 3 * D : 4 * D] = product(left, grad_attn_ref[...]).astype(BF)
    grad = product_back(grad_qkv_ref[...], weight_ref[:, : 3 * D])
    normed, factor = row_norm(rows_ref[...].astype(F32), 1e-06)
    sums_ref[...] = jnp.zeros(sums_ref.shape, F32)
    sums_ref[:16] = small_ref[...]
    sums_ref[0:1] = column_sum(grad * normed)
    sums_ref[1:2] = column_sum(grad)
    sums_ref[2:3] = column_sum(grad_qkv_ref[:, :D].astype(F32))
    sums_ref[3:4] = column_sum(grad_qkv_ref[:, 2 * D :].astype(F32))
    for at in range(0, D, DEC):
        rows = slice(at, at + DEC)
        grad_ref[rows, 4 * D : 4 * D + DEC] = turned(sums_ref[:, rows].astype(BF), unit)
        grad_ref[rows, 4 * D + DEC :] = jnp.zeros((DEC, DEC), BF)
    keep, send = cut_columns(grad_ref, place_ref[0])
    send_ref[...] = grad_ref[:, send]
    keep_ref[...] = grad_ref[:, keep]
    grad = grad_first_ref[...] + row_norm_back(grad * vectors_ref[0:1], normed, factor)
    grad_rows_ref[...] = grad.astype(BF)


def halves(value):
    rows, columns = value.shape
    cut = value.reshape(rows // 16, 2, 8, columns)
    return (cut[:, 0], cut[:, 1])


def join_halves(low, high):
    count, _, columns = low.shape
    return jnp.concatenate(
        [low.reshape(count, 1, 8, columns), high.reshape(count, 1, 8, columns)], axis=1
    ).reshape(count * 16, columns)


def side_steps(low, high):
    place = lax.broadcasted_iota(jnp.int32, low.shape, 1)
    back = jnp.where(place == 0, 0.0, pltpu.roll(high, 1, 1))
    ahead = jnp.where(place == 7, 0.0, pltpu.roll(low, 7, 1))
    return (join_halves(back, low), join_halves(high, ahead))


def put_stack(ref, z, value):
    columns = value.shape[1]
    before, after = side_steps(*halves(value))
    ref[z, :, :columns] = before.astype(BF)
    ref[z, :, columns : 2 * columns] = value.astype(BF)
    ref[z, :, 2 * columns :] = after.astype(BF)


def silu_gate(values):
    return 1.0 / (1.0 + jnp.exp(-values))


UNROLL = 4
PAIRS = 3


def planes(step, carry=None):
    return lax.fori_loop(0, SIDE, step, carry, unroll=UNROLL)


def forward_table(raw_ref, table_ref, first, ins):
    parts, _, rows, _ = raw_ref.shape
    for k in range(9):
        for along in range(3):
            for part in range(parts):
                table_ref[
                    k * DEC + part * rows : k * DEC + (part + 1) * rows,
                    along * ins : (along + 1) * ins,
                ] = raw_ref[part, 3 * k + along, :, first : first + ins]


def backward_table(raw_ref, table_ref, first, ins):
    parts, _, rows, _ = raw_ref.shape
    for k in range(9):
        for along in range(3):
            for part in range(parts):
                table_ref[
                    along * DEC + part * rows : along * DEC + (part + 1) * rows,
                    k * ins : (k + 1) * ins,
                ] = raw_ref[part, 3 * k + 2 - along, :, first : first + ins]


def skip_table(raw_ref):
    return jnp.concatenate([raw_ref[part, 27, :, : 2 * DEC] for part in range(raw_ref.shape[0])])


GROUP = 4


def conv_planes(source, table_ref, total_ref, columns, forward):
    for z in range(SIDE + 2):
        total_ref[z] = jnp.zeros((PLANE, columns), F32)

    def step(group, _):
        start = group * GROUP
        value = jnp.concatenate([source(start + k) for k in range(GROUP)])
        if forward:
            wide = product_back(value, table_ref[...])
        else:
            wide = product(value, table_ref[...])
        none = jnp.zeros((SIDE, columns), F32)
        for plane in range(GROUP):
            for along_d in (-1, 0, 1):
                parts = [
                    wide[plane * PLANE : (plane + 1) * PLANE, k * columns : (k + 1) * columns]
                    for k in range(3 * along_d + 3, 3 * along_d + 6)
                ]
                to = along_d if not forward else -along_d
                early, late = (parts[0], parts[2]) if not forward else (parts[2], parts[0])
                moved = (
                    parts[1]
                    + jnp.concatenate([early[SIDE:], none])
                    + jnp.concatenate([none, late[:-SIDE]])
                )
                at = start + plane + 1 + to
                total_ref[at] = total_ref[at] + moved

    lax.fori_loop(0, SIDE // GROUP, step, None)


def column_sum(value):
    return jnp.sum(value, axis=0, keepdims=True)


def row_sums(value):
    return jnp.sum(value.reshape(-1, 8, value.shape[1]), axis=0)


def map_stats(total_ref, first):
    zero = jnp.zeros((8, total_ref.shape[2]), F32)
    mean = planes(lambda z, run: run + row_sums(total_ref[z + first]), zero)
    mean = column_sum(mean) / VOX

    def spread(z, run):
        center = total_ref[z + first] - mean
        return run + row_sums(center * center)

    return (mean, lax.rsqrt(column_sum(planes(spread, zero)) / VOX + 1e-05))


def sort_matrix():
    here = lax.broadcasted_iota(jnp.int32, (PLANE, PLANE), 0)
    there = lax.broadcasted_iota(jnp.int32, (PLANE, PLANE), 1)
    own = (here & -16) + 2 * (here & 7) + ((here >> 3) & 1)
    return (own == there).astype(F32).astype(BF)


def plane_of(ref, z):
    return ref[lax.shift_right_logical(z, 1), z & 1].reshape(PLANE, ref.shape[-1])


def decoder_forward_kernel(
    block_ref, tap_ref, up_ref, raw_ref, cot_ref,
    joined_ref, hidden_ref, normed_ref, factor_ref, grad_two_ref, grad_skip_ref, section_ref,
    wide_ref, stack_ref, table_one, table_two, total_ref, skip_ref, grad_ref,
):
    forward_table(raw_ref, table_one, 0, 2 * DEC)
    forward_table(raw_ref, table_two, 2 * DEC, DEC)
    for source, rows_ref in enumerate((block_ref, tap_ref)):
        for i in range(2):
            for j in range(2):
                start = source * 8 * DEC + (i * 2 + j) * 2 * DEC
                part = product(rows_ref[...], up_ref[:, start : start + 2 * DEC])
                part = part.astype(BF).astype(F32)
                low = part[:, :DEC].reshape(GRID * GRID, 8, DEC)
                high = part[:, DEC:].reshape(GRID * GRID, 8, DEC)
                before, after = side_steps(low, high)
                for block, value in enumerate((before, join_halves(low, high), after)):
                    at = block * 2 * DEC + source * DEC
                    value = value.astype(BF).reshape(GRID, GRID, SIDE, DEC)
                    wide_ref[:, i, :, j, :, at : at + DEC] = value
                    if block == 1:
                        joined_ref[:, i, :, j, :, source * DEC : (source + 1) * DEC] = value

    conv_planes(lambda z: plane_of(wide_ref, z), table_one, total_ref, DEC, True)
    mean, factor = map_stats(total_ref, 1)
    factor_ref[...] = factor

    def act(z, _):
        normed = (total_ref[z + 1] - mean) * factor
        normed_ref[z] = normed
        value = (normed * silu_gate(normed)).astype(BF)
        hidden_ref[z] = value
        put_stack(stack_ref, z, value.astype(F32))

    planes(act)
    conv_planes(lambda z: stack_ref[z], table_two, total_ref, DEC, True)
    skip = skip_table(raw_ref)

    def skip_step(z, _):
        skip_ref[z] = product_back(plane_of(joined_ref, z), skip)

    planes(skip_step)
    mean_two, factor_two = map_stats(total_ref, 1)
    mean_skip, factor_skip = map_stats(skip_ref, 0)
    sort, unit = sort_matrix(), unit_matrix(DEC)
    zero = jnp.zeros((8, DEC), F32)

    def out_step(z, sums):
        two = (total_ref[z + 1] - mean_two) * factor_two
        side = (skip_ref[z] - mean_skip) * factor_skip
        both = two + side
        gate = silu_gate(both)
        columns = pl.ds(pl.multiple_of(z * PLANE, PLANE), PLANE)
        turned = product_back(unit, (both * gate).astype(BF)).astype(BF)
        section_ref[:, columns] = product(turned, sort).astype(BF)
        grad = product_back(sort, cot_ref[:, columns]) * (gate * (1.0 + both * (1.0 - gate)))
        total_ref[z + 1] = two
        skip_ref[z] = side
        grad_ref[z] = grad
        return (
            sums[0] + row_sums(grad),
            sums[1] + row_sums(grad * two),
            sums[2] + row_sums(grad * side),
        )

    plain, by_two, by_skip = (column_sum(item) for item in planes(out_step, (zero, zero, zero)))

    def back_step(z, _):
        middle = grad_ref[z] - plain / VOX
        grad_two_ref[z] = (factor_two * (middle - total_ref[z + 1] * (by_two / VOX))).astype(BF)
        grad_skip_ref[z] = (factor_skip * (middle - skip_ref[z] * (by_skip / VOX))).astype(BF)

    planes(back_step)


def decoder_backward_kernel(
    grad_two_ref, grad_skip_ref, normed_ref, factor_ref, raw_ref,
    grad_one_ref, rows_block_ref, rows_tap_ref,
    stack_ref, table_one, table_two, total_ref, wide_ref,
):
    backward_table(raw_ref, table_one, 0, 2 * DEC)
    backward_table(raw_ref, table_two, 2 * DEC, DEC)

    def stack_step(z, _):
        put_stack(stack_ref, z, grad_two_ref[z].astype(F32))

    planes(stack_step)
    conv_planes(lambda z: stack_ref[z], table_two, total_ref, DEC, False)
    zero = jnp.zeros((8, DEC), F32)

    def act(z, sums):
        normed = normed_ref[z]
        gate = silu_gate(normed)
        grad = total_ref[z + 1] * (gate * (1.0 + normed * (1.0 - gate)))
        total_ref[z + 1] = grad
        return (sums[0] + row_sums(grad), sums[1] + row_sums(grad * normed))

    plain, by_normed = (column_sum(item) for item in planes(act, (zero, zero)))

    def back_step(z, _):
        middle = total_ref[z + 1] - plain / VOX
        value = (factor_ref[...] * (middle - normed_ref[z] * (by_normed / VOX))).astype(BF)
        grad_one_ref[z] = value
        put_stack(stack_ref, z, value.astype(F32))

    planes(back_step)
    conv_planes(lambda z: stack_ref[z], table_one, wide_ref, 2 * DEC, False)
    skip = skip_table(raw_ref)

    def row_step(a, _):
        rows = pl.ds(pl.multiple_of(a * GRID * GRID, GRID * GRID), GRID * GRID)
        for i in range(2):
            z = 2 * a + i
            value = wide_ref[z + 1] + product(grad_skip_ref[z], skip)
            value = value.reshape(GRID, 2, 2, 8, 2 * DEC)
            for j in range(2):
                for l in range(2):
                    at = ((i * 2 + j) * 2 + l) * DEC
                    part = value[:, j, l].reshape(GRID * GRID, 2 * DEC).astype(BF)
                    rows_block_ref[rows, at : at + DEC] = part[:, :DEC]
                    rows_tap_ref[rows, at : at + DEC] = part[:, DEC:]

    lax.fori_loop(0, GRID, row_step, None)


def turn_stack(source_ref, turned_ref, unit):
    def step(z, _):
        value = source_ref[z].astype(F32)
        before, after = side_steps(*halves(value))
        columns = pl.ds(pl.multiple_of(z * PLANE, PLANE), PLANE)
        for block, item in enumerate((before, value, after)):
            turned_ref[block * DEC : (block + 1) * DEC, columns] = product_back(
                unit, item.astype(BF)
            ).astype(BF)

    planes(step)


def put_shifted(source, shifted_ref):
    columns = shifted_ref.shape[2] // 3
    for z in (0, SIDE + 1):
        shifted_ref[z] = jnp.zeros(shifted_ref.shape[1:], BF)

    def step(z, _):
        value = source(z)
        none = jnp.zeros((SIDE, columns), BF)
        shifted_ref[z + 1, :, :columns] = jnp.concatenate([none, value[:-SIDE]])
        shifted_ref[z + 1, :, columns : 2 * columns] = value
        shifted_ref[z + 1, :, 2 * columns :] = jnp.concatenate([value[SIDE:], none])

    planes(step)


def weight_grad(turned_ref, shifted_ref, out_ref, first, ins):
    parts, _, rows, _ = out_ref.shape
    for along_d in range(3):
        shifted = shifted_ref[along_d : along_d + SIDE].reshape(VOX, 3 * ins)
        table = product(turned_ref[...], shifted).astype(BF)
        for along_h in range(3):
            for block in range(3):
                slot = (along_d * 3 + along_h) * 3 + 2 - block
                for part in range(parts):
                    out_ref[part, slot, :, first : first + ins] = table[
                        block * DEC + part * rows : block * DEC + (part + 1) * rows,
                        along_h * ins : (along_h + 1) * ins,
                    ]


def decoder_weights_kernel(
    grad_two_ref, hidden_ref, grad_one_ref, joined_ref, grad_skip_ref,
    out_ref,
    turned_ref, shifted_ref, narrow_ref,
):
    unit = unit_matrix(DEC)
    turn_stack(grad_two_ref, turned_ref, unit)
    put_shifted(lambda z: hidden_ref[z], narrow_ref)
    weight_grad(turned_ref, narrow_ref, out_ref, 2 * DEC, DEC)
    turn_stack(grad_one_ref, turned_ref, unit)
    put_shifted(lambda z: joined_ref[z], shifted_ref)
    weight_grad(turned_ref, shifted_ref, out_ref, 0, 2 * DEC)

    def step(z, _):
        columns = pl.ds(pl.multiple_of(z * PLANE, PLANE), PLANE)
        turned_ref[:DEC, columns] = product_back(unit, grad_skip_ref[z]).astype(BF)

    planes(step)
    table = product(turned_ref[:DEC], joined_ref[...].reshape(VOX, 2 * DEC)).astype(BF)
    parts, _, rows, columns = out_ref.shape
    for part in range(parts):
        out_ref[part, 27, :, : 2 * DEC] = table[part * rows : (part + 1) * rows]
        out_ref[part, 27, :, 2 * DEC :] = jnp.zeros((rows, columns - 2 * DEC), BF)


def skip_operands(kernel, count, left):
    def run(*refs):
        kernel(*refs[:count], *refs[count + left :])

    return run


def local_call(kernel, outs, scratch, *operands, after=()):
    specs = [
        pl.BlockSpec(memory_space=pltpu.SMEM if item.ndim == 1 else pltpu.VMEM)
        for item in operands
    ]
    specs += [pl.BlockSpec(memory_space=pl.ANY)] * len(after)
    vmem = pl.BlockSpec(memory_space=pltpu.VMEM)
    return pl.pallas_call(
        skip_operands(kernel, len(operands), len(after)),
        out_shape=[jax.ShapeDtypeStruct(shape, dtype) for shape, dtype in outs],
        in_specs=specs,
        out_specs=[vmem] * len(outs),
        scratch_shapes=[pltpu.VMEM(shape, dtype) for shape, dtype in scratch],
        compiler_params=pltpu.CompilerParams(vmem_limit_bytes=VMEM_BYTES),
        cost_estimate=pl.CostEstimate(flops=COST, bytes_accessed=COST, transcendentals=0),
    )(*operands, *after)


MAP = (SIDE, PLANE, DEC)


def decoder_forward(*operands, after=()):
    cube = (GRID, 2, GRID, 2, SIDE)
    return local_call(
        decoder_forward_kernel,
        [
            (cube + (2 * DEC,), BF), (MAP, BF), (MAP, F32), ((1, DEC), F32), (MAP, BF), (MAP, BF),
            ((DEC, VOX), BF),
        ],
        [
            (cube + (6 * DEC,), BF), ((SIDE, PLANE, 3 * DEC), BF), ((9 * DEC, 6 * DEC), BF),
            ((9 * DEC, 3 * DEC), BF), ((SIDE + 2, PLANE, DEC), F32), (MAP, F32), (MAP, F32),
        ],
        *operands, after=after,
    )


def decoder_backward(*operands, after=()):
    return local_call(
        decoder_backward_kernel,
        [(MAP, BF), ((PATCHES, 8 * DEC), BF), ((PATCHES, 8 * DEC), BF)],
        [
            ((SIDE, PLANE, 3 * DEC), BF), ((3 * DEC, 18 * DEC), BF), ((3 * DEC, 9 * DEC), BF),
            ((SIDE + 2, PLANE, DEC), F32), ((SIDE + 2, PLANE, 2 * DEC), F32),
        ],
        *operands, after=after,
    )


def decoder_weights(*operands, shape, after=()):
    return local_call(
        decoder_weights_kernel,
        [(shape, BF)],
        [
            ((3 * DEC, VOX), BF), ((SIDE + 2, PLANE, 6 * DEC), BF),
            ((SIDE + 2, PLANE, 3 * DEC), BF),
        ],
        *operands, after=after,
    )[0]


def gate(value, *after):
    anywhere = pl.BlockSpec(memory_space=pl.ANY)
    return pl.pallas_call(
        lambda *refs: None,
        out_shape=jax.ShapeDtypeStruct(value.shape, value.dtype),
        in_specs=[anywhere] * (1 + len(after)),
        out_specs=anywhere,
        input_output_aliases={0: 0},
        cost_estimate=pl.CostEstimate(flops=0, bytes_accessed=0, transcendentals=0),
    )(value, *after)


def attention(rows, weight, after=()):
    flat = (PATCHES, D)
    return local_call(
        attention_kernel,
        [
            (flat, BF), ((PATCHES, 3 * D), BF), ((HEADS, PATCHES, PATCHES), BF), (flat, BF),
            (flat, F32), (flat, BF), ((16, D), F32),
        ],
        [], rows, weight, after=after,
    )


def mlp(rows, first, fc1, fc2, fc1_shift, fc2_shift, after=()):
    return local_call(
        mlp_kernel,
        [((PATCHES, MLP), BF), ((PATCHES, MLP), BF), ((PATCHES, D), BF)],
        [], rows, first, fc1, fc2, fc1_shift, fc2_shift, after=after,
    )


def up_back(grad_block, grad_tap, block_out, tap_rows, up_full, after=()):
    flat = (PATCHES, D)
    return local_call(
        up_back_kernel,
        [((D, 16 * DEC), BF), (flat, BF), (flat, F32), (flat, BF), ((1, D), F32)],
        [], grad_block, grad_tap, block_out, tap_rows, up_full, after=after,
    )


def fc2_back(place, grad_mlp, active, slope, fc2, after=()):
    half = ((MLP, D // 2), BF)
    return local_call(
        fc2_back_kernel,
        [half, half, ((PATCHES, MLP), BF), ((1, MLP), F32)],
        [], place, grad_mlp, active, slope, fc2, after=after,
    )


def fc1_back(place, grad_hidden, input_two, first, grad_second, fc1, weight, vectors, after=()):
    half, flat = ((D, MLP // 2), BF), (PATCHES, D)
    return local_call(
        fc1_back_kernel,
        [half, half, (flat, F32), (flat, BF), (flat, BF), ((8, D), F32)],
        [],
        place, grad_hidden, input_two, first, grad_second, fc1, weight, vectors, after=after,
    )


def attention_back(place, *operands, after=()):
    wide = 4 * D + 2 * DEC
    half = ((D, wide // 2), BF)
    return local_call(
        attention_back_kernel,
        [half, half, ((PATCHES, D), BF)],
        [((PATCHES, 3 * D), BF), ((D, wide), BF), ((DEC, D), F32)],
        place, *operands, after=after,
    )


def make_body(axes):
    names, wa, col = axes.names, axes.wa, axes.col
    both = wa + col

    def body(
        tokens,
        tap,
        ln1_gain,
        ln1_bias,
        qkv_weight,
        query_bias,
        value_bias,
        out_weight,
        out_bias,
        ln2_gain,
        ln2_bias,
        fc1_weight,
        fc1_bias,
        fc2_weight,
        fc2_bias,
        block_up,
        tap_up,
        conv1_weight,
        conv2_weight,
        skip_weight,
        cotangent,
    ):
        rows_here = ln1_gain.shape[0]
        place = lax.axis_index(axes.core).astype(jnp.int32).reshape(1)

        vectors = [
            item.reshape(rows_here, -1)
            for item in (
                ln1_gain, ln1_bias, query_bias, value_bias, out_bias, ln2_gain, ln2_bias,
                fc2_bias, *jnp.split(fc1_bias, MLP // D),
            )
        ]
        vectors = jnp.concatenate(vectors, axis=1)
        extra = vectors.shape[1]
        vectors = jnp.pad(vectors, ((0, 0), (0, 2 * DEC - extra)))
        get_first = RowGather(
            jnp.concatenate([qkv_weight, out_weight, vectors], axis=1), axes.links_a, axes
        )
        get_fc1 = RowGather(fc1_weight, axes.links_b, axes)
        get_fc2 = RowGather(fc2_weight, axes.links_a, axes)
        up_full = lax.all_gather(
            jnp.concatenate([block_up, tap_up], axis=1), both, axis=0, tiled=True
        )
        conv_shard = jnp.concatenate([conv1_weight, conv2_weight], axis=2)
        skip_shard = jnp.pad(skip_weight, ((0, 0), (0, DEC)))
        conv_shard = jnp.concatenate([conv_shard, skip_shard[None]], axis=0)
        raw = lax.all_gather(conv_shard, col, axis=0, tiled=False)
        rows_bf = swap_blocks(tokens.reshape(axes.wa_count, -1, D), wa).reshape(PATCHES, D)
        get_first.link()
        get_fc1.value = wait_for(get_fc1.value, corner(get_first.value))
        get_fc1.link()
        get_first.link()
        get_fc2.value = wait_for(get_fc2.value, corner(get_fc1.value))
        get_fc2.link()
        for item in (get_first, get_fc1, get_fc2):
            while item.left:
                item.link()
        first_weight = get_first.finish(get_first.rows())
        tap = wait_for(tap, corner(get_fc2.value))
        tap_rows = swap_blocks(tap.reshape(axes.wa_count, -1, D), wa).reshape(PATCHES, D)
        cotangent = wait_for(cotangent, corner(get_fc2.value))
        upstream = swap_blocks(cotangent.reshape(axes.col_count, -1, VOX), col).reshape(DEC, VOX)

        input_one, qkv_rows, probs, attn_rows, first, input_two, vectors = attention(
            rows_bf, first_weight
        )
        fc1_full = get_fc1.finish(get_fc1.rows())
        fc2_full = get_fc2.finish(wait_for(get_fc2.rows(), corner(input_two)))
        fc1_shift = vectors[8:extra].reshape(extra - 8, -1, rows_here).transpose(1, 0, 2)
        fc1_shift = fc1_shift.reshape(1, MLP)
        active, slope, block_out = mlp(
            input_two, first, fc1_full, fc2_full, fc1_shift, vectors[7:8],
            after=(tap_rows,),
        )
        joined, hidden_maps, normed_c1, factor_c1, grad_c2, grad_skip, section = decoder_forward(
            block_out, tap_rows, up_full, raw, upstream
        )
        section_out = swap_blocks(section.reshape(axes.col_count, -1, VOX), col)

        grad_c1, grad_up_block, grad_up_tap = decoder_backward(
            grad_c2, grad_skip, normed_c1, factor_c1, raw
        )
        grad_up, grad_tap_rows, grad_second, grad_mlp, fc2_shift_sums = up_back(
            grad_up_block, grad_up_tap, block_out, tap_rows, up_full,
        )
        grad_ups = lax.psum_scatter(grad_up, both, scatter_dimension=0, tiled=True)
        keep, send, grad_hidden, fc1_shift_sums = fc2_back(
            place, grad_mlp, active, slope, fc2_full
        )
        sum_fc2 = RowSum(keep, send, axes.links_a, axes)
        keep, send, grad_first, grad_attn, grad_mixed, sums_two = fc1_back(
            place, grad_hidden, input_two, first, grad_second, fc1_full, first_weight, vectors
        )
        sum_fc1 = RowSum(keep, send, axes.links_b, axes)
        small = jnp.concatenate(
            [
                jnp.zeros((4, D), F32), sums_two[2:3], sums_two[:2], fc2_shift_sums,
                fc1_shift_sums.reshape(-1, extra - 8, rows_here).transpose(1, 0, 2).reshape(-1, D),
                jnp.zeros((16 - extra, D), F32),
            ]
        )
        keep, send, grad_rows = attention_back(
            place, grad_mixed, grad_attn, grad_first, qkv_rows, probs, attn_rows, input_one,
            rows_bf, first_weight, vectors, small, after=(sum_fc2.value,),
        )
        sum_fc2.link()
        sum_first = RowSum(keep, send, axes.links_b, axes)
        conv_grads = decoder_weights(
            grad_c2, hidden_maps, grad_c1, joined.reshape(SIDE, PLANE, 2 * DEC), grad_skip,
            shape=raw.shape, after=(sum_fc1.value, sum_fc2.value),
        )
        sum_fc1.link()
        sum_fc2.link()

        columns = conv_grads.shape[3]
        conv_grads = conv_grads.reshape([lax.axis_size(n) for n in col] + [-1, columns])
        conv_grads = scatter_dims(conv_grads, axes.inside(col)[::-1], names)
        conv_grads = conv_grads.reshape([lax.axis_size(n) for n in wa] + [-1, columns])
        wa_order = axes.inside(wa)
        conv_grads = scatter_dims(conv_grads, wa_order[::-1], names).astype(BF)
        conv_grads = gather_dims(conv_grads, wa_order, names).reshape(28, -1, columns)
        conv_grads = conv_grads.astype(F32)

        home_rows = swap_blocks(grad_rows.reshape(axes.wa_count, -1, D), wa).astype(F32)[None]
        home_tap = swap_blocks(grad_tap_rows.reshape(axes.wa_count, -1, D), wa).astype(F32)[None]
        sums = (sum_fc2, sum_fc1, sum_first)
        for item in sums:
            while item.left:
                item.link()
        grad_ups = gate(grad_ups, sum_first.value).astype(F32)
        grad_fc2, grad_fc1, first_grads = (item.finish() for item in sums)
        small_sums = first_grads[:, 4 * D : 4 * D + extra]
        return (
            section_out[:, None],
            home_rows,
            home_tap,
            small_sums[:, 0],
            small_sums[:, 1],
            first_grads[:, : 3 * D],
            small_sums[:, 2],
            small_sums[:, 3],
            first_grads[:, 3 * D : 4 * D],
            small_sums[:, 4],
            small_sums[:, 5],
            small_sums[:, 6],
            grad_fc1,
            small_sums[:, 8:extra].T.reshape(-1),
            grad_fc2,
            small_sums[:, 7],
            grad_ups[:, : 8 * DEC],
            grad_ups[:, 8 * DEC :],
            conv_grads[:27, :, : 2 * DEC],
            conv_grads[:27, :, 2 * DEC :],
            conv_grads[27, :, : 2 * DEC],
        )

    return body


def solution(mesh):
    axes = Axes(mesh)
    wa, col = axes.wa, axes.col
    both = wa + col
    tall, flat = P(both, None), P(both)
    rows = P(col, None, wa, None)
    maps = P(None, wa, col, None)
    kernel, wide = P(None, col, None), P(col, None)
    in_specs = (
        rows, rows, flat, flat, tall, flat, flat, tall, flat, flat, flat, tall, flat, tall, flat,
        tall, tall, kernel, kernel, wide, maps,
    )
    out_specs = (
        maps, rows, rows, flat, flat, tall, flat, flat, tall, flat, flat, flat, tall, flat, tall,
        flat, tall, tall, kernel, kernel, wide,
    )
    return jax.shard_map(
        make_body(axes), mesh=axes.mesh, in_specs=in_specs, out_specs=out_specs, check_vma=False
    )
```

```python
import jax
import jax.numpy as jnp
from jax import lax
from jax.experimental import pallas as pl
from jax.experimental.pallas import tpu as pltpu
from jax.sharding import Mesh, PartitionSpec as P

D = 768
HEADS = 12
HEAD_DIM = 64
MLP = 3072
DEC = 128
GRID = 8
PATCHES = 512
SIDE = 16
VOX = 4096
PLANE = SIDE * SIDE
BF = jnp.bfloat16
F32 = jnp.float32
VMEM_BYTES = 56 * 2**20
COST = 3 * 10**10


def cut_axis(devices, label):
    places = [getattr(item, "coords", None) for item in devices]
    if len(devices) == 1 or any(place is None for place in places):
        return [(label, len(devices), False)]
    full = [tuple(item.coords) + (item.core_on_chip,) for item in devices]
    found = []
    for axis in range(4):
        values = [place[axis] for place in full]
        if len(set(values)) > 1:
            stride = next(k for k in range(len(values)) if values[k] != values[0])
            found.append((stride, len(set(values)), axis))
    found.sort(reverse=True)
    step = 1
    for stride, size, _ in reversed(found):
        if stride != step:
            return [(label, len(devices), False)]
        step *= size
    if step != len(devices):
        return [(label, len(devices), False)]
    return [(label + "xyzc"[axis], size, axis == 3) for _, size, axis in found]


class Axes:
    def __init__(self, mesh):
        grid = mesh.devices
        wa = cut_axis(list(grid[:, 0]), "wa")
        col = cut_axis(list(grid[0, :]), "col")
        parts = wa + col
        self.sizes = {name: size for name, size, _ in parts}
        self.names = tuple(self.sizes)
        self.wa = tuple(name for name, _, _ in wa)
        self.col = tuple(name for name, _, _ in col)
        self.wa_count, self.col_count = grid.shape
        self.mesh = Mesh(grid.reshape(tuple(self.sizes.values())), self.names)
        core = [name for name, _, is_core in parts if is_core]
        links = [name for name, _, is_core in parts if not is_core]
        links.sort(key=lambda name: -self.sizes[name])
        self.core = core[0] if core else None
        self.links_a = tuple(links)
        if len(links) > 2:
            links = links[:-2] + [links[-1], links[-2]]
        self.links_b = tuple(links)

    def inside(self, names):
        return [n for n in self.links_a if n in names] + [n for n in (self.core,) if n in names]


def swap(value, axis):
    return lax.ppermute(value, axis, [(0, 1), (1, 0)])


def turn(value, axis, size, step):
    return lax.ppermute(value, axis, [(k, (k + step) % size) for k in range(size)])


def gather_axis(value, axis, size):
    place = lax.axis_index(axis)
    if size == 2:
        mine, other = value[None], swap(value, axis)[None]
        return jnp.where(
            place == 0,
            jnp.concatenate([mine, other]),
            jnp.concatenate([other, mine]),
        )
    got = [turn(value, axis, size, step) for step in range(1, size)]
    out = jnp.zeros((size,) + value.shape, value.dtype)
    out = lax.dynamic_update_index_in_dim(out, value, place, 0)
    for step in range(1, size):
        out = lax.dynamic_update_index_in_dim(out, got[step - 1], (place - step) % size, 0)
    return out


def keep_order(first, second, place, axis):
    return jnp.where(
        place == 0,
        jnp.concatenate([first, second], axis),
        jnp.concatenate([second, first], axis),
    )


def column_half(value, place):
    half = value.shape[-1] // 2
    return lax.dynamic_slice_in_dim(value, place * half, half, value.ndim - 1)


def gather_dims(value, order, names):
    dims, inner = [], value.ndim
    for name in order:
        value = gather_axis(value, name, lax.axis_size(name))
        dims.insert(0, name)
    kept = [name for name in names if name in dims]
    return value.transpose([dims.index(n) for n in kept] + [len(dims) + k for k in range(inner)])


class RowGather:
    def __init__(self, value, links, axes):
        self.axes, self.left, self.dims = axes, list(links), []
        place = lax.axis_index(axes.core)
        mine, other = column_half(value, place), column_half(value, 1 - place)
        self.value = keep_order(mine[None], swap(other, axes.core)[None], place, 0)

    def link(self):
        name = self.left.pop(0)
        self.value = gather_axis(self.value, name, lax.axis_size(name))
        self.dims.insert(0, name)

    def rows(self):
        axes, value = self.axes, self.value
        kept = [name for name in axes.names if name in self.dims]
        count = len(kept)
        value = value.transpose([self.dims.index(n) for n in kept] + [count, count + 1, count + 2])
        value = jnp.moveaxis(value, count, axes.names.index(axes.core))
        return value.reshape(-1, value.shape[-1])

    def finish(self, half):
        place = lax.axis_index(self.axes.core)
        return keep_order(half, swap(half, self.axes.core), place, 1)


def wait_for(value, *others):
    return lax.optimization_barrier((value, *others))[0]


def corner(value):
    return value.reshape(-1, value.shape[-1])[:16, :128]


def scatter_axis(value, axis, dim):
    size, place = lax.axis_size(axis), lax.axis_index(axis)
    got = [
        turn(lax.dynamic_index_in_dim(value, (place + step) % size, dim, False), axis, size, step)
        for step in range(1, size)
    ]
    total = lax.dynamic_index_in_dim(value, place, dim, False).astype(F32)
    for item in got:
        total = total + item.astype(F32)
    return total


def scatter_dims(value, order, names):
    dims = [name for name in names if name in order]
    for name in order:
        dim = dims.index(name)
        dims.pop(dim)
        value = scatter_axis(value.astype(BF), name, dim)
    return value


class RowSum:
    def __init__(self, keep, send, links, axes):
        self.axes, self.left = axes, list(reversed(links))
        self.dims = list(axes.names)
        got = swap(send, axes.core)
        self.value = (keep.astype(F32) + got.astype(F32)).astype(BF)
        columns = keep.shape[1]
        self.value = self.value.reshape([lax.axis_size(n) for n in self.dims] + [-1, columns])

    def link(self):
        name = self.left.pop(0)
        dim = self.dims.index(name)
        self.dims.pop(dim)
        self.value = scatter_axis(self.value, name, dim)
        if self.left:
            self.value = self.value.astype(BF)

    def finish(self):
        axes = self.axes
        place = lax.axis_index(axes.core)
        mine = lax.dynamic_index_in_dim(self.value, place, 0, False)
        other = lax.dynamic_index_in_dim(self.value, 1 - place, 0, False).astype(BF)
        return keep_order(mine, swap(other, axes.core).astype(F32), place, 1)


def swap_blocks(value, axes):
    return lax.all_to_all(value, axes, 0, 0, tiled=True)


def product(left, right):
    return jnp.dot(left, right, preferred_element_type=F32)


def product_rows(left, right):
    return lax.dot_general(left, right, (((0,), (0,)), ((), ())), preferred_element_type=F32)


def product_back(left, right):
    return lax.dot_general(left, right, (((1,), (1,)), ((), ())), preferred_element_type=F32)


def row_norm(values, epsilon):
    center = values - jnp.mean(values, axis=-1, keepdims=True)
    factor = lax.rsqrt(jnp.mean(center * center, axis=-1, keepdims=True) + epsilon)
    return (center * factor, factor)


def row_norm_back(upstream, normed, factor):
    middle = upstream - jnp.mean(upstream, axis=-1, keepdims=True)
    return factor * (middle - normed * jnp.mean(upstream * normed, axis=-1, keepdims=True))


def unit_matrix(size):
    here = lax.broadcasted_iota(jnp.int32, (size, size), 0)
    there = lax.broadcasted_iota(jnp.int32, (size, size), 1)
    return (here == there).astype(F32).astype(BF)


def turned(value, unit):
    return product_back(unit, value).astype(BF)


def head_masks():
    lane = lax.broadcasted_iota(jnp.int32, (PATCHES, 2 * HEAD_DIM), 1)
    return [(lane < HEAD_DIM).astype(F32).astype(BF), (lane >= HEAD_DIM).astype(F32).astype(BF)]


def low_lanes(shape):
    return lax.broadcasted_iota(jnp.int32, shape, 1) < HEAD_DIM


def attention_kernel(
    rows_ref, weight_ref,
    input_one_ref, qkv_ref, probs_ref, attn_ref, first_ref, input_two_ref, vectors_ref,
):
    rows = rows_ref[...].astype(F32)
    unit = unit_matrix(2 * HEAD_DIM)
    vectors_ref[...] = product_back(unit, weight_ref[:, 4 * D : 4 * D + DEC])[:16]
    gain_one, bias_one, query_bias, value_bias, out_shift, gain_two, bias_two = (
        vectors_ref[k : k + 1] for k in range(7)
    )
    normed, _ = row_norm(rows, 1e-06)
    input_one_ref[...] = (normed * gain_one + bias_one).astype(BF)
    for block, bias in enumerate((query_bias, None, value_bias)):
        columns = slice(block * D, (block + 1) * D)
        value = product(input_one_ref[...], weight_ref[:, columns])
        qkv_ref[:, columns] = (value if bias is None else value + bias).astype(BF)
    masks, wide_unit = head_masks(), unit_matrix(PATCHES)

    def pair_step(pair, _):
        at = pl.multiple_of(pair * 2 * HEAD_DIM, 2 * HEAD_DIM)
        columns = pl.ds(at, 2 * HEAD_DIM)
        queries = qkv_ref[:, columns]
        keys = qkv_ref[:, pl.ds(at + D, 2 * HEAD_DIM)]
        values = turned(qkv_ref[:, pl.ds(at + 2 * D, 2 * HEAD_DIM)], unit)
        mixed = []
        for head in range(2):
            scores = product_back(keys * masks[head], queries) * 0.125
            expo = jnp.exp(scores - jnp.max(scores, axis=0, keepdims=True))
            probs = (expo * (1.0 / jnp.sum(expo, axis=0, keepdims=True))).astype(BF)
            probs_ref[2 * pair + head] = probs
            part = product(values[head * HEAD_DIM : (head + 1) * HEAD_DIM], probs)
            mixed.append(part.astype(BF))
        attn_ref[:, columns] = product_back(wide_unit, jnp.concatenate(mixed)).astype(BF)

    lax.fori_loop(0, HEADS // 2, pair_step, None, unroll=PAIRS)
    first = rows + product(attn_ref[...], weight_ref[:, 3 * D : 4 * D]) + out_shift
    first_ref[...] = first
    normed, _ = row_norm(first, 1e-06)
    input_two_ref[...] = (normed * gain_two + bias_two).astype(BF)


CHUNK = 512


def mlp_kernel(
    input_ref, first_ref, fc1_ref, fc2_ref, fc1_shift_ref, fc2_shift_ref,
    active_ref, slope_ref, out_ref,
):
    total = first_ref[...] + fc2_shift_ref[...]
    for at in range(0, MLP, CHUNK):
        columns = slice(at, at + CHUNK)
        hidden = product(input_ref[...], fc1_ref[:, columns]) + fc1_shift_ref[:, columns]
        below = 0.5 * (1.0 + lax.erf(hidden * 0.7071067811865476))
        slope = below + hidden * (0.3989422804014327 * jnp.exp(-0.5 * hidden * hidden))
        slope_ref[:, columns] = slope.astype(BF)
        active_ref[:, columns] = (hidden * below).astype(BF)
        total = total + product(active_ref[:, columns], fc2_ref[columns])
    out_ref[...] = total.astype(BF)


def cut_columns(ref, place):
    half = ref.shape[1] // 2
    keep = pl.ds(pl.multiple_of(place * half, DEC), half)
    send = pl.ds(pl.multiple_of((1 - place) * half, DEC), half)
    return (keep, send)


def up_back_kernel(
    grad_block_ref, grad_tap_ref, block_ref, tap_ref, up_ref,
    grad_up_ref, grad_rows_ref, grad_second_ref, grad_mlp_ref, sums_ref,
):
    unit = unit_matrix(PLANE)
    for source, (grad_ref, rows_ref) in enumerate(
        ((grad_block_ref, block_ref), (grad_tap_ref, tap_ref))
    ):
        columns = slice(source * 8 * DEC, (source + 1) * 8 * DEC)
        for at in range(0, D, PLANE):
            rows = slice(at, at + PLANE)
            left = turned(rows_ref[:, rows], unit)
            grad_up_ref[rows, columns] = product(left, grad_ref[...]).astype(BF)
        back = product_back(grad_ref[...], up_ref[:, columns])
        if source == 0:
            grad_second_ref[...] = back
            grad_mlp_ref[...] = back.astype(BF)
            sums_ref[...] = column_sum(back.astype(BF).astype(F32))
        else:
            grad_rows_ref[...] = back.astype(BF)


def fc2_back_kernel(
    place_ref, grad_mlp_ref, active_ref, slope_ref, fc2_ref,
    keep_ref, send_ref, grad_hidden_ref, sums_ref,
):
    unit = unit_matrix(PLANE)
    keep, send = cut_columns(grad_mlp_ref, place_ref[0])
    for at in range(0, MLP, PLANE):
        rows = slice(at, at + PLANE)
        left = turned(active_ref[:, rows], unit)
        send_ref[rows] = product(left, grad_mlp_ref[:, send]).astype(BF)
        keep_ref[rows] = product(left, grad_mlp_ref[:, keep]).astype(BF)
    for at in range(0, MLP, CHUNK):
        rows = slice(at, at + CHUNK)
        grad = product_back(grad_mlp_ref[...], fc2_ref[rows]) * slope_ref[:, rows].astype(F32)
        grad = grad.astype(BF)
        grad_hidden_ref[:, rows] = grad
        sums_ref[:, rows] = column_sum(grad.astype(F32))


def fc1_back_kernel(
    place_ref, grad_hidden_ref, input_ref, first_ref, grad_second_ref, fc1_ref, weight_ref,
    vectors_ref,
    keep_ref, send_ref, grad_first_ref, grad_attn_ref, grad_mixed_ref, sums_ref,
):
    unit = unit_matrix(PLANE)
    keep, send = cut_columns(grad_hidden_ref, place_ref[0])
    for at in range(0, D, PLANE):
        rows = slice(at, at + PLANE)
        left = turned(input_ref[:, rows], unit)
        send_ref[rows] = product(left, grad_hidden_ref[:, send]).astype(BF)
        keep_ref[rows] = product(left, grad_hidden_ref[:, keep]).astype(BF)
    grad = product_back(grad_hidden_ref[...], fc1_ref[...])
    normed, factor = row_norm(first_ref[...], 1e-06)
    sums_ref[0:1] = column_sum(grad * normed)
    sums_ref[1:2] = column_sum(grad)
    grad = grad_second_ref[...] + row_norm_back(grad * vectors_ref[5:6], normed, factor)
    grad_first_ref[...] = grad
    grad = grad.astype(BF)
    grad_attn_ref[...] = grad
    sums_ref[2:3] = column_sum(grad.astype(F32))
    grad_mixed_ref[...] = product_back(grad, weight_ref[:, 3 * D : 4 * D]).astype(BF)


def attention_back_kernel(
    place_ref, grad_mixed_ref, grad_attn_ref, grad_first_ref, qkv_ref, probs_ref, attn_ref,
    input_ref, rows_ref, weight_ref, vectors_ref, small_ref,
    keep_ref, send_ref, grad_rows_ref,
    grad_qkv_ref, grad_ref, sums_ref,
):
    masks, unit, wide_unit = head_masks(), unit_matrix(2 * HEAD_DIM), unit_matrix(PATCHES)

    def pair_step(pair, _):
        at = pl.multiple_of(pair * 2 * HEAD_DIM, 2 * HEAD_DIM)
        columns = pl.ds(at, 2 * HEAD_DIM)
        queries = qkv_ref[:, columns]
        keys_turned = turned(qkv_ref[:, pl.ds(at + D, 2 * HEAD_DIM)], unit)
        values = qkv_ref[:, pl.ds(at + 2 * D, 2 * HEAD_DIM)]
        grads = grad_mixed_ref[:, columns]
        grad_q, grad_k, grad_v = [], [], []
        for head in range(2):
            probs = probs_ref[2 * pair + head]
            grad_probs = product_back(values * masks[head], grads)
            wide = probs.astype(F32)
            inner = jnp.sum(grad_probs * wide, axis=0, keepdims=True)
            grad_scores = (wide * (grad_probs - inner)).astype(BF)
            grad_v.append(product(probs, grads))
            grad_k.append(product(grad_scores, queries) * 0.125)
            part = product(keys_turned[head * HEAD_DIM : (head + 1) * HEAD_DIM], grad_scores)
            grad_q.append((part * 0.125).astype(BF))
        first = low_lanes((PATCHES, 2 * HEAD_DIM))
        grad_qkv_ref[:, columns] = product_back(wide_unit, jnp.concatenate(grad_q)).astype(BF)
        grad_qkv_ref[:, pl.ds(at + D, 2 * HEAD_DIM)] = jnp.where(first, *grad_k).astype(BF)
        grad_qkv_ref[:, pl.ds(at + 2 * D, 2 * HEAD_DIM)] = jnp.where(first, *grad_v).astype(BF)

    lax.fori_loop(0, HEADS // 2, pair_step, None, unroll=PAIRS)
    square = unit_matrix(PLANE)
    for at in range(0, D, PLANE):
        rows = slice(at, at + PLANE)
        left = turned(input_ref[:, rows], square)
        grad_ref[rows, : 3 * D] = product(left, grad_qkv_ref[...]).astype(BF)
        left = turned(attn_ref[:, rows], square)
        grad_ref[rows, 3 * D : 4 * D] = product(left, grad_attn_ref[...]).astype(BF)
    grad = product_back(grad_qkv_ref[...], weight_ref[:, : 3 * D])
    normed, factor = row_norm(rows_ref[...].astype(F32), 1e-06)
    sums_ref[...] = jnp.zeros(sums_ref.shape, F32)
    sums_ref[:16] = small_ref[...]
    sums_ref[0:1] = column_sum(grad * normed)
    sums_ref[1:2] = column_sum(grad)
    sums_ref[2:3] = column_sum(grad_qkv_ref[:, :D].astype(F32))
    sums_ref[3:4] = column_sum(grad_qkv_ref[:, 2 * D :].astype(F32))
    for at in range(0, D, DEC):
        rows = slice(at, at + DEC)
        grad_ref[rows, 4 * D : 4 * D + DEC] = turned(sums_ref[:, rows].astype(BF), unit)
        grad_ref[rows, 4 * D + DEC :] = jnp.zeros((DEC, DEC), BF)
    keep, send = cut_columns(grad_ref, place_ref[0])
    send_ref[...] = grad_ref[:, send]
    keep_ref[...] = grad_ref[:, keep]
    grad = grad_first_ref[...] + row_norm_back(grad * vectors_ref[0:1], normed, factor)
    grad_rows_ref[...] = grad.astype(BF)


def halves(value):
    rows, columns = value.shape
    cut = value.reshape(rows // 16, 2, 8, columns)
    return (cut[:, 0], cut[:, 1])


def join_halves(low, high):
    count, _, columns = low.shape
    return jnp.concatenate(
        [low.reshape(count, 1, 8, columns), high.reshape(count, 1, 8, columns)], axis=1
    ).reshape(count * 16, columns)


def side_steps(low, high):
    place = lax.broadcasted_iota(jnp.int32, low.shape, 1)
    back = jnp.where(place == 0, 0.0, pltpu.roll(high, 1, 1))
    ahead = jnp.where(place == 7, 0.0, pltpu.roll(low, 7, 1))
    return (join_halves(back, low), join_halves(high, ahead))


def put_stack(ref, z, value):
    columns = value.shape[1]
    before, after = side_steps(*halves(value))
    ref[z, :, :columns] = before.astype(BF)
    ref[z, :, columns : 2 * columns] = value.astype(BF)
    ref[z, :, 2 * columns :] = after.astype(BF)


def silu_gate(values):
    return 1.0 / (1.0 + jnp.exp(-values))


UNROLL = 8
PAIRS = 3


def planes(step, carry=None):
    return lax.fori_loop(0, SIDE, step, carry, unroll=UNROLL)


def forward_table(raw_ref, table_ref, first, ins):
    parts, _, rows, _ = raw_ref.shape
    for k in range(9):
        for along in range(3):
            for part in range(parts):
                table_ref[
                    k * DEC + part * rows : k * DEC + (part + 1) * rows,
                    along * ins : (along + 1) * ins,
                ] = raw_ref[part, 3 * k + along, :, first : first + ins]


def backward_table(raw_ref, table_ref, first, ins):
    parts, _, rows, _ = raw_ref.shape
    for k in range(9):
        for along in range(3):
            for part in range(parts):
                table_ref[
                    along * DEC + part * rows : along * DEC + (part + 1) * rows,
                    k * ins : (k + 1) * ins,
                ] = raw_ref[part, 3 * k + 2 - along, :, first : first + ins]


def skip_table(raw_ref):
    return jnp.concatenate([raw_ref[part, 27, :, : 2 * DEC] for part in range(raw_ref.shape[0])])


GROUP = 4


def conv_planes(source, table_ref, total_ref, columns, forward):
    for z in range(SIDE + 2):
        total_ref[z] = jnp.zeros((PLANE, columns), F32)

    def step(group, _):
        start = group * GROUP
        value = jnp.concatenate([source(start + k) for k in range(GROUP)])
        if forward:
            wide = product_back(value, table_ref[...])
        else:
            wide = product(value, table_ref[...])
        none = jnp.zeros((SIDE, columns), F32)
        for plane in range(GROUP):
            for along_d in (-1, 0, 1):
                parts = [
                    wide[plane * PLANE : (plane + 1) * PLANE, k * columns : (k + 1) * columns]
                    for k in range(3 * along_d + 3, 3 * along_d + 6)
                ]
                to = along_d if not forward else -along_d
                early, late = (parts[0], parts[2]) if not forward else (parts[2], parts[0])
                moved = (
                    parts[1]
                    + jnp.concatenate([early[SIDE:], none])
                    + jnp.concatenate([none, late[:-SIDE]])
                )
                at = start + plane + 1 + to
                total_ref[at] = total_ref[at] + moved

    lax.fori_loop(0, SIDE // GROUP, step, None)


def column_sum(value):
    return jnp.sum(value, axis=0, keepdims=True)


def row_sums(value):
    return jnp.sum(value.reshape(-1, 8, value.shape[1]), axis=0)


def map_stats(total_ref, first):
    zero = jnp.zeros((8, total_ref.shape[2]), F32)
    mean = planes(lambda z, run: run + row_sums(total_ref[z + first]), zero)
    mean = column_sum(mean) / VOX

    def spread(z, run):
        center = total_ref[z + first] - mean
        return run + row_sums(center * center)

    return (mean, lax.rsqrt(column_sum(planes(spread, zero)) / VOX + 1e-05))


def sort_matrix():
    here = lax.broadcasted_iota(jnp.int32, (PLANE, PLANE), 0)
    there = lax.broadcasted_iota(jnp.int32, (PLANE, PLANE), 1)
    own = (here & -16) + 2 * (here & 7) + ((here >> 3) & 1)
    return (own == there).astype(F32).astype(BF)


def plane_of(ref, z):
    return ref[lax.shift_right_logical(z, 1), z & 1].reshape(PLANE, ref.shape[-1])


def decoder_forward_kernel(
    block_ref, tap_ref, up_ref, raw_ref, cot_ref,
    joined_ref, hidden_ref, normed_ref, factor_ref, grad_two_ref, grad_skip_ref, section_ref,
    wide_ref, stack_ref, table_one, table_two, total_ref, skip_ref, grad_ref,
):
    forward_table(raw_ref, table_one, 0, 2 * DEC)
    forward_table(raw_ref, table_two, 2 * DEC, DEC)
    for source, rows_ref in enumerate((block_ref, tap_ref)):
        for i in range(2):
            for j in range(2):
                start = source * 8 * DEC + (i * 2 + j) * 2 * DEC
                part = product(rows_ref[...], up_ref[:, start : start + 2 * DEC])
                part = part.astype(BF).astype(F32)
                low = part[:, :DEC].reshape(GRID * GRID, 8, DEC)
                high = part[:, DEC:].reshape(GRID * GRID, 8, DEC)
                before, after = side_steps(low, high)
                for block, value in enumerate((before, join_halves(low, high), after)):
                    at = block * 2 * DEC + source * DEC
                    value = value.astype(BF).reshape(GRID, GRID, SIDE, DEC)
                    wide_ref[:, i, :, j, :, at : at + DEC] = value
                    if block == 1:
                        joined_ref[:, i, :, j, :, source * DEC : (source + 1) * DEC] = value

    conv_planes(lambda z: plane_of(wide_ref, z), table_one, total_ref, DEC, True)
    mean, factor = map_stats(total_ref, 1)
    factor_ref[...] = factor

    def act(z, _):
        normed = (total_ref[z + 1] - mean) * factor
        normed_ref[z] = normed
        value = (normed * silu_gate(normed)).astype(BF)
        hidden_ref[z] = value
        put_stack(stack_ref, z, value.astype(F32))

    planes(act)
    conv_planes(lambda z: stack_ref[z], table_two, total_ref, DEC, True)
    skip = skip_table(raw_ref)

    def skip_step(z, _):
        skip_ref[z] = product_back(plane_of(joined_ref, z), skip)

    planes(skip_step)
    mean_two, factor_two = map_stats(total_ref, 1)
    mean_skip, factor_skip = map_stats(skip_ref, 0)
    sort, unit = sort_matrix(), unit_matrix(DEC)
    zero = jnp.zeros((8, DEC), F32)

    def out_step(z, sums):
        two = (total_ref[z + 1] - mean_two) * factor_two
        side = (skip_ref[z] - mean_skip) * factor_skip
        both = two + side
        gate = silu_gate(both)
        columns = pl.ds(pl.multiple_of(z * PLANE, PLANE), PLANE)
        turned = product_back(unit, (both * gate).astype(BF)).astype(BF)
        section_ref[:, columns] = product(turned, sort).astype(BF)
        grad = product_back(sort, cot_ref[:, columns]) * (gate * (1.0 + both * (1.0 - gate)))
        total_ref[z + 1] = two
        skip_ref[z] = side
        grad_ref[z] = grad
        return (
            sums[0] + row_sums(grad),
            sums[1] + row_sums(grad * two),
            sums[2] + row_sums(grad * side),
        )

    plain, by_two, by_skip = (column_sum(item) for item in planes(out_step, (zero, zero, zero)))

    def back_step(z, _):
        middle = grad_ref[z] - plain / VOX
        grad_two_ref[z] = (factor_two * (middle - total_ref[z + 1] * (by_two / VOX))).astype(BF)
        grad_skip_ref[z] = (factor_skip * (middle - skip_ref[z] * (by_skip / VOX))).astype(BF)

    planes(back_step)


def decoder_backward_kernel(
    grad_two_ref, grad_skip_ref, normed_ref, factor_ref, raw_ref,
    grad_one_ref, rows_block_ref, rows_tap_ref,
    stack_ref, table_one, table_two, total_ref, wide_ref,
):
    backward_table(raw_ref, table_one, 0, 2 * DEC)
    backward_table(raw_ref, table_two, 2 * DEC, DEC)

    def stack_step(z, _):
        put_stack(stack_ref, z, grad_two_ref[z].astype(F32))

    planes(stack_step)
    conv_planes(lambda z: stack_ref[z], table_two, total_ref, DEC, False)
    zero = jnp.zeros((8, DEC), F32)

    def act(z, sums):
        normed = normed_ref[z]
        gate = silu_gate(normed)
        grad = total_ref[z + 1] * (gate * (1.0 + normed * (1.0 - gate)))
        total_ref[z + 1] = grad
        return (sums[0] + row_sums(grad), sums[1] + row_sums(grad * normed))

    plain, by_normed = (column_sum(item) for item in planes(act, (zero, zero)))

    def back_step(z, _):
        middle = total_ref[z + 1] - plain / VOX
        value = (factor_ref[...] * (middle - normed_ref[z] * (by_normed / VOX))).astype(BF)
        grad_one_ref[z] = value
        put_stack(stack_ref, z, value.astype(F32))

    planes(back_step)
    conv_planes(lambda z: stack_ref[z], table_one, wide_ref, 2 * DEC, False)
    skip = skip_table(raw_ref)

    def row_step(a, _):
        rows = pl.ds(pl.multiple_of(a * GRID * GRID, GRID * GRID), GRID * GRID)
        for i in range(2):
            z = 2 * a + i
            value = wide_ref[z + 1] + product(grad_skip_ref[z], skip)
            value = value.reshape(GRID, 2, 2, 8, 2 * DEC)
            for j in range(2):
                for l in range(2):
                    at = ((i * 2 + j) * 2 + l) * DEC
                    part = value[:, j, l].reshape(GRID * GRID, 2 * DEC).astype(BF)
                    rows_block_ref[rows, at : at + DEC] = part[:, :DEC]
                    rows_tap_ref[rows, at : at + DEC] = part[:, DEC:]

    lax.fori_loop(0, GRID, row_step, None)


def turn_stack(source_ref, turned_ref, unit):
    def step(z, _):
        value = source_ref[z].astype(F32)
        before, after = side_steps(*halves(value))
        columns = pl.ds(pl.multiple_of(z * PLANE, PLANE), PLANE)
        for block, item in enumerate((before, value, after)):
            turned_ref[block * DEC : (block + 1) * DEC, columns] = product_back(
                unit, item.astype(BF)
            ).astype(BF)

    planes(step)


def put_shifted(source, shifted_ref):
    columns = shifted_ref.shape[2] // 3
    for z in (0, SIDE + 1):
        shifted_ref[z] = jnp.zeros(shifted_ref.shape[1:], BF)

    def step(z, _):
        value = source(z)
        none = jnp.zeros((SIDE, columns), BF)
        shifted_ref[z + 1, :, :columns] = jnp.concatenate([none, value[:-SIDE]])
        shifted_ref[z + 1, :, columns : 2 * columns] = value
        shifted_ref[z + 1, :, 2 * columns :] = jnp.concatenate([value[SIDE:], none])

    planes(step)


def weight_grad(turned_ref, shifted_ref, out_ref, first, ins):
    parts, _, rows, _ = out_ref.shape
    for along_d in range(3):
        shifted = shifted_ref[along_d : along_d + SIDE].reshape(VOX, 3 * ins)
        table = product(turned_ref[...], shifted).astype(BF)
        for along_h in range(3):
            for block in range(3):
                slot = (along_d * 3 + along_h) * 3 + 2 - block
                for part in range(parts):
                    out_ref[part, slot, :, first : first + ins] = table[
                        block * DEC + part * rows : block * DEC + (part + 1) * rows,
                        along_h * ins : (along_h + 1) * ins,
                    ]


def decoder_weights_kernel(
    grad_two_ref, hidden_ref, grad_one_ref, joined_ref, grad_skip_ref,
    out_ref,
    turned_ref, shifted_ref, narrow_ref,
):
    unit = unit_matrix(DEC)
    turn_stack(grad_two_ref, turned_ref, unit)
    put_shifted(lambda z: hidden_ref[z], narrow_ref)
    weight_grad(turned_ref, narrow_ref, out_ref, 2 * DEC, DEC)
    turn_stack(grad_one_ref, turned_ref, unit)
    put_shifted(lambda z: joined_ref[z], shifted_ref)
    weight_grad(turned_ref, shifted_ref, out_ref, 0, 2 * DEC)

    def step(z, _):
        columns = pl.ds(pl.multiple_of(z * PLANE, PLANE), PLANE)
        turned_ref[:DEC, columns] = product_back(unit, grad_skip_ref[z]).astype(BF)

    planes(step)
    table = product(turned_ref[:DEC], joined_ref[...].reshape(VOX, 2 * DEC)).astype(BF)
    parts, _, rows, columns = out_ref.shape
    for part in range(parts):
        out_ref[part, 27, :, : 2 * DEC] = table[part * rows : (part + 1) * rows]
        out_ref[part, 27, :, 2 * DEC :] = jnp.zeros((rows, columns - 2 * DEC), BF)


def skip_operands(kernel, count, left):
    def run(*refs):
        kernel(*refs[:count], *refs[count + left :])

    return run


def local_call(kernel, outs, scratch, *operands, after=()):
    specs = [
        pl.BlockSpec(memory_space=pltpu.SMEM if item.ndim == 1 else pltpu.VMEM)
        for item in operands
    ]
    specs += [pl.BlockSpec(memory_space=pl.ANY)] * len(after)
    vmem = pl.BlockSpec(memory_space=pltpu.VMEM)
    return pl.pallas_call(
        skip_operands(kernel, len(operands), len(after)),
        out_shape=[jax.ShapeDtypeStruct(shape, dtype) for shape, dtype in outs],
        in_specs=specs,
        out_specs=[vmem] * len(outs),
        scratch_shapes=[pltpu.VMEM(shape, dtype) for shape, dtype in scratch],
        compiler_params=pltpu.CompilerParams(vmem_limit_bytes=VMEM_BYTES),
        cost_estimate=pl.CostEstimate(flops=COST, bytes_accessed=COST, transcendentals=0),
    )(*operands, *after)


MAP = (SIDE, PLANE, DEC)


def decoder_forward(*operands, after=()):
    cube = (GRID, 2, GRID, 2, SIDE)
    return local_call(
        decoder_forward_kernel,
        [
            (cube + (2 * DEC,), BF), (MAP, BF), (MAP, F32), ((1, DEC), F32), (MAP, BF), (MAP, BF),
            ((DEC, VOX), BF),
        ],
        [
            (cube + (6 * DEC,), BF), ((SIDE, PLANE, 3 * DEC), BF), ((9 * DEC, 6 * DEC), BF),
            ((9 * DEC, 3 * DEC), BF), ((SIDE + 2, PLANE, DEC), F32), (MAP, F32), (MAP, F32),
        ],
        *operands, after=after,
    )


def decoder_backward(*operands, after=()):
    return local_call(
        decoder_backward_kernel,
        [(MAP, BF), ((PATCHES, 8 * DEC), BF), ((PATCHES, 8 * DEC), BF)],
        [
            ((SIDE, PLANE, 3 * DEC), BF), ((3 * DEC, 18 * DEC), BF), ((3 * DEC, 9 * DEC), BF),
            ((SIDE + 2, PLANE, DEC), F32), ((SIDE + 2, PLANE, 2 * DEC), F32),
        ],
        *operands, after=after,
    )


def decoder_weights(*operands, shape, after=()):
    return local_call(
        decoder_weights_kernel,
        [(shape, BF)],
        [
            ((3 * DEC, VOX), BF), ((SIDE + 2, PLANE, 6 * DEC), BF),
            ((SIDE + 2, PLANE, 3 * DEC), BF),
        ],
        *operands, after=after,
    )[0]


def gate(value, *after):
    anywhere = pl.BlockSpec(memory_space=pl.ANY)
    return pl.pallas_call(
        lambda *refs: None,
        out_shape=jax.ShapeDtypeStruct(value.shape, value.dtype),
        in_specs=[anywhere] * (1 + len(after)),
        out_specs=anywhere,
        input_output_aliases={0: 0},
        cost_estimate=pl.CostEstimate(flops=0, bytes_accessed=0, transcendentals=0),
    )(value, *after)


def attention(rows, weight, after=()):
    flat = (PATCHES, D)
    return local_call(
        attention_kernel,
        [
            (flat, BF), ((PATCHES, 3 * D), BF), ((HEADS, PATCHES, PATCHES), BF), (flat, BF),
            (flat, F32), (flat, BF), ((16, D), F32),
        ],
        [], rows, weight, after=after,
    )


def mlp(rows, first, fc1, fc2, fc1_shift, fc2_shift, after=()):
    return local_call(
        mlp_kernel,
        [((PATCHES, MLP), BF), ((PATCHES, MLP), BF), ((PATCHES, D), BF)],
        [], rows, first, fc1, fc2, fc1_shift, fc2_shift, after=after,
    )


def up_back(grad_block, grad_tap, block_out, tap_rows, up_full, after=()):
    flat = (PATCHES, D)
    return local_call(
        up_back_kernel,
        [((D, 16 * DEC), BF), (flat, BF), (flat, F32), (flat, BF), ((1, D), F32)],
        [], grad_block, grad_tap, block_out, tap_rows, up_full, after=after,
    )


def fc2_back(place, grad_mlp, active, slope, fc2, after=()):
    half = ((MLP, D // 2), BF)
    return local_call(
        fc2_back_kernel,
        [half, half, ((PATCHES, MLP), BF), ((1, MLP), F32)],
        [], place, grad_mlp, active, slope, fc2, after=after,
    )


def fc1_back(place, grad_hidden, input_two, first, grad_second, fc1, weight, vectors, after=()):
    half, flat = ((D, MLP // 2), BF), (PATCHES, D)
    return local_call(
        fc1_back_kernel,
        [half, half, (flat, F32), (flat, BF), (flat, BF), ((8, D), F32)],
        [],
        place, grad_hidden, input_two, first, grad_second, fc1, weight, vectors, after=after,
    )


def attention_back(place, *operands, after=()):
    wide = 4 * D + 2 * DEC
    half = ((D, wide // 2), BF)
    return local_call(
        attention_back_kernel,
        [half, half, ((PATCHES, D), BF)],
        [((PATCHES, 3 * D), BF), ((D, wide), BF), ((DEC, D), F32)],
        place, *operands, after=after,
    )


def make_body(axes):
    names, wa, col = axes.names, axes.wa, axes.col
    both = wa + col

    def body(
        tokens,
        tap,
        ln1_gain,
        ln1_bias,
        qkv_weight,
        query_bias,
        value_bias,
        out_weight,
        out_bias,
        ln2_gain,
        ln2_bias,
        fc1_weight,
        fc1_bias,
        fc2_weight,
        fc2_bias,
        block_up,
        tap_up,
        conv1_weight,
        conv2_weight,
        skip_weight,
        cotangent,
    ):
        rows_here = ln1_gain.shape[0]
        place = lax.axis_index(axes.core).astype(jnp.int32).reshape(1)

        vectors = [
            item.reshape(rows_here, -1)
            for item in (
                ln1_gain, ln1_bias, query_bias, value_bias, out_bias, ln2_gain, ln2_bias,
                fc2_bias, *jnp.split(fc1_bias, MLP // D),
            )
        ]
        vectors = jnp.concatenate(vectors, axis=1)
        extra = vectors.shape[1]
        vectors = jnp.pad(vectors, ((0, 0), (0, 2 * DEC - extra)))
        get_first = RowGather(
            jnp.concatenate([qkv_weight, out_weight, vectors], axis=1), axes.links_a, axes
        )
        get_fc1 = RowGather(fc1_weight, axes.links_b, axes)
        get_fc2 = RowGather(fc2_weight, axes.links_a, axes)
        up_full = lax.all_gather(
            jnp.concatenate([block_up, tap_up], axis=1), both, axis=0, tiled=True
        )
        conv_shard = jnp.concatenate([conv1_weight, conv2_weight], axis=2)
        skip_shard = jnp.pad(skip_weight, ((0, 0), (0, DEC)))
        conv_shard = jnp.concatenate([conv_shard, skip_shard[None]], axis=0)
        raw = lax.all_gather(conv_shard, col, axis=0, tiled=False)
        rows_bf = swap_blocks(tokens.reshape(axes.wa_count, -1, D), wa).reshape(PATCHES, D)
        get_first.link()
        get_fc1.value = wait_for(get_fc1.value, corner(get_first.value))
        get_fc1.link()
        get_first.link()
        get_fc2.value = wait_for(get_fc2.value, corner(get_fc1.value))
        get_fc2.link()
        for item in (get_first, get_fc1, get_fc2):
            while item.left:
                item.link()
        first_weight = get_first.finish(get_first.rows())
        tap = wait_for(tap, corner(get_fc2.value))
        tap_rows = swap_blocks(tap.reshape(axes.wa_count, -1, D), wa).reshape(PATCHES, D)
        cotangent = wait_for(cotangent, corner(get_fc2.value))
        upstream = swap_blocks(cotangent.reshape(axes.col_count, -1, VOX), col).reshape(DEC, VOX)

        input_one, qkv_rows, probs, attn_rows, first, input_two, vectors = attention(
            rows_bf, first_weight
        )
        fc1_full = get_fc1.finish(get_fc1.rows())
        fc2_full = get_fc2.finish(wait_for(get_fc2.rows(), corner(input_two)))
        fc1_shift = vectors[8:extra].reshape(extra - 8, -1, rows_here).transpose(1, 0, 2)
        fc1_shift = fc1_shift.reshape(1, MLP)
        active, slope, block_out = mlp(
            input_two, first, fc1_full, fc2_full, fc1_shift, vectors[7:8],
            after=(tap_rows,),
        )
        joined, hidden_maps, normed_c1, factor_c1, grad_c2, grad_skip, section = decoder_forward(
            block_out, tap_rows, up_full, raw, upstream
        )
        section_out = swap_blocks(section.reshape(axes.col_count, -1, VOX), col)

        grad_c1, grad_up_block, grad_up_tap = decoder_backward(
            grad_c2, grad_skip, normed_c1, factor_c1, raw
        )
        grad_up, grad_tap_rows, grad_second, grad_mlp, fc2_shift_sums = up_back(
            grad_up_block, grad_up_tap, block_out, tap_rows, up_full,
        )
        grad_ups = lax.psum_scatter(grad_up, both, scatter_dimension=0, tiled=True)
        keep, send, grad_hidden, fc1_shift_sums = fc2_back(
            place, grad_mlp, active, slope, fc2_full
        )
        sum_fc2 = RowSum(keep, send, axes.links_a, axes)
        keep, send, grad_first, grad_attn, grad_mixed, sums_two = fc1_back(
            place, grad_hidden, input_two, first, grad_second, fc1_full, first_weight, vectors
        )
        sum_fc1 = RowSum(keep, send, axes.links_b, axes)
        small = jnp.concatenate(
            [
                jnp.zeros((4, D), F32), sums_two[2:3], sums_two[:2], fc2_shift_sums,
                fc1_shift_sums.reshape(-1, extra - 8, rows_here).transpose(1, 0, 2).reshape(-1, D),
                jnp.zeros((16 - extra, D), F32),
            ]
        )
        keep, send, grad_rows = attention_back(
            place, grad_mixed, grad_attn, grad_first, qkv_rows, probs, attn_rows, input_one,
            rows_bf, first_weight, vectors, small, after=(sum_fc2.value,),
        )
        sum_fc2.link()
        sum_first = RowSum(keep, send, axes.links_b, axes)
        conv_grads = decoder_weights(
            grad_c2, hidden_maps, grad_c1, joined.reshape(SIDE, PLANE, 2 * DEC), grad_skip,
            shape=raw.shape, after=(sum_fc1.value, sum_fc2.value),
        )
        sum_fc1.link()
        sum_fc2.link()

        columns = conv_grads.shape[3]
        conv_grads = conv_grads.reshape([lax.axis_size(n) for n in col] + [-1, columns])
        conv_grads = scatter_dims(conv_grads, axes.inside(col)[::-1], names)
        conv_grads = conv_grads.reshape([lax.axis_size(n) for n in wa] + [-1, columns])
        wa_order = axes.inside(wa)
        conv_grads = scatter_dims(conv_grads, wa_order[::-1], names).astype(BF)
        conv_grads = gather_dims(conv_grads, wa_order, names).reshape(28, -1, columns)
        conv_grads = conv_grads.astype(F32)

        home_rows = swap_blocks(grad_rows.reshape(axes.wa_count, -1, D), wa).astype(F32)[None]
        home_tap = swap_blocks(grad_tap_rows.reshape(axes.wa_count, -1, D), wa).astype(F32)[None]
        sums = (sum_fc2, sum_fc1, sum_first)
        for item in sums:
            while item.left:
                item.link()
        grad_ups = gate(grad_ups, sum_first.value).astype(F32)
        grad_fc2, grad_fc1, first_grads = (item.finish() for item in sums)
        small_sums = first_grads[:, 4 * D : 4 * D + extra]
        return (
            section_out[:, None],
            home_rows,
            home_tap,
            small_sums[:, 0],
            small_sums[:, 1],
            first_grads[:, : 3 * D],
            small_sums[:, 2],
            small_sums[:, 3],
            first_grads[:, 3 * D : 4 * D],
            small_sums[:, 4],
            small_sums[:, 5],
            small_sums[:, 6],
            grad_fc1,
            small_sums[:, 8:extra].T.reshape(-1),
            grad_fc2,
            small_sums[:, 7],
            grad_ups[:, : 8 * DEC],
            grad_ups[:, 8 * DEC :],
            conv_grads[:27, :, : 2 * DEC],
            conv_grads[:27, :, 2 * DEC :],
            conv_grads[27, :, : 2 * DEC],
        )

    return body


def solution(mesh):
    axes = Axes(mesh)
    wa, col = axes.wa, axes.col
    both = wa + col
    tall, flat = P(both, None), P(both)
    rows = P(col, None, wa, None)
    maps = P(None, wa, col, None)
    kernel, wide = P(None, col, None), P(col, None)
    in_specs = (
        rows, rows, flat, flat, tall, flat, flat, tall, flat, flat, flat, tall, flat, tall, flat,
        tall, tall, kernel, kernel, wide, maps,
    )
    out_specs = (
        maps, rows, rows, flat, flat, tall, flat, flat, tall, flat, flat, flat, tall, flat, tall,
        flat, tall, tall, kernel, kernel, wide,
    )
    return jax.shard_map(
        make_body(axes), mesh=axes.mesh, in_specs=in_specs, out_specs=out_specs, check_vma=False
    )
```
